128 devices in a mesh: row: 16 (over x, y), col: 8 (over z, core).
Axes of the slice: x: 4, y: 4, z: 4, core: 2. Of those that a mesh axis runs over, the one named last changes fastest.
Arguments:
- residual: bfloat16 [1024, 16, 5120], P('row', None, 'col'), may hold values from -6 to 6
- positions: int32 [1024], P('row'), may hold values from 0 to 15
- norm_gain: float32 [5120], P('col'), may hold values from 0.1 to 1.9
- w_gate: bfloat16 [5120, 16384], P('col', 'row'), may hold values from -0.078125 to 0.078125
- w_up: bfloat16 [5120, 16384], P('col', 'row'), may hold values from -0.078125 to 0.078125
- covariance: float32 [16384, 16384], P('row', 'col'), may hold values from -1 to 4, as said below
Outputs:
- factor: float32 [16384, 16384], P('row', 'col')
The draws below stay inside these ranges and needn't reach their ends.
Inputs may be any that keep to these rules, and one draw needn't show every extreme that they name: `covariance`: symmetric positive definite in the natural order of hidden units.
All inputs are finite; a program needn't handle non-finite values.
Results may differ from the reference program's by a relative error of at most 0.0041.
Values may be sent and summed in bfloat16 or wider, within the bound.
A program may use at most 128 MiB of HBM per device.

```python
import math
import jax
import jax.numpy as jnp
from jax import lax

D = 5120
KW = 16384
TILE = 64
PANEL = 256
NPANEL = 2
LEN = 16
PROMPTS = 1024
N_ROW = 16
N_COL = 8


def draw_covariance(key, part):
    amplitude = 1.1 / KW
    first_key = jax.random.fold_in(key, 11)
    second_key = jax.random.fold_in(key, 12)
    third_key = jax.random.fold_in(key, 13)
    factor_rank = max(PANEL, 64)
    noise_field = jax.random.uniform(first_key, (KW, KW), jnp.float32, -amplitude, amplitude)
    loadings = jax.random.normal(third_key, (KW, factor_rank), jnp.float32)
    symmetric = 0.5 * (noise_field + noise_field.T)
    correlated = jnp.dot(loadings, loadings.T, precision=lax.Precision.HIGHEST, preferred_element_type=jnp.float32) * (0.5 / factor_rank)
    diagonal = jnp.exp(jax.random.uniform(second_key, (KW,), jnp.float32, math.log(1.2), math.log(2.4)))
    diag_index = jnp.arange(KW)
    natural = (symmetric + correlated).at[diag_index, diag_index].add(diagonal)
    tile_rows = KW // (N_ROW * TILE)
    tile_cols = KW // (N_COL * TILE)
    return natural.reshape(tile_rows, N_ROW, TILE, tile_cols, N_COL, TILE).transpose(1, 0, 2, 4, 3, 5).reshape(KW, KW)


def set_ends(entries, stream_key, low, largest):
    dims = entries.shape
    place = [jax.random.randint(jax.random.fold_in(stream_key, axis), (), 0, dims[axis]) for axis in range(len(dims))]
    entries = entries.at[tuple(place)].set(low)
    longest = dims.index(max(dims))
    place[longest] = (place[longest] + 1) % dims[longest]
    return entries.at[tuple(place)].set(largest)


def block_scale(key, extent, shards, least, top_value):
    gain = 1.0
    for position, shards_of in shards:
        draws = jax.random.uniform(jax.random.fold_in(jax.random.fold_in(key, 6), position), (shards_of,), jnp.float32, least / len(shards), top_value / len(shards))
        gain = gain * jnp.repeat(jnp.exp(draws), extent[position] // shards_of).reshape((-1,) + (1,) * (len(extent) - 1 - position))
    return gain


def bell_draw(rng, dims, deviation, reach, cuts=(), kind=jnp.bfloat16):
    values = jax.random.normal(rng, dims, jnp.float32) * deviation
    if len(cuts) > 0:
        values = block_scale(rng, dims, cuts, -0.22, 0.18) * values
    return jnp.clip(values, min=-reach, max=reach).astype(kind)


def setup_inputs(seed: int = 0) -> dict:
    seeds = jax.random.split(jax.random.key(seed), 7)
    return {
        "residual": bell_draw(seeds[0], (PROMPTS, LEN, D), 1.0, 6.0, ((0, 16), (2, 8))),
        "positions": set_ends(jax.random.randint(seeds[1], (PROMPTS,), 0, LEN), jax.random.fold_in(seeds[1], 1), 0, LEN - 1).astype(jnp.int32),
        "norm_gain": jnp.clip(1.0 + 0.18 * jax.random.normal(seeds[2], (D,), jnp.float32), 0.1, 1.9),
        "w_gate": bell_draw(seeds[3], (D, KW), D ** -0.5, 0.078125, ((0, 8), (1, 16))),
        "w_up": bell_draw(seeds[4], (D, KW), D ** -0.5, 0.078125, ((0, 8), (1, 16))),
        "covariance": draw_covariance(jax.random.fold_in(seeds[6], 71), 0),
    }


EPSILON = 1e-06

def to_natural(stored):
    tile_rows = KW // (N_ROW * TILE)
    tile_cols = KW // (N_COL * TILE)
    return stored.reshape(N_ROW, tile_rows, TILE, N_COL, tile_cols, TILE).transpose(1, 0, 2, 4, 3, 5).reshape(KW, KW)

def to_stored(natural):
    tile_rows = KW // (N_ROW * TILE)
    tile_cols = KW // (N_COL * TILE)
    return natural.reshape(tile_rows, N_ROW, TILE, tile_cols, N_COL, TILE).transpose(1, 0, 2, 4, 3, 5).reshape(KW, KW)

def reference(residual, positions, norm_gain, w_gate, w_up, covariance):
    prompt_total = residual.shape[0]
    pick_index = jnp.broadcast_to(positions[:, None, None], (prompt_total, 1, D))
    subject = jnp.take_along_axis(residual, pick_index, axis=1)[:, 0, :].astype(jnp.float32)
    inverse_rms = lax.rsqrt(lax.optimization_barrier(jnp.mean(subject * subject, axis=1, keepdims=True)) + EPSILON)
    normed = (subject * inverse_rms * norm_gain[None, :]).astype(jnp.bfloat16)
    gate_total = jnp.dot(normed.astype(jnp.float32), w_gate.astype(jnp.float32), preferred_element_type=jnp.float32)
    up_total = jnp.dot(normed.astype(jnp.float32), w_up.astype(jnp.float32), preferred_element_type=jnp.float32)
    raw_keys = jax.nn.silu(gate_total) * up_total
    key_scale = lax.rsqrt(lax.optimization_barrier(jnp.mean(raw_keys * raw_keys, axis=1, keepdims=True)) + EPSILON)
    unit_keys = (raw_keys * key_scale).astype(jnp.bfloat16)
    keys_outer = lax.dot_general(unit_keys.astype(jnp.float32), unit_keys.astype(jnp.float32), (((0,), (0,)), ((), ())), preferred_element_type=jnp.float32)
    matrix = to_natural(covariance) + keys_outer * (1.0 / prompt_total)
    indices = jnp.arange(KW, dtype=jnp.int32)
    for number in range(NPANEL):
        panel_start = number * PANEL
        panel_cols = matrix[:, panel_start:panel_start + PANEL]
        diag_block = panel_cols[panel_start:panel_start + PANEL]
        lower_factor = jnp.linalg.cholesky(diag_block)
        solved = jax.scipy.linalg.solve_triangular(lower_factor, panel_cols.T, lower=True).T
        shifted = indices - panel_start
        within = (shifted >= 0) & (shifted < PANEL)
        from_lower = jnp.take(lower_factor, jnp.clip(shifted, 0, PANEL - 1).astype(jnp.int32), axis=0)
        panel_factor = jnp.where((shifted >= PANEL)[:, None], solved, jnp.where(within[:, None], from_lower, jnp.zeros_like(solved)))
        matrix = matrix - lax.dot_general(panel_factor.astype(jnp.float32), panel_factor.astype(jnp.float32), (((1,), (1,)), ((), ())), precision=lax.Precision.HIGHEST, preferred_element_type=jnp.float32)
        matrix = matrix.at[:, panel_start:panel_start + PANEL].set(panel_factor)
    result = jnp.where(indices[:, None] >= indices[None, :], matrix, jnp.zeros_like(matrix))
    return to_stored(result)
```

```python
import functools

import jax
import jax.numpy as jnp
from jax import lax
from jax.experimental import pallas as pl
from jax.experimental.pallas import tpu as pltpu
from jax.sharding import Mesh
from jax.sharding import PartitionSpec as P

MESH = pl.DeviceIdType.MESH
BF16 = jnp.bfloat16
F32 = jnp.float32
EPSILON = 1e-06
HIDDEN = 16384
WIDTH = 5120
PROMPTS = 1024
VMEM_LIMIT = 60 * 1024 * 1024
BASE = 16


def here():
    return tuple(lax.axis_index(name) for name in ("x", "y", "z", "k"))


def moved(position, axis, step):
    place = list(position)
    size = 2 if axis == 3 else 4
    place[axis] = lax.rem(place[axis] + (step % size), size)
    return tuple(place)


def remote(src, dst, send, recv, target):
    return pltpu.make_async_remote_copy(
        src_ref=src, dst_ref=dst, send_sem=send, recv_sem=recv, device_id=target, device_id_type=MESH
    )


def greet(targets):
    barrier = pltpu.get_barrier_semaphore()
    for target in targets:
        pl.semaphore_signal(barrier, inc=1, device_id=target, device_id_type=MESH)
    pl.semaphore_wait(barrier, len(targets))


def when(condition, action):
    if condition is None:
        action()
    else:
        pl.when(condition)(action)


class PlaneGather:
    ORDER = (0, -1, 1, 2)

    def __init__(self, buf, rows, send, recv, pos, only=None):
        self.buf, self.rows, self.send, self.recv, self.pos, self.only = buf, rows, send, recv, pos, only

    def block(self, half, first, second):
        x, y = self.pos[0], self.pos[1]
        dx, dy = (second, first) if half == 0 else (first, second)
        return lax.rem(x + dx % 4, 4) * 4 + lax.rem(y + dy % 4, 4)

    def piece(self, half, first, second, part=None):
        size = self.rows // 2
        start = half * size
        if part is not None:
            size //= 2
            start += part * size
        return self.buf.at[self.block(half, first, second), pl.ds(start, size)]

    def copy(self, half, kind, first, second, axis, step, part=None):
        axis = axis if half == 0 else 1 - axis
        ref = self.piece(half, first, second, part)
        return remote(ref, ref, self.send.at[half, kind], self.recv.at[half, kind], moved(self.pos, axis, step))

    def sent(self):
        return {
            0: (0, 0, 1, 1, None), 1: (0, 0, 1, -1, None),
            2: (-1, 0, 1, 1, 0), 3: (1, 0, 1, -1, 1),
            4: (0, 0, 0, 1, None), 5: (-1, 0, 0, 1, None), 6: (1, 0, 0, 1, None), 7: (2, 0, 0, 1, None),
            8: (0, 0, 0, -1, None), 9: (-1, 0, 0, -1, None), 10: (1, 0, 0, -1, None), 11: (2, 0, 0, -1, None),
            12: (0, -1, 0, 1, None), 13: (-1, -1, 0, 1, None), 14: (1, 1, 0, -1, None), 15: (2, 1, 0, -1, None),
        }

    def got(self):
        return {
            0: (-1, 0, None), 1: (1, 0, None), 2: (2, 0, 0), 3: (2, 0, 1),
            4: (0, -1, None), 5: (-1, -1, None), 6: (1, -1, None), 7: (2, -1, None),
            8: (0, 1, None), 9: (-1, 1, None), 10: (1, 1, None), 11: (2, 1, None),
            12: (0, 2, None), 13: (-1, 2, None), 14: (1, 2, None), 15: (2, 2, None),
        }

    def go(self, half, kind):
        first, second, axis, step, part = self.sent()[kind]
        cond = None if self.only is None else self.block(half, first, second) < self.only
        when(cond, lambda: self.copy(half, kind, first, second, axis, step, part).start())

    def arrive(self, half, kind):
        first, second, part = self.got()[kind]
        cond = None if self.only is None else self.block(half, first, second) < self.only
        when(cond, lambda: self.copy(half, kind, first, second, 0, 1, part).wait_recv())

    def begin(self):
        for half in (0, 1):
            for kind in (0, 1, 4, 8):
                self.go(half, kind)

    def steps(self):
        for half in (0, 1):
            for kind, on in ((0, (2, 5, 9)), (1, (3, 6, 10))):
                self.arrive(half, kind)
                for nxt in on:
                    self.go(half, nxt)
                yield half, self.got()[kind][0], self.got()[kind][1]
        for half in (0, 1):
            self.arrive(half, 4)
            self.go(half, 12)
            yield half, 0, -1
            self.arrive(half, 8)
            yield half, 0, 1
        for half in (0, 1):
            self.arrive(half, 2)
            self.arrive(half, 3)
            self.go(half, 7)
            self.go(half, 11)
            yield half, 2, 0
        for half in (0, 1):
            for kind, nxt in ((5, 13), (10, 14), (9, None), (6, None), (11, 15), (7, None), (12, None), (13, None), (14, None), (15, None)):
                self.arrive(half, kind)
                if nxt is not None:
                    self.go(half, nxt)
                yield half, self.got()[kind][0], self.got()[kind][1]

    def finish(self):
        for half in (0, 1):
            for kind in range(16):
                first, second, axis, step, part = self.sent()[kind]
                cond = None if self.only is None else self.block(half, first, second) < self.only
                when(cond, lambda: self.copy(half, kind, first, second, axis, step, part).wait_send())


class ColumnGather:
    def __init__(self, buf, send, recv, pos):
        self.buf, self.send, self.recv, self.pos = buf, send, recv, pos

    def piece(self, dz, dk=0, part=None):
        z, k = self.pos[2], self.pos[3]
        slot = lax.rem(z + dz % 4, 4) * 2 + lax.rem(k + dk, 2)
        if part is None:
            return self.buf.at[slot]
        return self.buf.at[slot, pl.ds(32 * part, 32)]

    SENT = {0: (0, 2, 1, None), 1: (0, 2, -1, None), 2: (-1, 2, 1, 0), 3: (1, 2, -1, 1),
            4: (0, 3, 1, None), 5: (-1, 3, 1, None), 6: (1, 3, 1, None), 7: (2, 3, 1, None)}
    GOT = {0: (-1, 0, None), 1: (1, 0, None), 2: (2, 0, 0), 3: (2, 0, 1),
           4: (0, 1, None), 5: (-1, 1, None), 6: (1, 1, None), 7: (2, 1, None)}

    def go(self, kind):
        dz, axis, step, part = self.SENT[kind]
        ref = self.piece(dz, 0, part)
        remote(ref, ref, self.send.at[kind], self.recv.at[kind], moved(self.pos, axis, step)).start()

    def arrive(self, kind):
        dz, dk, part = self.GOT[kind]
        ref = self.piece(dz, dk, part)
        remote(ref, ref, self.send.at[kind], self.recv.at[kind], moved(self.pos, 2, 1)).wait_recv()

    def begin(self):
        for kind in (0, 1, 4):
            self.go(kind)

    def middle(self):
        self.arrive(0)
        self.go(2)
        self.go(5)
        self.arrive(1)
        self.go(3)
        self.go(6)

    def end(self):
        self.arrive(2)
        self.arrive(3)
        self.go(7)
        for kind in (4, 5, 6, 7):
            self.arrive(kind)

    def finish(self):
        for kind in range(8):
            dz, axis, step, part = self.SENT[kind]
            ref = self.piece(dz, 0, part)
            remote(ref, ref, self.send.at[kind], self.recv.at[kind], moved(self.pos, axis, step)).wait_send()


def column_peers(pos):
    peers = []
    for dz in range(4):
        for dk in range(2):
            if dz or dk:
                peers.append(moved(moved(pos, 2, dz), 3, dk))
    return peers


def to_all_columns(buf, send, recv, pos):
    copies = []
    mine = pos[2] * 2 + pos[3]
    number = 0
    for dz in range(4):
        for dk in range(2):
            if dz == 0 and dk == 0:
                continue
            target = moved(moved(pos, 2, dz), 3, dk)
            out = remote(buf.at[mine], buf.at[mine], send.at[number], recv.at[number], target)
            origin = moved(moved(pos, 2, -dz), 3, -dk)
            slot = origin[2] * 2 + origin[3]
            into = remote(buf.at[slot], buf.at[slot], send.at[number], recv.at[number], target)
            copies.append((out, into))
            number += 1
    return copies


def to_axis(buf, send, recv, pos, axis):
    copies = []
    mine = pos[axis]
    for step in (1, 2, 3):
        target = moved(pos, axis, step)
        out = remote(buf.at[mine], buf.at[mine], send.at[step - 1], recv.at[step - 1], target)
        slot = moved(pos, axis, -step)[axis]
        into = remote(buf.at[slot], buf.at[slot], send.at[step - 1], recv.at[step - 1], target)
        copies.append((out, into))
    return copies


def exchange(copies):
    for out, _ in copies:
        out.start()
    for _, into in copies:
        into.wait_recv()


def keys_kernel(
    subject_ref, gain_ref, gate_ref, up_ref, keys_ref,
    xx, own_w, other_w, sel_w, squares, part, hop_out, hop_in, total, sum_y, sum_x, sum_c,
    local_sem, w_send, w_recv, sq_send, sq_recv, x_send, x_recv, sib_send, sib_recv,
    hop_send, hop_recv, sy_send, sy_recv, sx_send, sx_recv, sc_send, sc_recv,
):
    pos = here()
    x, y, z, k = pos
    sibling = moved(pos, 3, 1)
    plane = [moved(pos, axis, step) for axis in (0, 1) for step in (1, 2, 3)]
    greet(plane + column_peers(pos))

    for index, ref in enumerate((gate_ref, up_ref)):
        remote(ref, other_w.at[index], w_send.at[index], w_recv.at[index], sibling).start()
        pltpu.make_async_copy(ref, own_w.at[index], local_sem.at[index]).start()

    subject = subject_ref[...].astype(F32)
    squared = subject * subject
    folded = squared[:, 0:128]
    for group in range(1, 5):
        folded = folded + squared[:, group * 128 : (group + 1) * 128]
    col = z * 2 + k
    squares[col] = folded
    square_copies = to_all_columns(squares, sq_send, sq_recv, pos)
    exchange(square_copies)
    everyone = squares[0]
    for member in range(1, 8):
        everyone = everyone + squares[member]
    inverse_rms = lax.rsqrt(jnp.sum(everyone, axis=1, keepdims=True) / WIDTH + EPSILON)
    mine = x * 4 + y
    xx[k, mine] = (subject * inverse_rms * gain_ref[...]).astype(BF16)

    gather = PlaneGather(xx.at[k], 64, x_send, x_recv, pos)
    gather.begin()

    def to_sibling(half, kind, first, second):
        ref = gather.piece(half, first, second)
        return remote(ref, ref, sib_send.at[half, kind], sib_recv.at[half, kind], sibling)

    def from_sibling(half, kind, first, second):
        block = gather.block(half, first, second)
        ref = xx.at[1 - k, block, pl.ds(half * 32, 32)]
        return remote(ref, ref, sib_send.at[half, kind], sib_recv.at[half, kind], sibling)

    passed = []
    for half in (0, 1):
        to_sibling(half, 0, 0, 0).start()
        passed.append((half, 0, 0, 0))

    def select(source, core):
        def body(step, carry):
            for index in range(2):
                low = source[index, :, pl.ds(pl.multiple_of(step * 128, 128), 128)]
                high = source[index, :, pl.ds(pl.multiple_of(512 + step * 128, 128), 128)]

                @pl.when(k == 0)
                def _():
                    sel_w[step, pl.ds(pl.multiple_of(core * 640, 128), 640), pl.ds(index * 128, 128)] = jnp.concatenate(
                        [low[:, :64], high[:, :64]], axis=1
                    )

                @pl.when(k == 1)
                def _():
                    sel_w[step, pl.ds(pl.multiple_of(core * 640, 128), 640), pl.ds(index * 128, 128)] = jnp.concatenate(
                        [low[:, 64:], high[:, 64:]], axis=1
                    )

            return carry

        lax.fori_loop(0, 4, body, 0)

    number = [1, 1]
    for count, (half, first, second) in enumerate(gather.steps()):
        kind = number[half]
        number[half] += 1
        to_sibling(half, kind, first, second).start()
        passed.append((half, kind, first, second))
        if count == 3:
            for index, ref in enumerate((gate_ref, up_ref)):
                pltpu.make_async_copy(ref, own_w.at[index], local_sem.at[index]).wait()
            select(own_w, k)
        if count == 7:
            for index, ref in enumerate((gate_ref, up_ref)):
                remote(ref, other_w.at[index], w_send.at[index], w_recv.at[index], sibling).wait_recv()
            select(other_w, 1 - k)
    for half, kind, first, second in passed:
        from_sibling(half, kind, first, second).wait_recv()

    def product(direction, dest):
        blocks = pl.ds(direction * 8, 8)
        left = xx[0, blocks].reshape(512, 640)
        right = xx[1, blocks].reshape(512, 640)
        return jnp.dot(left, sel_w[dest, 0:640], preferred_element_type=F32) + jnp.dot(
            right, sel_w[dest, 640:1280], preferred_element_type=F32
        )

    def hop(direction, step, sub):
        target = moved(pos, 2, 1 if direction == 0 else -1)
        return remote(
            hop_out.at[direction, step, sub], hop_in.at[direction, step, sub],
            hop_send.at[direction, step, sub], hop_recv.at[direction, step, sub], target,
        )

    def dest_of(direction, step):
        return lax.rem(z + (3 - step if direction == 0 else 1 + step), 4)

    for direction in (0, 1):
        value = product(direction, dest_of(direction, 0)).astype(BF16)
        for sub in (0, 1):
            hop_out[direction, 0, sub] = value[sub * 256 : (sub + 1) * 256]
            hop(direction, 0, sub).start()
    for step in (1, 2, 3):
        for direction in (0, 1):
            part[direction, step - 1] = product(direction, dest_of(direction, step))
    for step in (1, 2, 3):
        for sub in (0, 1):
            for direction in (0, 1):
                hop(direction, step - 1, sub).wait_recv()
                value = part[direction, step - 1, sub * 256 : (sub + 1) * 256] + hop_in[direction, step - 1, sub].astype(F32)
                if step < 3:
                    hop_out[direction, step, sub] = value.astype(BF16)
                    hop(direction, step, sub).start()
                else:
                    gate, up = value[:, :128], value[:, 128:]
                    raw = gate / (1.0 + jnp.exp(-gate)) * up
                    start = direction * 512 + sub * 256
                    total[:, start : start + 256] = raw.T
    raw = total[...]
    mass = jnp.sum(raw * raw, axis=0, keepdims=True)
    sum_y[y] = jnp.broadcast_to(mass, (8, PROMPTS))
    y_copies = to_axis(sum_y, sy_send, sy_recv, pos, 1)
    exchange(y_copies)
    sum_x[x] = sum_y[0] + sum_y[1] + sum_y[2] + sum_y[3]
    x_copies = to_axis(sum_x, sx_send, sx_recv, pos, 0)
    exchange(x_copies)
    sum_c[col] = sum_x[0] + sum_x[1] + sum_x[2] + sum_x[3]
    c_copies = to_all_columns(sum_c, sc_send, sc_recv, pos)
    exchange(c_copies)
    mass = sum_c[0]
    for member in range(1, 8):
        mass = mass + sum_c[member]
    scale = lax.rsqrt(mass[0:1] / HIDDEN + EPSILON)
    keys_ref[...] = (raw * scale).astype(BF16)

    for index, ref in enumerate((gate_ref, up_ref)):
        remote(ref, other_w.at[index], w_send.at[index], w_recv.at[index], sibling).wait_send()
    for copies in (square_copies, y_copies, x_copies, c_copies):
        for out, _ in copies:
            out.wait_send()
    gather.finish()
    for half, kind, first, second in passed:
        to_sibling(half, kind, first, second).wait_send()
    for direction in (0, 1):
        for step in range(3):
            for sub in (0, 1):
                hop(direction, step, sub).wait_send()


def make_keys(subject, gain, w_gate, w_up):
    dma = pltpu.SemaphoreType.DMA
    return pl.pallas_call(
        keys_kernel,
        name="make_keys",
        out_shape=jax.ShapeDtypeStruct((128, PROMPTS), BF16),
        in_specs=[pl.BlockSpec(memory_space=pltpu.VMEM)] * 2 + [pl.BlockSpec(memory_space=pl.ANY)] * 2,
        out_specs=pl.BlockSpec(memory_space=pltpu.VMEM),
        scratch_shapes=[
            pltpu.VMEM((2, 16, 64, 640), BF16),
            pltpu.VMEM((2, 640, 1024), BF16),
            pltpu.VMEM((2, 640, 1024), BF16),
            pltpu.VMEM((4, 1280, 256), BF16),
            pltpu.VMEM((8, 64, 128), F32),
            pltpu.VMEM((2, 3, 512, 256), F32),
            pltpu.VMEM((2, 3, 2, 256, 256), BF16),
            pltpu.VMEM((2, 3, 2, 256, 256), BF16),
            pltpu.VMEM((128, PROMPTS), F32),
            pltpu.VMEM((4, 8, PROMPTS), F32),
            pltpu.VMEM((4, 8, PROMPTS), F32),
            pltpu.VMEM((8, 8, PROMPTS), F32),
            dma((2,)), dma((2,)), dma((2,)), dma((7,)), dma((7,)), dma((2, 16)), dma((2, 16)), dma((2, 16)), dma((2, 16)),
            dma((2, 3, 2)), dma((2, 3, 2)), dma((3,)), dma((3,)), dma((3,)), dma((3,)), dma((7,)), dma((7,)),
        ],
        compiler_params=pltpu.CompilerParams(collective_id=0, has_side_effects=True, vmem_limit_bytes=VMEM_LIMIT),
    )(subject, gain, w_gate, w_up)


def spread_kernel(
    keys_ref, covr_ref, covc_ref, kc, kr, k5, cr, cc, jj,
    kc_send, kc_recv, k5_send, k5_recv, cr_send, cr_recv, cc_send, cc_recv, jj_send, jj_recv,
    row_send, row_recv, local_sem,
):
    pos = here()
    x, y, z, k = pos
    sibling = moved(pos, 3, 1)
    row = x * 4 + y
    col = z * 2 + k
    plane = [moved(pos, axis, step) for axis in (0, 1) for step in (1, -1)]
    ring = [moved(pos, 2, 1), moved(pos, 2, -1), sibling]
    greet(plane + ring)

    kc[row] = keys_ref[...]
    keys = PlaneGather(kc, 128, kc_send, kc_recv, pos)
    keys.begin()

    cr[col] = covr_ref[...]
    panel_rows = ColumnGather(cr, cr_send, cr_recv, pos)
    panel_rows.begin()

    @pl.when(row < 8)
    def _():
        cc[row] = covc_ref[...]

    covs = PlaneGather(cc, 64, cc_send, cc_recv, pos, only=8)
    covs.begin()

    panel_rows.middle()
    for _ in keys.steps():
        pass
    for _ in covs.steps():
        pass
    panel_rows.end()

    k5[col] = kc[0, 0:64]
    first_keys = ColumnGather(k5, k5_send, k5_recv, pos)
    first_keys.begin()
    jj[col] = cc[:, :, 0:64].reshape(512, 64).astype(F32).T.astype(BF16)
    corner = ColumnGather(jj, jj_send, jj_recv, pos)
    corner.begin()

    source = lax.rem(row, 8)
    source_z = source // 2
    source_k = lax.rem(source, 2)
    start = pl.multiple_of(row // 8 * 64, 64)
    away = lax.rem(z + 4 - source_z, 4)
    same = k == source_k

    def wave(group, kind, step, part=None, own=False):
        blocks = pl.ds(group * 4, 4)
        rows = pl.ds(0, 64) if part is None else pl.ds(part * 32, 32)
        dst = kr.at[blocks, rows]
        src = kc.at[blocks, pl.ds(start, 64)] if own else dst
        target = sibling if step == 0 else moved(pos, 2, step)
        return remote(src, dst, row_send.at[group, kind], row_recv.at[group, kind], target)

    def own_copy(group):
        blocks = pl.ds(group * 4, 4)
        return pltpu.make_async_copy(kc.at[blocks, pl.ds(start, 64)], kr.at[blocks], local_sem.at[group])

    @pl.when(same & (away == 0))
    def _():
        for group in range(4):
            wave(group, 0, 1, own=True).start()
            wave(group, 1, -1, own=True).start()
            wave(group, 2, 0, own=True).start()
            own_copy(group).start()

    first_keys.middle()
    corner.middle()
    first_keys.end()
    corner.end()

    @pl.when(same & (away == 1))
    def _():
        for group in range(4):
            wave(group, 0, 1).wait_recv()
            wave(group, 3, 1, part=0).start()
            wave(group, 2, 0).start()

    @pl.when(same & (away == 3))
    def _():
        for group in range(4):
            wave(group, 1, 1).wait_recv()
            wave(group, 4, -1, part=1).start()
            wave(group, 2, 0).start()

    @pl.when(same & (away == 2))
    def _():
        for group in range(4):
            wave(group, 3, 1, part=0).wait_recv()
            wave(group, 4, 1, part=1).wait_recv()
            wave(group, 2, 0).start()

    @pl.when(k != source_k)
    def _():
        for group in range(4):
            wave(group, 2, 0).wait_recv()

    @pl.when(same & (away == 0))
    def _():
        for group in range(4):
            wave(group, 0, 1, own=True).wait_send()
            wave(group, 1, -1, own=True).wait_send()
            wave(group, 2, 0, own=True).wait_send()
            own_copy(group).wait()

    @pl.when(same & (away == 1))
    def _():
        for group in range(4):
            wave(group, 3, 1, part=0).wait_send()
            wave(group, 2, 0).wait_send()

    @pl.when(same & (away == 3))
    def _():
        for group in range(4):
            wave(group, 4, -1, part=1).wait_send()
            wave(group, 2, 0).wait_send()

    @pl.when(same & (away == 2))
    def _():
        for group in range(4):
            wave(group, 2, 0).wait_send()

    keys.finish()
    covs.finish()
    panel_rows.finish()
    first_keys.finish()
    corner.finish()


def spread(keys, covr, covc):
    dma = pltpu.SemaphoreType.DMA
    return pl.pallas_call(
        spread_kernel,
        name="spread_keys",
        out_shape=(
            jax.ShapeDtypeStruct((16, 128, PROMPTS), BF16),
            jax.ShapeDtypeStruct((16, 64, PROMPTS), BF16),
            jax.ShapeDtypeStruct((8, 64, PROMPTS), BF16),
            jax.ShapeDtypeStruct((8, 64, 1024), BF16),
            jax.ShapeDtypeStruct((8, 64, 2048), BF16),
            jax.ShapeDtypeStruct((8, 64, 512), BF16),
        ),
        in_specs=[pl.BlockSpec(memory_space=pltpu.VMEM)] * 3,
        out_specs=(pl.BlockSpec(memory_space=pltpu.VMEM),) * 6,
        scratch_shapes=[
            dma((2, 16)), dma((2, 16)), dma((8,)), dma((8,)), dma((8,)), dma((8,)), dma((2, 16)), dma((2, 16)), dma((8,)), dma((8,)),
            dma((4, 5)), dma((4, 5)), dma((4,)),
        ],
        compiler_params=pltpu.CompilerParams(collective_id=1, has_side_effects=True, vmem_limit_bytes=VMEM_LIMIT),
    )(keys, covr, covc)


def split(value):
    high = value.astype(BF16)
    return high, (value - high.astype(F32)).astype(BF16)


def dot3(left, right, dims):
    lh, ll = split(left)
    rh, rl = split(right)
    dot = functools.partial(lax.dot_general, dimension_numbers=(dims, ((), ())), preferred_element_type=F32)
    return dot(lh, rh) + (dot(lh, rl) + dot(ll, rh))


def small_factor(work):
    lane = lax.broadcasted_iota(jnp.int32, (1, 128), 1)

    def body(step, carry):
        start = pl.multiple_of(step * BASE, BASE)
        rows = work[pl.ds(start, BASE), :]
        turned = pltpu.roll(rows[:, :128], lax.rem(128 - start, 128), 1)
        entry = [[jnp.broadcast_to(turned[i : i + 1, j : j + 1], (1, 128)) for j in range(i + 1)] for i in range(BASE)]
        solved = []
        for j in range(BASE):
            inverse = lax.rsqrt(entry[j][j])
            row = rows[j : j + 1, :]
            for m in range(j):
                row = row - jnp.concatenate([entry[j][m]] * 2, axis=1) * solved[m]
            solved.append(row * jnp.concatenate([inverse] * 2, axis=1))
            for i in range(j + 1, BASE):
                entry[i][j] = entry[i][j] * inverse
            for i in range(j + 1, BASE):
                for m in range(j + 1, i + 1):
                    entry[i][m] = entry[i][m] - entry[i][j] * entry[m][j]
        block = jnp.concatenate(solved, axis=0)
        work[pl.ds(start, BASE), :] = block
        later = jnp.where(lane >= start + BASE, block[:, :128], 0.0)
        lh, ll = split(later)
        rh, rl = split(block)
        left = jnp.concatenate([lh, lh, ll], axis=0)
        right = jnp.concatenate([rh, rl, rh], axis=0)
        work[...] = work[...] - lax.dot_general(left, right, (((0,), (0,)), ((), ())), preferred_element_type=F32)
        return carry

    lax.fori_loop(0, 128 // BASE, body, 0)


def factor_kernel(k5_ref, jj_ref, lower_ref, aug, work):
    keys = k5_ref[...].reshape(512, PROMPTS)
    outer = lax.dot_general(keys, keys, (((1,), (1,)), ((), ())), preferred_element_type=F32)
    aug[:, 0:512] = jj_ref[...].reshape(512, 512).astype(F32) + outer * (1.0 / PROMPTS)
    eye = (lax.broadcasted_iota(jnp.int32, (512, 512), 0) == lax.broadcasted_iota(jnp.int32, (512, 512), 1)).astype(F32)
    aug[:, 512:1024] = eye
    for number in range(4):
        lo, hi = number * 128, (number + 1) * 128
        work[:, 0:128] = aug[lo:hi, lo:hi]
        work[:, 128:256] = eye[0:128, 0:128]
        small_factor(work)
        inverse = work[:, 128:256]
        if hi < 512:
            right = dot3(inverse, aug[lo:hi, hi : 512 + lo], ((1,), (0,)))
            full = jnp.concatenate([right, inverse], axis=1)
            aug[lo:hi, hi : 512 + hi] = full
            ahead = right[:, 0 : 512 - hi]
            aug[hi:512, hi : 512 + hi] = aug[hi:512, hi : 512 + hi] - dot3(ahead, full, ((0,), (0,)))
        else:
            aug[lo:hi, 512 : 512 + lo] = dot3(inverse, aug[lo:hi, 512 : 512 + lo], ((1,), (0,)))
            aug[lo:hi, 512 + lo : 512 + hi] = inverse
    lower_ref[...] = aug[:, 512:1024]


def factor(k5, jj):
    return pl.pallas_call(
        factor_kernel,
        name="factor_corner",
        out_shape=jax.ShapeDtypeStruct((512, 512), F32),
        in_specs=[pl.BlockSpec(memory_space=pltpu.VMEM)] * 2,
        out_specs=pl.BlockSpec(memory_space=pltpu.VMEM),
        scratch_shapes=[pltpu.VMEM((512, 1024), F32), pltpu.VMEM((128, 256), F32)],
        compiler_params=pltpu.CompilerParams(vmem_limit_bytes=VMEM_LIMIT),
    )(k5, jj)


def update_kernel(cov_ref, kc_ref, kr_ref, k5_ref, cr_ref, cc_ref, inv_ref, out_ref, covb, outb, panel, in_sem, out_sem):
    x, y, z, k = here()
    row = x * 4 + y
    col = z * 2 + k
    scale = 1.0 / PROMPTS
    nt = (((1,), (1,)), ((), ()))
    nn = (((1,), (0,)), ((), ()))
    tn = (((0,), (0,)), ((), ()))
    dot = functools.partial(lax.dot_general, preferred_element_type=F32)

    def load(step):
        area = (pl.ds(step * 128, 1024 - step * 128), pl.ds(step * 256, 256))
        return pltpu.make_async_copy(cov_ref.at[area], covb.at[step % 2, pl.ds(step * 128, 1024 - step * 128)], in_sem.at[step % 2])

    def store(step):
        return pltpu.make_async_copy(outb.at[step % 2], out_ref.at[:, pl.ds(step * 256, 256)], out_sem.at[step % 2])

    load(0).start()
    load(1).start()
    inverse = inv_ref[...]
    inverse_high = inverse.astype(BF16)
    first = k5_ref[...].reshape(512, PROMPTS)
    rows = kr_ref[...].reshape(1024, PROMPTS)
    matrix_rows = cr_ref[...].reshape(512, 1024).astype(F32) + dot(first, rows, nt) * scale
    high, low = split(matrix_rows)
    panel[...] = dot(inverse_high, high, nn)
    own = inv_ref[pl.ds(pl.multiple_of(col * 64, 64), 64), :]
    own_high, own_low = split(own)
    own_panel = dot(own_high, high, nn) + (dot(own_low, high, nn) + dot(own_high, low, nn))
    panel_low = panel[...].astype(BF16)
    for step in range(8):
        top = step * 128
        height = 1024 - top
        load(step).wait()
        if step >= 2:
            store(step - 2).wait()
        cols = kc_ref[2 * step : 2 * step + 2].reshape(256, PROMPTS)
        matrix_cols = cc_ref[:, :, step * 256 : (step + 1) * 256].reshape(512, 256).astype(F32) + dot(first, cols, nt) * scale
        panel_cols = dot(inverse_high, matrix_cols.astype(BF16), nn).astype(BF16)
        value = covb[step % 2, top:1024] + dot(rows[top:], cols, nt) * scale - dot(panel_low[:, top:], panel_cols, tn)
        if step == 0:
            value = jnp.concatenate([own_panel.T, value[:, 64:]], axis=1)
        i = lax.broadcasted_iota(jnp.int32, (height, 256), 0) + top
        j = lax.broadcasted_iota(jnp.int32, (height, 256), 1) + step * 256
        row_global = (i // 64 * 16 + row) * 64 + i % 64
        col_global = (j // 64 * 8 + col) * 64 + j % 64
        outb[step % 2, top:1024] = jnp.where(row_global >= col_global, value, 0.0)
        if step:
            outb[step % 2, 0:top] = jnp.zeros((top, 256), F32)
        store(step).start()
        if step + 2 < 8:
            load(step + 2).start()
    store(6).wait()
    store(7).wait()


def update(cov, kc, kr, k5, cr, cc, inverse):
    dma = pltpu.SemaphoreType.DMA
    vmem = pl.BlockSpec(memory_space=pltpu.VMEM)
    return pl.pallas_call(
        update_kernel,
        name="update_lower",
        out_shape=jax.ShapeDtypeStruct((1024, 2048), F32),
        in_specs=[pl.BlockSpec(memory_space=pl.ANY)] + [vmem] * 6,
        out_specs=pl.BlockSpec(memory_space=pl.ANY),
        scratch_shapes=[
            pltpu.VMEM((2, 1024, 256), F32), pltpu.VMEM((2, 1024, 256), F32), pltpu.VMEM((512, 1024), F32), dma((2,)), dma((2,)),
        ],
        compiler_params=pltpu.CompilerParams(vmem_limit_bytes=VMEM_LIMIT),
    )(cov, kc, kr, k5, cr, cc, inverse)


def on_device(residual, positions, norm_gain, w_gate, w_up, covariance):
    prompts, tokens, _ = residual.shape
    token = lax.broadcasted_iota(jnp.int32, (prompts, tokens), 1)
    picked = jnp.where((token == positions[:, None])[:, :, None], residual, jnp.zeros_like(residual))
    subject = jnp.sum(picked.astype(F32), axis=1).astype(BF16)
    keys = make_keys(subject, norm_gain[None, :], w_gate, w_up)
    covr = covariance[:, 0:64].T.astype(BF16)
    covc = covariance[0:64, :].astype(BF16)
    kc, kr, k5, cr, cc, jj = spread(keys, covr, covc)
    inverse = factor(k5, jj)
    return update(covariance, kc, kr, k5, cr, cc, inverse)


def solution(mesh):
    torus = Mesh(mesh.devices.reshape(4, 4, 4, 2), ("x", "y", "z", "k"))
    row, col = ("x", "y"), ("z", "k")
    placed = (P(row, None, col), P(row), P(col), P(col, row), P(col, row), P(row, col))
    return jax.shard_map(on_device, mesh=torus, in_specs=placed, out_specs=P(row, col), check_vma=False)
```

```python
import functools

import jax
import jax.numpy as jnp
from jax import lax
from jax.experimental import pallas as pl
from jax.experimental.pallas import tpu as pltpu
from jax.sharding import Mesh
from jax.sharding import PartitionSpec as P

MESH = pl.DeviceIdType.MESH
BF16 = jnp.bfloat16
F32 = jnp.float32
EPSILON = 1e-06
HIDDEN = 16384
WIDTH = 5120
PROMPTS = 1024
VMEM_LIMIT = 60 * 1024 * 1024
BASE = 16


def here():
    return tuple(lax.axis_index(name) for name in ("x", "y", "z", "k"))


def moved(position, axis, step):
    place = list(position)
    size = 2 if axis == 3 else 4
    place[axis] = lax.rem(place[axis] + (step % size), size)
    return tuple(place)


def remote(src, dst, send, recv, target):
    return pltpu.make_async_remote_copy(
        src_ref=src, dst_ref=dst, send_sem=send, recv_sem=recv, device_id=target, device_id_type=MESH
    )


def greet(targets):
    barrier = pltpu.get_barrier_semaphore()
    for target in targets:
        pl.semaphore_signal(barrier, inc=1, device_id=target, device_id_type=MESH)
    pl.semaphore_wait(barrier, len(targets))


def when(condition, action):
    if condition is None:
        action()
    else:
        pl.when(condition)(action)


class PlaneGather:
    SENT = (
        (0, 0, 1, 1, None), (0, 0, 1, -1, None), (-1, 0, 1, 1, 0), (1, 0, 1, -1, 1),
        (0, 0, 0, 1, None), (-1, 0, 0, 1, None), (1, 0, 0, 1, None), (2, 0, 0, 1, None),
        (0, 0, 0, -1, None), (-1, 0, 0, -1, None), (1, 0, 0, -1, None), (2, 0, 0, -1, None),
        (0, -1, 0, 1, None), (-1, -1, 0, 1, None), (1, 1, 0, -1, None), (2, 1, 0, -1, None),
    )
    GOT = (
        (-1, 0, None), (1, 0, None), (2, 0, 0), (2, 0, 1),
        (0, -1, None), (-1, -1, None), (1, -1, None), (2, -1, None),
        (0, 1, None), (-1, 1, None), (1, 1, None), (2, 1, None),
        (0, 2, None), (-1, 2, None), (1, 2, None), (2, 2, None),
    )
    EVENTS = (
        ((0,), (2, 5, 9)), ((1,), (3, 6, 10)), ((4,), (12,)), ((8,), ()), ((2, 3), (7, 11)), ((5,), (13,)), ((10,), (14,)),
        ((9,), ()), ((6,), ()), ((11,), (15,)), ((7,), ()), ((12,), ()), ((13,), ()), ((14,), ()), ((15,), ()),
    )
    PLACES = tuple(((-1, 0), (1, 0), (0, -1), (0, 1), (2, 0), (-1, -1), (1, 1), (-1, 1), (1, -1), (2, 1), (2, -1), (0, 2), (-1, 2), (1, 2), (2, 2)))

    def __init__(self, buf, rows, send, recv, pos, only=None):
        self.buf, self.rows, self.send, self.recv, self.pos, self.only = buf, rows, send, recv, pos, only

    def block(self, half, first, second):
        dx, dy = (second, first) if half == 0 else (first, second)
        return lax.rem(self.pos[0] + dx % 4, 4), lax.rem(self.pos[1] + dy % 4, 4)

    def piece(self, half, first, second, part=None):
        size = self.rows // 2
        start = half * size
        if part is not None:
            size //= 2
            start += part * size
        bx, by = self.block(half, first, second)
        return self.buf.at[bx, by, pl.ds(start, size)]

    def cond(self, half, first, second):
        return None if self.only is None else self.only(*self.block(half, first, second))

    def copy(self, half, kind, first, second, axis, step, part=None):
        axis = axis if half == 0 else 1 - axis
        ref = self.piece(half, first, second, part)
        return remote(ref, ref, self.send.at[half, kind], self.recv.at[half, kind], moved(self.pos, axis, step))

    def go(self, half, kind):
        first, second, axis, step, part = self.SENT[kind]
        when(self.cond(half, first, second), lambda: self.copy(half, kind, first, second, axis, step, part).start())

    def arrive(self, half, kind):
        first, second, part = self.GOT[kind]
        when(self.cond(half, first, second), lambda: self.copy(half, kind, first, second, 0, 1, part).wait_recv())

    def begin(self):
        for kind in (0, 1, 4, 8):
            for half in (0, 1):
                self.go(half, kind)

    def event(self, number, half):
        kinds, on = self.EVENTS[number]
        for kind in kinds:
            self.arrive(half, kind)
        for kind in on:
            self.go(half, kind)

    def finish(self):
        for half in (0, 1):
            for kind in range(16):
                first, second, axis, step, part = self.SENT[kind]
                when(
                    self.cond(half, first, second),
                    lambda: self.copy(half, kind, first, second, axis, step, part).wait_send(),
                )


class ColumnGather:
    def __init__(self, buf, send, recv, pos):
        self.buf, self.send, self.recv, self.pos = buf, send, recv, pos

    def piece(self, dz, dk=0, part=None):
        z, k = self.pos[2], self.pos[3]
        slot = lax.rem(z + dz % 4, 4) * 2 + lax.rem(k + dk, 2)
        if part is None:
            return self.buf.at[slot]
        return self.buf.at[slot, pl.ds(32 * part, 32)]

    SENT = {0: (0, 2, 1, None), 1: (0, 2, -1, None), 2: (-1, 2, 1, 0), 3: (1, 2, -1, 1),
            4: (0, 3, 1, None), 5: (-1, 3, 1, None), 6: (1, 3, 1, None), 7: (2, 3, 1, None)}
    GOT = {0: (-1, 0, None), 1: (1, 0, None), 2: (2, 0, 0), 3: (2, 0, 1),
           4: (0, 1, None), 5: (-1, 1, None), 6: (1, 1, None), 7: (2, 1, None)}

    def go(self, kind):
        dz, axis, step, part = self.SENT[kind]
        ref = self.piece(dz, 0, part)
        remote(ref, ref, self.send.at[kind], self.recv.at[kind], moved(self.pos, axis, step)).start()

    def arrive(self, kind):
        dz, dk, part = self.GOT[kind]
        ref = self.piece(dz, dk, part)
        remote(ref, ref, self.send.at[kind], self.recv.at[kind], moved(self.pos, 2, 1)).wait_recv()

    def begin(self):
        for kind in (0, 1, 4):
            self.go(kind)

    def middle(self):
        self.arrive(0)
        self.go(2)
        self.go(5)
        self.arrive(1)
        self.go(3)
        self.go(6)

    def end(self):
        self.arrive(2)
        self.arrive(3)
        self.go(7)
        for kind in (4, 5, 6, 7):
            self.arrive(kind)

    def finish(self):
        for kind in range(8):
            dz, axis, step, part = self.SENT[kind]
            ref = self.piece(dz, 0, part)
            remote(ref, ref, self.send.at[kind], self.recv.at[kind], moved(self.pos, axis, step)).wait_send()


def column_peers(pos):
    peers = []
    for dz in range(4):
        for dk in range(2):
            if dz or dk:
                peers.append(moved(moved(pos, 2, dz), 3, dk))
    return peers


def to_all_columns(buf, send, recv, pos):
    copies = []
    mine = pos[2] * 2 + pos[3]
    number = 0
    for dz in range(4):
        for dk in range(2):
            if dz == 0 and dk == 0:
                continue
            target = moved(moved(pos, 2, dz), 3, dk)
            out = remote(buf.at[mine], buf.at[mine], send.at[number], recv.at[number], target)
            origin = moved(moved(pos, 2, -dz), 3, -dk)
            slot = origin[2] * 2 + origin[3]
            into = remote(buf.at[slot], buf.at[slot], send.at[number], recv.at[number], target)
            copies.append((out, into))
            number += 1
    return copies


def to_axis(buf, send, recv, pos, axis):
    copies = []
    mine = pos[axis]
    for step in (1, 2, 3):
        target = moved(pos, axis, step)
        out = remote(buf.at[mine], buf.at[mine], send.at[step - 1], recv.at[step - 1], target)
        slot = moved(pos, axis, -step)[axis]
        into = remote(buf.at[slot], buf.at[slot], send.at[step - 1], recv.at[step - 1], target)
        copies.append((out, into))
    return copies


def exchange(copies):
    for out, _ in copies:
        out.start()
    for _, into in copies:
        into.wait_recv()


def keys_kernel(
    subject_ref, gain_ref, gate_ref, up_ref, cov_ref, keys_ref, cc, jj_ref, cr_ref,
    xx, own_w, other_w, sel_w, squares, part, hop_out, hop_in, total, sum_y, sum_x, sum_c, cov_rows, cov_cols,
    local_sem, w_send, w_recv, sq_send, sq_recv, x_send, x_recv, sib_send, sib_recv,
    hop_send, hop_recv, sy_send, sy_recv, sx_send, sx_recv, sc_send, sc_recv, cc_send, cc_recv,
):
    pos = here()
    x, y, z, k = pos
    sibling = moved(pos, 3, 1)
    col = z * 2 + k
    plane = [moved(pos, axis, step) for axis in (0, 1) for step in (1, 2, 3)]
    greet(plane + column_peers(pos))

    weights = ((gate_ref, 0), (up_ref, 1))

    def swap(ref, index):
        return remote(ref, other_w.at[index], w_send.at[index], w_recv.at[index], sibling)

    def fetch(ref, index):
        return pltpu.make_async_copy(ref, own_w.at[index], local_sem.at[index])

    fetch_rows = pltpu.make_async_copy(cov_ref.at[pl.ds(0, 64)], cov_rows, local_sem.at[2])
    fetch_cols = pltpu.make_async_copy(cov_ref.at[:, pl.ds(0, 128)], cov_cols, local_sem.at[3])

    subject = subject_ref[...].astype(F32)
    squared = subject * subject
    folded = squared[:, 0:128]
    for group in range(1, 5):
        folded = folded + squared[:, group * 128 : (group + 1) * 128]
    squares[col] = folded
    square_copies = to_all_columns(squares, sq_send, sq_recv, pos)
    for out, _ in square_copies:
        out.start()
    for ref, index in weights:
        fetch(ref, index).start()
        swap(ref, index).start()
    fetch_rows.start()
    fetch_cols.start()

    def select(source, core):
        def body(step, carry):
            for index in range(2):
                low = source[index, :, pl.ds(pl.multiple_of(step * 128, 128), 128)]
                high = source[index, :, pl.ds(pl.multiple_of(512 + step * 128, 128), 128)]

                @pl.when(k == 0)
                def _():
                    sel_w[step, pl.ds(pl.multiple_of(core * 640, 128), 640), pl.ds(index * 128, 128)] = jnp.concatenate(
                        [low[:, :64], high[:, :64]], axis=1
                    )

                @pl.when(k == 1)
                def _():
                    sel_w[step, pl.ds(pl.multiple_of(core * 640, 128), 640), pl.ds(index * 128, 128)] = jnp.concatenate(
                        [low[:, 64:], high[:, 64:]], axis=1
                    )

            return carry

        lax.fori_loop(0, 4, body, 0)

    for _, into in square_copies:
        into.wait_recv()
    everyone = squares[0]
    for member in range(1, 8):
        everyone = everyone + squares[member]
    inverse_rms = lax.rsqrt(jnp.sum(everyone, axis=1, keepdims=True) / WIDTH + EPSILON)
    xx[k, x, y] = (subject * inverse_rms * gain_ref[...]).astype(BF16)

    gather = PlaneGather(xx.at[k], 64, x_send, x_recv, pos)
    gather.begin()

    def to_sibling(half, number, first, second):
        ref = gather.piece(half, first, second)
        return remote(ref, ref, sib_send.at[half, number], sib_recv.at[half, number], sibling)

    def from_sibling(half, number, first, second):
        bx, by = gather.block(half, first, second)
        ref = xx.at[1 - k, bx, by, pl.ds(half * 32, 32)]
        return remote(ref, ref, sib_send.at[half, number], sib_recv.at[half, number], sibling)

    places = ((0, 0),) + PlaneGather.PLACES
    for half in (0, 1):
        to_sibling(half, 0, 0, 0).start()

    for ref, index in weights:
        fetch(ref, index).wait()
    select(own_w, k)

    def arrivals(numbers):
        for number in numbers:
            for half in (0, 1):
                gather.event(number, half)
                to_sibling(half, number + 1, *places[number + 1]).start()

    def siblings(numbers):
        for number in numbers:
            for half in (0, 1):
                from_sibling(half, number, *places[number]).wait_recv()

    def line(core, half, second):
        if half == 0:
            value = xx[core, lax.rem(x + second % 4, 4), :, 0:32, :]
        else:
            value = xx[core, :, lax.rem(y + second % 4, 4), 32:64, :]
        return value.reshape(128, 640)

    def product(chunk, dest):
        second = (0, -1, 1, 2)[chunk]
        value = None
        for core in (0, 1):
            left = jnp.concatenate([line(core, 0, second), line(core, 1, second)], axis=0)
            term = jnp.dot(left, sel_w[dest, core * 640 : core * 640 + 640], preferred_element_type=F32)
            value = term if value is None else value + term
        return value

    def dest(step):
        return lax.rem(z + step % 4, 4)

    def hop(chunk, kind):
        target = moved(pos, 2, 1 if kind % 2 == 0 else -1)
        return remote(
            hop_out.at[chunk, kind], hop_in.at[chunk, kind], hop_send.at[chunk, kind], hop_recv.at[chunk, kind], target
        )

    def send(chunk, kind, value):
        hop_out[chunk, kind] = value.astype(BF16)
        hop(chunk, kind).start()

    def multiply(chunk):
        value = product(chunk, dest(2))
        send(chunk, 0, value[:128])
        send(chunk, 1, value[128:])
        value = product(chunk, dest(1))
        send(chunk, 2, value[128:])
        part[chunk, 0] = value[:128]
        value = product(chunk, dest(-1))
        send(chunk, 3, value[:128])
        part[chunk, 1] = value[128:]
        value = product(chunk, dest(0))
        part[chunk, 2] = value[:128]
        part[chunk, 3] = value[128:]

    def join(chunk):
        hop(chunk, 0).wait_recv()
        send(chunk, 4, part[chunk, 0] + hop_in[chunk, 0].astype(F32))
        hop(chunk, 1).wait_recv()
        send(chunk, 5, part[chunk, 1] + hop_in[chunk, 1].astype(F32))

    def finish(chunk):
        second = (0, -1, 1, 2)[chunk]
        for half in (0, 1):
            kinds = (4, 3) if half == 0 else (2, 5)
            for kind in kinds:
                hop(chunk, kind).wait_recv()
            value = part[chunk, 2 + half] + (hop_in[chunk, kinds[0]].astype(F32) + hop_in[chunk, kinds[1]].astype(F32))
            gate, up = value[:, :128], value[:, 128:]
            raw = gate / (1.0 + jnp.exp(-gate)) * up
            place = lax.rem((x if half == 0 else y) + second % 4, 4)
            total[:, pl.ds(pl.multiple_of(half * 512 + place * 128, 128), 128)] = raw.T

    covs = PlaneGather(cc, 64, cc_send, cc_recv, pos, only=lambda bx, by: bx < 2)

    def cov_events(numbers):
        for number in numbers:
            for half in (0, 1):
                covs.event(number, half)

    arrivals((0, 1, 4))
    for ref, index in weights:
        swap(ref, index).wait_recv()
    select(other_w, 1 - k)
    arrivals((2, 3))
    siblings((0, 1, 2, 5))
    multiply(0)
    arrivals((5, 8, 10))
    siblings((3, 6, 9, 11))
    multiply(1)
    join(0)
    arrivals((6, 7, 9))
    siblings((4, 7, 8, 10))
    multiply(2)
    join(1)
    arrivals((11, 12, 13, 14))

    fetch_rows.wait()

    @pl.when(x < 2)
    def _():
        cc[x, y] = cov_rows[...].astype(BF16)

    covs.begin()
    siblings((12, 13, 14, 15))
    multiply(3)
    join(2)
    fetch_cols.wait()
    cr_ref[...] = cov_cols[...].T[0:64].astype(BF16)
    cov_events((0, 1))
    finish(0)
    cov_events((2, 3, 4))
    join(3)
    finish(1)
    cov_events((5, 6))
    finish(2)
    cov_events((7, 8, 9))
    finish(3)
    raw = total[...]
    mass = jnp.sum(raw * raw, axis=0, keepdims=True)
    sum_y[y] = jnp.broadcast_to(mass, (8, PROMPTS))
    y_copies = to_axis(sum_y, sy_send, sy_recv, pos, 1)
    exchange(y_copies)
    sum_x[x] = sum_y[0] + sum_y[1] + sum_y[2] + sum_y[3]
    x_copies = to_axis(sum_x, sx_send, sx_recv, pos, 0)
    exchange(x_copies)
    sum_c[col] = sum_x[0] + sum_x[1] + sum_x[2] + sum_x[3]
    c_copies = to_all_columns(sum_c, sc_send, sc_recv, pos)
    exchange(c_copies)
    mass = sum_c[0]
    for member in range(1, 8):
        mass = mass + sum_c[member]
    scale = lax.rsqrt(mass[0:1] / HIDDEN + EPSILON)
    keys_ref[...] = (raw * scale).astype(BF16)
    cov_events((10, 11, 12, 13, 14))
    jj_ref[...] = cc[:, :, :, 0:128].reshape(512, 128).astype(F32).T[0:64].astype(BF16)

    for ref, index in weights:
        swap(ref, index).wait_send()
    for copies in (square_copies, y_copies, x_copies, c_copies):
        for out, _ in copies:
            out.wait_send()
    gather.finish()
    covs.finish()
    for half in (0, 1):
        for number in range(16):
            to_sibling(half, number, *places[number]).wait_send()
    for chunk in range(4):
        for kind in range(6):
            hop(chunk, kind).wait_send()


def make_keys(subject, gain, w_gate, w_up, cov):
    dma = pltpu.SemaphoreType.DMA
    vmem = pl.BlockSpec(memory_space=pltpu.VMEM)
    return pl.pallas_call(
        keys_kernel,
        name="make_keys",
        out_shape=(
            jax.ShapeDtypeStruct((128, PROMPTS), BF16),
            jax.ShapeDtypeStruct((2, 4, 64, 2048), BF16),
            jax.ShapeDtypeStruct((64, 512), BF16),
            jax.ShapeDtypeStruct((64, 1024), BF16),
        ),
        in_specs=[vmem] * 2 + [pl.BlockSpec(memory_space=pl.ANY)] * 3,
        out_specs=(vmem,) * 4,
        scratch_shapes=[
            pltpu.VMEM((2, 4, 4, 64, 640), BF16),
            pltpu.VMEM((2, 640, 1024), BF16),
            pltpu.VMEM((2, 640, 1024), BF16),
            pltpu.VMEM((4, 1280, 256), BF16),
            pltpu.VMEM((8, 64, 128), F32),
            pltpu.VMEM((4, 4, 128, 256), F32),
            pltpu.VMEM((4, 6, 128, 256), BF16),
            pltpu.VMEM((4, 6, 128, 256), BF16),
            pltpu.VMEM((128, PROMPTS), F32),
            pltpu.VMEM((4, 8, PROMPTS), F32),
            pltpu.VMEM((4, 8, PROMPTS), F32),
            pltpu.VMEM((8, 8, PROMPTS), F32),
            pltpu.VMEM((64, 2048), F32),
            pltpu.VMEM((1024, 128), F32),
            dma((4,)), dma((2,)), dma((2,)), dma((7,)), dma((7,)), dma((2, 16)), dma((2, 16)), dma((2, 16)), dma((2, 16)),
            dma((4, 6)), dma((4, 6)), dma((3,)), dma((3,)), dma((3,)), dma((3,)), dma((7,)), dma((7,)), dma((2, 16)), dma((2, 16)),
        ],
        compiler_params=pltpu.CompilerParams(collective_id=0, has_side_effects=True, vmem_limit_bytes=VMEM_LIMIT),
    )(subject, gain, w_gate, w_up, cov)


def split(value):
    high = value.astype(BF16)
    return high, (value - high.astype(F32)).astype(BF16)


def dot3(left, right, dims):
    lh, ll = split(left)
    rh, rl = split(right)
    dot = functools.partial(lax.dot_general, dimension_numbers=(dims, ((), ())), preferred_element_type=F32)
    return dot(lh, rh) + (dot(lh, rl) + dot(ll, rh))


def small_factor(work, extra):
    lane = lax.broadcasted_iota(jnp.int32, (1, 128), 1)

    def body(step, carry):
        start = pl.multiple_of(step * BASE, BASE)
        rows = work[pl.ds(start, BASE), :]
        turned = pltpu.roll(rows[:, :128], lax.rem(128 - start, 128), 1)
        entry = [[jnp.broadcast_to(turned[i : i + 1, j : j + 1], (1, 128)) for j in range(i + 1)] for i in range(BASE)]
        solved = []
        for j in range(BASE):
            inverse = lax.rsqrt(entry[j][j])
            row = rows[j : j + 1, :]
            for m in range(j):
                row = row - jnp.concatenate([entry[j][m]] * 2, axis=1) * solved[m]
            solved.append(row * jnp.concatenate([inverse] * 2, axis=1))
            for i in range(j + 1, BASE):
                entry[i][j] = entry[i][j] * inverse
            for i in range(j + 1, BASE):
                for m in range(j + 1, i + 1):
                    entry[i][m] = entry[i][m] - entry[i][j] * entry[m][j]
        block = jnp.concatenate(solved, axis=0)
        work[pl.ds(start, BASE), :] = block
        later = jnp.where(lane >= start + BASE, block[:, :128], 0.0)
        lh, ll = split(later)
        rh, rl = split(block)
        left = jnp.concatenate([lh, lh, ll], axis=0)
        right = jnp.concatenate([rh, rl, rh], axis=0)
        work[...] = work[...] - lax.dot_general(left, right, (((0,), (0,)), ((), ())), preferred_element_type=F32)
        for number, action in extra.items():
            pl.when(step == number)(action)
        return carry

    lax.fori_loop(0, 128 // BASE, body, 0)


def factor(aug, work, extras):
    eye = (lax.broadcasted_iota(jnp.int32, (128, 128), 0) == lax.broadcasted_iota(jnp.int32, (128, 128), 1)).astype(F32)
    for number in range(4):
        lo, hi = number * 128, (number + 1) * 128
        work[:, 0:128] = aug[lo:hi, lo:hi]
        work[:, 128:256] = eye
        small_factor(work, extras[number])
        inverse = work[:, 128:256]
        if hi < 512:
            right = dot3(inverse, aug[lo:hi, hi : 512 + lo], ((1,), (0,)))
            full = jnp.concatenate([right, inverse], axis=1)
            aug[lo:hi, hi : 512 + hi] = full
            ahead = right[:, 0 : 512 - hi]
            aug[hi:512, hi : 512 + hi] = aug[hi:512, hi : 512 + hi] - dot3(ahead, full, ((0,), (0,)))
        else:
            aug[lo:hi, 512 : 512 + lo] = dot3(inverse, aug[lo:hi, 512 : 512 + lo], ((1,), (0,)))
            aug[lo:hi, 512 + lo : 512 + hi] = inverse


def spread_kernel(
    keys_ref, jjb_ref, crb_ref, kc, kr, k5, cr, inv_ref, first, jj, aug, work,
    kc_send, kc_recv, k5_send, k5_recv, cr_send, cr_recv, jj_send, jj_recv, f_send, f_recv, row_send, row_recv, local_sem,
):
    pos = here()
    x, y, z, k = pos
    sibling = moved(pos, 3, 1)
    row = x * 4 + y
    col = z * 2 + k
    plane = [moved(pos, axis, step) for axis in (0, 1) for step in (1, -1)]
    ring = [moved(pos, 2, 1), moved(pos, 2, -1), sibling]
    greet(plane + ring)

    @pl.when(row == 0)
    def _():
        first[0, 0] = keys_ref[0:64]

    first_tile = PlaneGather(first, 64, f_send, f_recv, pos, only=lambda bx, by: (bx == 0) & (by == 0))
    first_tile.begin()
    jj[col] = jjb_ref[...]
    corner = ColumnGather(jj, jj_send, jj_recv, pos)
    corner.begin()
    kc[x, y] = keys_ref[...]
    keys = PlaneGather(kc, 128, kc_send, kc_recv, pos)
    keys.begin()

    source = lax.rem(row, 8)
    source_z = source // 2
    upper = row // 8
    away = lax.rem(z + 4 - source_z, 4)
    same = k == lax.rem(source, 2)
    places = ((0, 0),) + PlaneGather.PLACES

    def wave(number, kind, own=False):
        one, two = keys.block(0, *places[number]), keys.block(1, *places[number])
        bx = jnp.where(upper == 0, one[0], two[0])
        by = jnp.where(upper == 0, one[1], two[1])
        part = kind % 2
        dst = kr.at[bx, by, pl.ds(part * 32, 32)]
        src = kc.at[bx, by, pl.ds(pl.multiple_of(upper * 64 + part * 32, 32), 32)] if own else dst
        target = sibling if kind >= 2 else moved(pos, 2, 1 if kind == 0 else -1)
        return remote(src, dst, row_send.at[number, kind], row_recv.at[number, kind], target)

    def own_copy(number):
        one, two = keys.block(0, *places[number]), keys.block(1, *places[number])
        bx = jnp.where(upper == 0, one[0], two[0])
        by = jnp.where(upper == 0, one[1], two[1])
        return pltpu.make_async_copy(
            kc.at[bx, by, pl.ds(pl.multiple_of(upper * 64, 64), 64)], kr.at[bx, by], local_sem.at[number]
        )

    def relay(number):
        if number < 16:

            @pl.when(same & (away == 0))
            def _():
                for kind in (0, 1, 2, 3):
                    wave(number, kind, own=True).start()
                own_copy(number).start()

        for distance in (1, 2, 3):
            for kind, lag in ((0, distance), (1, 4 - distance)):
                block = number - lag
                if 0 <= block < 16:

                    @pl.when(same & (away == distance))
                    def _():
                        wave(block, kind).wait_recv()
                        if lag < 3:
                            wave(block, kind).start()
                        wave(block, kind + 2).start()

    def key_event(number):
        if number < 15:
            keys.event(number, 0)
            keys.event(number, 1)
        relay(number + 1)

    cr[col] = crb_ref[...]
    panel_rows = ColumnGather(cr, cr_send, cr_recv, pos)

    for number in range(15):
        first_tile.event(number, 0)
        first_tile.event(number, 1)
    k5[col] = first[0, 0]
    first_keys = ColumnGather(k5, k5_send, k5_recv, pos)
    first_keys.begin()
    corner.middle()
    relay(0)
    key_event(0)
    first_keys.middle()
    corner.end()
    key_event(1)
    first_keys.end()
    panel_rows.begin()
    key_event(2)

    corner_keys = k5[...].reshape(512, PROMPTS)
    outer = lax.dot_general(corner_keys, corner_keys, (((1,), (1,)), ((), ())), preferred_element_type=F32)
    aug[:, 0:512] = jj[...].reshape(512, 512).astype(F32) + outer * (1.0 / PROMPTS)
    aug[:, 512:1024] = (
        lax.broadcasted_iota(jnp.int32, (512, 512), 0) == lax.broadcasted_iota(jnp.int32, (512, 512), 1)
    ).astype(F32)
    beside = [functools.partial(key_event, number) for number in range(3, 18)]
    beside.insert(2, panel_rows.middle)
    beside.insert(5, panel_rows.end)
    extras = [{} for _ in range(4)]
    for number, action in enumerate(beside):
        extras[number // 8][number % 8] = action
    factor(aug, work, extras)
    inv_ref[...] = aug[:, 512:1024]

    for number in range(16):

        @pl.when(k != lax.rem(source, 2))
        def _():
            wave(number, 2).wait_recv()
            wave(number, 3).wait_recv()

        @pl.when(same & (away == 0))
        def _():
            for kind in range(4):
                wave(number, kind, own=True).wait_send()
            own_copy(number).wait()

        for distance in (1, 2, 3):

            @pl.when(same & (away == distance))
            def _():
                for kind, lag in ((0, distance), (1, 4 - distance)):
                    if lag < 3:
                        wave(number, kind).wait_send()
                    wave(number, kind + 2).wait_send()

    first_tile.finish()
    keys.finish()
    panel_rows.finish()
    first_keys.finish()
    corner.finish()


def spread(keys, jjb, crb):
    dma = pltpu.SemaphoreType.DMA
    vmem = pl.BlockSpec(memory_space=pltpu.VMEM)
    return pl.pallas_call(
        spread_kernel,
        name="spread_factor",
        out_shape=(
            jax.ShapeDtypeStruct((4, 4, 128, PROMPTS), BF16),
            jax.ShapeDtypeStruct((4, 4, 64, PROMPTS), BF16),
            jax.ShapeDtypeStruct((8, 64, PROMPTS), BF16),
            jax.ShapeDtypeStruct((8, 64, 1024), BF16),
            jax.ShapeDtypeStruct((512, 512), F32),
        ),
        in_specs=[vmem] * 3,
        out_specs=(vmem,) * 5,
        scratch_shapes=[
            pltpu.VMEM((1, 1, 64, PROMPTS), BF16),
            pltpu.VMEM((8, 64, 512), BF16),
            pltpu.VMEM((512, 1024), F32),
            pltpu.VMEM((128, 256), F32),
            dma((2, 16)), dma((2, 16)), dma((8,)), dma((8,)), dma((8,)), dma((8,)), dma((8,)), dma((8,)), dma((2, 16)), dma((2, 16)),
            dma((16, 4)), dma((16, 4)), dma((16,)),
        ],
        compiler_params=pltpu.CompilerParams(collective_id=1, has_side_effects=True, vmem_limit_bytes=VMEM_LIMIT),
    )(keys, jjb, crb)


def update_kernel(cov_ref, kc_ref, kr_ref, k5_ref, cr_ref, cc_ref, inv_ref, out_ref, covb, outb, panel, in_sem, out_sem):
    x, y, z, k = here()
    row = x * 4 + y
    col = z * 2 + k
    scale = 1.0 / PROMPTS
    nt = (((1,), (1,)), ((), ()))
    nn = (((1,), (0,)), ((), ()))
    tn = (((0,), (0,)), ((), ()))
    dot = functools.partial(lax.dot_general, preferred_element_type=F32)

    def load(step):
        area = (pl.ds(step * 128, 1024 - step * 128), pl.ds(step * 256, 256))
        return pltpu.make_async_copy(cov_ref.at[area], covb.at[step % 2, pl.ds(step * 128, 1024 - step * 128)], in_sem.at[step % 2])

    def store(step):
        return pltpu.make_async_copy(outb.at[step % 2], out_ref.at[:, pl.ds(step * 256, 256)], out_sem.at[step % 2])

    load(0).start()
    load(1).start()
    inverse = inv_ref[...]
    inverse_high = inverse.astype(BF16)
    first = k5_ref[...].reshape(512, PROMPTS)
    rows = kr_ref[...].reshape(1024, PROMPTS)
    matrix_rows = cr_ref[...].reshape(512, 1024).astype(F32) + dot(first, rows, nt) * scale
    high, low = split(matrix_rows)
    panel[...] = dot(inverse_high, high, nn)
    own = inv_ref[pl.ds(pl.multiple_of(col * 64, 64), 64), :]
    own_high, own_low = split(own)
    own_panel = dot(own_high, high, nn) + (dot(own_low, high, nn) + dot(own_high, low, nn))
    panel_low = panel[...].astype(BF16)
    for step in range(8):
        top = step * 128
        height = 1024 - top
        load(step).wait()
        if step >= 2:
            store(step - 2).wait()
        cols = kc_ref[2 * step : 2 * step + 2].reshape(256, PROMPTS)
        matrix_cols = cc_ref[:, :, step * 256 : (step + 1) * 256].reshape(512, 256).astype(F32) + dot(first, cols, nt) * scale
        panel_cols = dot(inverse_high, matrix_cols.astype(BF16), nn).astype(BF16)
        value = covb[step % 2, top:1024] + dot(rows[top:], cols, nt) * scale - dot(panel_low[:, top:], panel_cols, tn)
        if step == 0:
            value = jnp.concatenate([own_panel.T, value[:, 64:]], axis=1)
        i = lax.broadcasted_iota(jnp.int32, (height, 256), 0) + top
        j = lax.broadcasted_iota(jnp.int32, (height, 256), 1) + step * 256
        row_global = (i // 64 * 16 + row) * 64 + i % 64
        col_global = (j // 64 * 8 + col) * 64 + j % 64
        outb[step % 2, top:1024] = jnp.where(row_global >= col_global, value, 0.0)
        if step:
            outb[step % 2, 0:top] = jnp.zeros((top, 256), F32)
        store(step).start()
        if step + 2 < 8:
            load(step + 2).start()
    store(6).wait()
    store(7).wait()


def update(cov, kc, kr, k5, cr, cc, inverse):
    dma = pltpu.SemaphoreType.DMA
    vmem = pl.BlockSpec(memory_space=pltpu.VMEM)
    return pl.pallas_call(
        update_kernel,
        name="update_lower",
        out_shape=jax.ShapeDtypeStruct((1024, 2048), F32),
        in_specs=[pl.BlockSpec(memory_space=pl.ANY)] + [vmem] * 6,
        out_specs=pl.BlockSpec(memory_space=pl.ANY),
        scratch_shapes=[
            pltpu.VMEM((2, 1024, 256), F32), pltpu.VMEM((2, 1024, 256), F32), pltpu.VMEM((512, 1024), F32), dma((2,)), dma((2,)),
        ],
        compiler_params=pltpu.CompilerParams(vmem_limit_bytes=VMEM_LIMIT),
    )(cov, kc, kr, k5, cr, cc, inverse)


def on_device(residual, positions, norm_gain, w_gate, w_up, covariance):
    prompts, tokens, _ = residual.shape
    token = lax.broadcasted_iota(jnp.int32, (prompts, tokens), 1)
    picked = jnp.where((token == positions[:, None])[:, :, None], residual, jnp.zeros_like(residual))
    subject = jnp.sum(picked.astype(F32), axis=1).astype(BF16)
    keys, cc, jjb, crb = make_keys(subject, norm_gain[None, :], w_gate, w_up, covariance)
    kc, kr, k5, cr, inverse = spread(keys, jjb, crb)
    kc = kc.reshape(16, 128, PROMPTS)
    kr = kr.reshape(16, 64, PROMPTS)
    cc = cc.reshape(8, 64, 2048)
    return update(covariance, kc, kr, k5, cr, cc, inverse)


def solution(mesh):
    torus = Mesh(mesh.devices.reshape(4, 4, 4, 2), ("x", "y", "z", "k"))
    row, col = ("x", "y"), ("z", "k")
    placed = (P(row, None, col), P(row), P(col), P(col, row), P(col, row), P(row, col))
    return jax.shard_map(on_device, mesh=torus, in_specs=placed, out_specs=P(row, col), check_vma=False)
```

```python
import functools

import jax
import jax.numpy as jnp
from jax import lax
from jax.experimental import pallas as pl
from jax.experimental.pallas import tpu as pltpu
from jax.sharding import Mesh
from jax.sharding import PartitionSpec as P

MESH = pl.DeviceIdType.MESH
BF16 = jnp.bfloat16
F32 = jnp.float32
EPSILON = 1e-06
HIDDEN = 16384
WIDTH = 5120
PROMPTS = 1024
VMEM_LIMIT = 60 * 1024 * 1024
BASE = 16
LAG = 2


def here():
    return tuple(lax.axis_index(name) for name in ("x", "y", "z", "k"))


def moved(position, axis, step):
    place = list(position)
    size = 2 if axis == 3 else 4
    place[axis] = lax.rem(place[axis] + (step % size), size)
    return tuple(place)


def remote(src, dst, send, recv, target):
    return pltpu.make_async_remote_copy(
        src_ref=src, dst_ref=dst, send_sem=send, recv_sem=recv, device_id=target, device_id_type=MESH
    )


def greet(targets):
    barrier = pltpu.get_barrier_semaphore()
    for target in targets:
        pl.semaphore_signal(barrier, inc=1, device_id=target, device_id_type=MESH)
    pl.semaphore_wait(barrier, len(targets))


def when(condition, action):
    if condition is None:
        action()
    else:
        pl.when(condition)(action)


class PlaneGather:
    SENT = (
        (0, 0, 1, 1, None), (0, 0, 1, -1, None), (-1, 0, 1, 1, 0), (1, 0, 1, -1, 1),
        (0, 0, 0, 1, None), (-1, 0, 0, 1, None), (1, 0, 0, 1, None), (2, 0, 0, 1, None),
        (0, 0, 0, -1, None), (-1, 0, 0, -1, None), (1, 0, 0, -1, None), (2, 0, 0, -1, None),
        (0, -1, 0, 1, None), (-1, -1, 0, 1, None), (1, 1, 0, -1, None), (2, 1, 0, -1, None),
    )
    GOT = (
        (-1, 0, None), (1, 0, None), (2, 0, 0), (2, 0, 1),
        (0, -1, None), (-1, -1, None), (1, -1, None), (2, -1, None),
        (0, 1, None), (-1, 1, None), (1, 1, None), (2, 1, None),
        (0, 2, None), (-1, 2, None), (1, 2, None), (2, 2, None),
    )
    EVENTS = (
        ((0,), (2, 5, 9)), ((1,), (3, 6, 10)), ((4,), (12,)), ((8,), ()), ((2, 3), (7, 11)), ((5,), (13,)), ((10,), (14,)),
        ((9,), ()), ((6,), ()), ((11,), (15,)), ((7,), ()), ((12,), ()), ((13,), ()), ((14,), ()), ((15,), ()),
    )
    PLACES = tuple(((-1, 0), (1, 0), (0, -1), (0, 1), (2, 0), (-1, -1), (1, 1), (-1, 1), (1, -1), (2, 1), (2, -1), (0, 2), (-1, 2), (1, 2), (2, 2)))

    def __init__(self, buf, rows, send, recv, pos, only=None):
        self.buf, self.rows, self.send, self.recv, self.pos, self.only = buf, rows, send, recv, pos, only

    def block(self, half, first, second):
        dx, dy = (second, first) if half == 0 else (first, second)
        return lax.rem(self.pos[0] + dx % 4, 4), lax.rem(self.pos[1] + dy % 4, 4)

    def piece(self, half, first, second, part=None):
        size = self.rows // 2
        start = half * size
        if part is not None:
            size //= 2
            start += part * size
        bx, by = self.block(half, first, second)
        return self.buf.at[bx, by, pl.ds(start, size)]

    def cond(self, half, first, second):
        return None if self.only is None else self.only(*self.block(half, first, second))

    def copy(self, half, kind, first, second, axis, step, part=None):
        axis = axis if half == 0 else 1 - axis
        ref = self.piece(half, first, second, part)
        return remote(ref, ref, self.send.at[half, kind], self.recv.at[half, kind], moved(self.pos, axis, step))

    def go(self, half, kind):
        first, second, axis, step, part = self.SENT[kind]
        when(self.cond(half, first, second), lambda: self.copy(half, kind, first, second, axis, step, part).start())

    def arrive(self, half, kind):
        first, second, part = self.GOT[kind]
        when(self.cond(half, first, second), lambda: self.copy(half, kind, first, second, 0, 1, part).wait_recv())

    def begin(self):
        for kind in (0, 1, 4, 8):
            for half in (0, 1):
                self.go(half, kind)

    def event(self, number, half):
        kinds, on = self.EVENTS[number]
        for kind in kinds:
            self.arrive(half, kind)
        for kind in on:
            self.go(half, kind)

    def finish(self):
        for half in (0, 1):
            for kind in range(16):
                first, second, axis, step, part = self.SENT[kind]
                when(
                    self.cond(half, first, second),
                    lambda: self.copy(half, kind, first, second, axis, step, part).wait_send(),
                )


class ColumnGather:
    def __init__(self, buf, send, recv, pos):
        self.buf, self.send, self.recv, self.pos = buf, send, recv, pos

    def piece(self, dz, dk=0, part=None):
        z, k = self.pos[2], self.pos[3]
        slot = lax.rem(z + dz % 4, 4) * 2 + lax.rem(k + dk, 2)
        if part is None:
            return self.buf.at[slot]
        return self.buf.at[slot, pl.ds(32 * part, 32)]

    SENT = {0: (0, 2, 1, None), 1: (0, 2, -1, None), 2: (-1, 2, 1, 0), 3: (1, 2, -1, 1),
            4: (0, 3, 1, None), 5: (-1, 3, 1, None), 6: (1, 3, 1, None), 7: (2, 3, 1, None)}
    GOT = {0: (-1, 0, None), 1: (1, 0, None), 2: (2, 0, 0), 3: (2, 0, 1),
           4: (0, 1, None), 5: (-1, 1, None), 6: (1, 1, None), 7: (2, 1, None)}

    def go(self, kind):
        dz, axis, step, part = self.SENT[kind]
        ref = self.piece(dz, 0, part)
        remote(ref, ref, self.send.at[kind], self.recv.at[kind], moved(self.pos, axis, step)).start()

    def arrive(self, kind):
        dz, dk, part = self.GOT[kind]
        ref = self.piece(dz, dk, part)
        remote(ref, ref, self.send.at[kind], self.recv.at[kind], moved(self.pos, 2, 1)).wait_recv()

    def begin(self):
        for kind in (0, 1, 4):
            self.go(kind)

    def middle(self):
        self.arrive(0)
        self.go(2)
        self.go(5)
        self.arrive(1)
        self.go(3)
        self.go(6)

    def end(self):
        self.arrive(2)
        self.arrive(3)
        self.go(7)
        for kind in (4, 5, 6, 7):
            self.arrive(kind)

    def finish(self):
        for kind in range(8):
            dz, axis, step, part = self.SENT[kind]
            ref = self.piece(dz, 0, part)
            remote(ref, ref, self.send.at[kind], self.recv.at[kind], moved(self.pos, axis, step)).wait_send()


def column_peers(pos):
    peers = []
    for dz in range(4):
        for dk in range(2):
            if dz or dk:
                peers.append(moved(moved(pos, 2, dz), 3, dk))
    return peers


def to_all_columns(buf, send, recv, pos):
    copies = []
    mine = pos[2] * 2 + pos[3]
    number = 0
    for dz in range(4):
        for dk in range(2):
            if dz == 0 and dk == 0:
                continue
            target = moved(moved(pos, 2, dz), 3, dk)
            out = remote(buf.at[mine], buf.at[mine], send.at[number], recv.at[number], target)
            origin = moved(moved(pos, 2, -dz), 3, -dk)
            slot = origin[2] * 2 + origin[3]
            into = remote(buf.at[slot], buf.at[slot], send.at[number], recv.at[number], target)
            copies.append((out, into))
            number += 1
    return copies


def to_axis(buf, send, recv, pos, axis):
    copies = []
    mine = pos[axis]
    for step in (1, 2, 3):
        target = moved(pos, axis, step)
        out = remote(buf.at[mine], buf.at[mine], send.at[step - 1], recv.at[step - 1], target)
        slot = moved(pos, axis, -step)[axis]
        into = remote(buf.at[slot], buf.at[slot], send.at[step - 1], recv.at[step - 1], target)
        copies.append((out, into))
    return copies


def exchange(copies):
    for out, _ in copies:
        out.start()
    for _, into in copies:
        into.wait_recv()


def split(value):
    high = value.astype(BF16)
    return high, (value - high.astype(F32)).astype(BF16)


def dot3(left, right, dims):
    lh, ll = split(left)
    rh, rl = split(right)
    dot = functools.partial(lax.dot_general, dimension_numbers=(dims, ((), ())), preferred_element_type=F32)
    return dot(lh, rh) + (dot(lh, rl) + dot(ll, rh))


def small_factor(work, extra):
    lane = lax.broadcasted_iota(jnp.int32, (1, 128), 1)

    def body(step, carry):
        start = pl.multiple_of(step * BASE, BASE)
        rows = work[pl.ds(start, BASE), :]
        turned = pltpu.roll(rows[:, :128], lax.rem(128 - start, 128), 1)
        entry = [[jnp.broadcast_to(turned[i : i + 1, j : j + 1], (1, 128)) for j in range(i + 1)] for i in range(BASE)]
        solved = []
        for j in range(BASE):
            inverse = lax.rsqrt(entry[j][j])
            row = rows[j : j + 1, :]
            for m in range(j):
                row = row - jnp.concatenate([entry[j][m]] * 2, axis=1) * solved[m]
            solved.append(row * jnp.concatenate([inverse] * 2, axis=1))
            for i in range(j + 1, BASE):
                entry[i][j] = entry[i][j] * inverse
            for i in range(j + 1, BASE):
                for m in range(j + 1, i + 1):
                    entry[i][m] = entry[i][m] - entry[i][j] * entry[m][j]
        block = jnp.concatenate(solved, axis=0)
        work[pl.ds(start, BASE), :] = block
        later = jnp.where(lane >= start + BASE, block[:, :128], 0.0)
        lh, ll = split(later)
        rh, rl = split(block)
        left = jnp.concatenate([lh, lh, ll], axis=0)
        right = jnp.concatenate([rh, rl, rh], axis=0)
        work[...] = work[...] - lax.dot_general(left, right, (((0,), (0,)), ((), ())), preferred_element_type=F32)
        for number, action in extra.items():
            pl.when(step == number)(action)
        return carry

    lax.fori_loop(0, 128 // BASE, body, 0)


def factor(aug, work, extras):
    eye = (lax.broadcasted_iota(jnp.int32, (128, 128), 0) == lax.broadcasted_iota(jnp.int32, (128, 128), 1)).astype(F32)
    for number in range(4):
        lo, hi = number * 128, (number + 1) * 128
        work[:, 0:128] = aug[lo:hi, lo:hi]
        work[:, 128:256] = eye
        small_factor(work, extras[number])
        inverse = work[:, 128:256]
        if hi < 512:
            right = dot3(inverse, aug[lo:hi, hi : 512 + lo], ((1,), (0,)))
            full = jnp.concatenate([right, inverse], axis=1)
            aug[lo:hi, hi : 512 + hi] = full
            ahead = right[:, 0 : 512 - hi]
            aug[hi:512, hi : 512 + hi] = aug[hi:512, hi : 512 + hi] - dot3(ahead, full, ((0,), (0,)))
        else:
            aug[lo:hi, 512 : 512 + lo] = dot3(inverse, aug[lo:hi, 512 : 512 + lo], ((1,), (0,)))
            aug[lo:hi, 512 + lo : 512 + hi] = inverse


def panel_kernel(
    subject_ref, gain_ref, gate_ref, up_ref, cov_ref, kc_out, kr_out, k5_out, cr_out, cc_out, inv_ref, scale_ref,
    kc, kr, k5, k5_scaled, cr, cc, first, jj, aug, work,
    xx, own_w, other_w, sel_w, squares, part, hop_out, hop_in, total, sum_y, sum_x, sum_c, cov_rows, cov_cols,
    local_sem, w_send, w_recv, sq_send, sq_recv, x_send, x_recv, sib_send, sib_recv,
    hop_send, hop_recv, sy_send, sy_recv, sx_send, sx_recv, sc_send, sc_recv, cc_send, cc_recv,
    kc_send, kc_recv, k5_send, k5_recv, cr_send, cr_recv, jj_send, jj_recv, f_send, f_recv, row_send, row_recv, out_sem,
):
    pos = here()
    x, y, z, k = pos
    sibling = moved(pos, 3, 1)
    col = z * 2 + k
    plane = [moved(pos, axis, step) for axis in (0, 1) for step in (1, 2, 3)]
    greet(plane + column_peers(pos))

    weights = ((gate_ref, 0), (up_ref, 1))

    def swap(ref, index):
        return remote(ref, other_w.at[index], w_send.at[index], w_recv.at[index], sibling)

    def fetch(ref, index):
        return pltpu.make_async_copy(ref, own_w.at[index], local_sem.at[index])

    fetch_rows = pltpu.make_async_copy(cov_ref.at[pl.ds(0, 64)], cov_rows, local_sem.at[2])
    fetch_cols = pltpu.make_async_copy(cov_ref.at[:, pl.ds(0, 128)], cov_cols, local_sem.at[3])

    subject = subject_ref[...].astype(F32)
    squared = subject * subject
    folded = squared[:, 0:128]
    for group in range(1, 5):
        folded = folded + squared[:, group * 128 : (group + 1) * 128]
    squares[col] = folded
    square_copies = to_all_columns(squares, sq_send, sq_recv, pos)
    for out, _ in square_copies:
        out.start()
    for ref, index in weights:
        fetch(ref, index).start()
        swap(ref, index).start()
    fetch_rows.start()
    fetch_cols.start()

    def select(source, core):
        def body(step, carry):
            for index in range(2):
                low = source[index, :, pl.ds(pl.multiple_of(step * 128, 128), 128)]
                high = source[index, :, pl.ds(pl.multiple_of(512 + step * 128, 128), 128)]

                @pl.when(k == 0)
                def _():
                    sel_w[step, pl.ds(pl.multiple_of(core * 640, 128), 640), pl.ds(index * 128, 128)] = jnp.concatenate(
                        [low[:, :64], high[:, :64]], axis=1
                    )

                @pl.when(k == 1)
                def _():
                    sel_w[step, pl.ds(pl.multiple_of(core * 640, 128), 640), pl.ds(index * 128, 128)] = jnp.concatenate(
                        [low[:, 64:], high[:, 64:]], axis=1
                    )

            return carry

        lax.fori_loop(0, 4, body, 0)

    for _, into in square_copies:
        into.wait_recv()
    everyone = squares[0]
    for member in range(1, 8):
        everyone = everyone + squares[member]
    inverse_rms = lax.rsqrt(jnp.sum(everyone, axis=1, keepdims=True) / WIDTH + EPSILON)
    xx[k, x, y] = (subject * inverse_rms * gain_ref[...]).astype(BF16)

    gather = PlaneGather(xx.at[k], 64, x_send, x_recv, pos)
    gather.begin()

    def to_sibling(half, number, first, second):
        ref = gather.piece(half, first, second)
        return remote(ref, ref, sib_send.at[half, number], sib_recv.at[half, number], sibling)

    def from_sibling(half, number, first, second):
        bx, by = gather.block(half, first, second)
        ref = xx.at[1 - k, bx, by, pl.ds(half * 32, 32)]
        return remote(ref, ref, sib_send.at[half, number], sib_recv.at[half, number], sibling)

    places = ((0, 0),) + PlaneGather.PLACES
    for half in (0, 1):
        to_sibling(half, 0, 0, 0).start()

    for ref, index in weights:
        fetch(ref, index).wait()
    select(own_w, k)

    def arrivals(numbers):
        for number in numbers:
            for half in (0, 1):
                gather.event(number, half)
                to_sibling(half, number + 1, *places[number + 1]).start()

    def siblings(numbers):
        for number in numbers:
            for half in (0, 1):
                from_sibling(half, number, *places[number]).wait_recv()

    def line(core, half, second):
        if half == 0:
            value = xx[core, lax.rem(x + second % 4, 4), :, 0:32, :]
        else:
            value = xx[core, :, lax.rem(y + second % 4, 4), 32:64, :]
        return value.reshape(128, 640)

    def product(chunk, dest):
        second = (0, -1, 1, 2)[chunk]
        value = None
        for core in (0, 1):
            left = jnp.concatenate([line(core, 0, second), line(core, 1, second)], axis=0)
            term = jnp.dot(left, sel_w[dest, core * 640 : core * 640 + 640], preferred_element_type=F32)
            value = term if value is None else value + term
        return value

    def dest(step):
        return lax.rem(z + step % 4, 4)

    def hop(chunk, kind):
        target = moved(pos, 2, 1 if kind % 2 == 0 else -1)
        return remote(
            hop_out.at[chunk, kind], hop_in.at[chunk, kind], hop_send.at[chunk, kind], hop_recv.at[chunk, kind], target
        )

    def send(chunk, kind, value):
        hop_out[chunk, kind] = value.astype(BF16)
        hop(chunk, kind).start()

    def multiply(chunk):
        value = product(chunk, dest(2))
        send(chunk, 0, value[:128])
        send(chunk, 1, value[128:])
        value = product(chunk, dest(1))
        send(chunk, 2, value[128:])
        part[chunk, 0] = value[:128]
        value = product(chunk, dest(-1))
        send(chunk, 3, value[:128])
        part[chunk, 1] = value[128:]
        value = product(chunk, dest(0))
        part[chunk, 2] = value[:128]
        part[chunk, 3] = value[128:]

    def join(chunk):
        hop(chunk, 0).wait_recv()
        send(chunk, 4, part[chunk, 0] + hop_in[chunk, 0].astype(F32))
        hop(chunk, 1).wait_recv()
        send(chunk, 5, part[chunk, 1] + hop_in[chunk, 1].astype(F32))

    def finish(chunk):
        second = (0, -1, 1, 2)[chunk]
        for half in (0, 1):
            kinds = (4, 3) if half == 0 else (2, 5)
            for kind in kinds:
                hop(chunk, kind).wait_recv()
            value = part[chunk, 2 + half] + (hop_in[chunk, kinds[0]].astype(F32) + hop_in[chunk, kinds[1]].astype(F32))
            gate, up = value[:, :128], value[:, 128:]
            raw = gate / (1.0 + jnp.exp(-gate)) * up
            place = lax.rem((x if half == 0 else y) + second % 4, 4)
            total[:, pl.ds(pl.multiple_of(half * 512 + place * 128, 128), 128)] = raw.T

    covs = PlaneGather(cc, 64, cc_send, cc_recv, pos, only=lambda bx, by: bx < 2)

    def cov_events(numbers):
        for number in numbers:
            for half in (0, 1):
                covs.event(number, half)

    arrivals((0, 1, 4))
    for ref, index in weights:
        swap(ref, index).wait_recv()
    select(other_w, 1 - k)
    arrivals((2, 3))
    siblings((0, 1, 2, 5))
    multiply(0)
    arrivals((5, 8, 10))
    siblings((3, 6, 9, 11))
    multiply(1)
    join(0)
    arrivals((6, 7, 9))
    siblings((4, 7, 8, 10))
    multiply(2)
    join(1)
    arrivals((11, 12, 13, 14))

    fetch_rows.wait()

    @pl.when(x < 2)
    def _():
        cc[x, y] = cov_rows[...].astype(BF16)

    covs.begin()
    siblings((12, 13, 14, 15))
    multiply(3)
    join(2)
    fetch_cols.wait()
    cr[col] = cov_cols[...].T[0:64].astype(BF16)
    cov_events((0, 1))
    finish(0)
    cov_events((2, 3, 4))
    join(3)
    finish(1)
    cov_events((5, 6))
    finish(2)
    cov_events((7, 8, 9))
    finish(3)
    raw = total[...]
    mass = jnp.sum(raw * raw, axis=0, keepdims=True)
    own_keys = raw.astype(BF16)
    row = x * 4 + y

    @pl.when(row == 0)
    def _():
        first[0, 0] = own_keys[0:64]

    first_tile = PlaneGather(first, 64, f_send, f_recv, pos, only=lambda bx, by: (bx == 0) & (by == 0))
    first_tile.begin()
    sum_y[y] = jnp.broadcast_to(mass, (8, PROMPTS))
    y_copies = to_axis(sum_y, sy_send, sy_recv, pos, 1)
    for out, _ in y_copies:
        out.start()
    kc[x, y] = own_keys
    keys = PlaneGather(kc, 128, kc_send, kc_recv, pos)
    keys.begin()
    cov_events((10, 11, 12, 13, 14))
    jj[col] = cc[:, :, :, 0:128].reshape(512, 128).astype(F32).T[0:64].astype(BF16)
    corner = ColumnGather(jj, jj_send, jj_recv, pos)
    corner.begin()
    for _, into in y_copies:
        into.wait_recv()
    sum_x[x] = sum_y[0] + sum_y[1] + sum_y[2] + sum_y[3]
    x_copies = to_axis(sum_x, sx_send, sx_recv, pos, 0)
    for out, _ in x_copies:
        out.start()

    def first_events(numbers):
        for number in numbers:
            first_tile.event(number, 0)
            first_tile.event(number, 1)

    first_events((0, 1, 2, 3))
    for _, into in x_copies:
        into.wait_recv()
    sum_c[col] = sum_x[0] + sum_x[1] + sum_x[2] + sum_x[3]
    c_copies = to_all_columns(sum_c, sc_send, sc_recv, pos)
    for out, _ in c_copies:
        out.start()
    first_events(range(4, 15))
    k5[col] = first[0, 0]
    first_keys = ColumnGather(k5, k5_send, k5_recv, pos)
    first_keys.begin()

    source = lax.rem(row, 8)
    source_z = source // 2
    upper = row // 8
    away = lax.rem(z + 4 - source_z, 4)
    same = k == lax.rem(source, 2)

    def wave(number, kind, own=False):
        one, two = keys.block(0, *places[number]), keys.block(1, *places[number])
        bx = jnp.where(upper == 0, one[0], two[0])
        by = jnp.where(upper == 0, one[1], two[1])
        part = kind % 2
        dst = kr.at[bx, by, pl.ds(part * 32, 32)]
        src = kc.at[bx, by, pl.ds(pl.multiple_of(upper * 64 + part * 32, 32), 32)] if own else dst
        target = sibling if kind >= 2 else moved(pos, 2, 1 if kind == 0 else -1)
        return remote(src, dst, row_send.at[number, kind], row_recv.at[number, kind], target)

    def own_copy(number):
        one, two = keys.block(0, *places[number]), keys.block(1, *places[number])
        bx = jnp.where(upper == 0, one[0], two[0])
        by = jnp.where(upper == 0, one[1], two[1])
        return pltpu.make_async_copy(
            kc.at[bx, by, pl.ds(pl.multiple_of(upper * 64, 64), 64)], kr.at[bx, by], out_sem.at[number]
        )

    def relay(number):
        if number < 16:

            @pl.when(same & (away == 0))
            def _():
                for kind in (0, 1, 2, 3):
                    wave(number, kind, own=True).start()
                own_copy(number).start()

        for distance in (1, 2, 3):
            for kind, hops in ((0, distance), (1, 4 - distance)):
                block = number - LAG * hops
                if 0 <= block < 16:

                    @pl.when(same & (away == distance))
                    def _():
                        wave(block, kind).wait_recv()
                        if hops < 3:
                            wave(block, kind).start()
                        wave(block, kind + 2).start()

    def key_event(number):
        if number < 15:
            keys.event(number, 0)
            keys.event(number, 1)
        relay(number + 1)

    panel_rows = ColumnGather(cr, cr_send, cr_recv, pos)
    corner.middle()
    relay(0)
    key_event(0)
    for _, into in c_copies:
        into.wait_recv()
    mass = sum_c[0]
    for member in range(1, 8):
        mass = mass + sum_c[member]
    scale = lax.rsqrt(mass / HIDDEN + EPSILON) * (1.0 / 32.0)
    scale_ref[...] = scale * scale
    first_keys.middle()
    corner.end()
    key_event(1)
    first_keys.end()
    panel_rows.begin()
    key_event(2)

    def save(number, source, target):
        return pltpu.make_async_copy(source, target, out_sem.at[16 + number])

    corner_raw = k5[...].reshape(512, PROMPTS).astype(F32)
    corner_keys = (corner_raw * scale[0:1]).astype(BF16)
    outer = lax.dot_general(corner_keys, corner_keys, (((1,), (1,)), ((), ())), preferred_element_type=F32)
    aug[:, 0:512] = jj[...].reshape(512, 512).astype(F32) + outer
    aug[:, 512:1024] = (
        lax.broadcasted_iota(jnp.int32, (512, 512), 0) == lax.broadcasted_iota(jnp.int32, (512, 512), 1)
    ).astype(F32)
    k5_scaled[...] = (corner_raw * (scale * scale)[0:1]).astype(BF16).reshape(8, 64, PROMPTS)
    save(0, k5_scaled, k5_out).start()
    save(1, cc, cc_out).start()
    beside = {
        3: 0, 4: 1, 5: 3, 6: 5, 7: 7, 8: 9, 9: 11, 10: 13, 11: 15, 12: 17, 13: 19, 14: 21, 15: 23, 16: 24, 17: 25, 18: 26, 19: 28, 20: 30,
    }
    extras = [{} for _ in range(4)]
    for number, step in beside.items():
        extras[step // 8][step % 8] = functools.partial(key_event, number)
    extras[0][2] = panel_rows.middle
    extras[0][6] = panel_rows.end
    extras[2][6] = lambda: save(2, kc, kc_out).start()
    extras[2][4] = lambda: save(3, cr, cr_out).start()
    factor(aug, work, extras)
    inv_ref[...] = aug[:, 512:1024]

    for number in range(16):

        @pl.when(k != lax.rem(source, 2))
        def _():
            wave(number, 2).wait_recv()
            wave(number, 3).wait_recv()

        @pl.when(same & (away == 0))
        def _():
            for kind in range(4):
                wave(number, kind, own=True).wait_send()
            own_copy(number).wait()

        for distance in (1, 2, 3):

            @pl.when(same & (away == distance))
            def _():
                for kind, hops in ((0, distance), (1, 4 - distance)):
                    if hops < 3:
                        wave(number, kind).wait_send()
                    wave(number, kind + 2).wait_send()

    first_tile.finish()
    keys.finish()
    panel_rows.finish()
    first_keys.finish()
    corner.finish()
    save(4, kr, kr_out).start()
    for ref, index in weights:
        swap(ref, index).wait_send()
    for copies in (square_copies, y_copies, x_copies, c_copies):
        for out, _ in copies:
            out.wait_send()
    gather.finish()
    covs.finish()
    for half in (0, 1):
        for number in range(16):
            to_sibling(half, number, *places[number]).wait_send()
    for chunk in range(4):
        for kind in range(6):
            hop(chunk, kind).wait_send()
    save(0, k5_scaled, k5_out).wait()
    save(1, cc, cc_out).wait()
    save(2, kc, kc_out).wait()
    save(3, cr, cr_out).wait()
    save(4, kr, kr_out).wait()


def panel(subject, gain, w_gate, w_up, cov):
    dma = pltpu.SemaphoreType.DMA
    vmem = pl.BlockSpec(memory_space=pltpu.VMEM)
    anywhere = pl.BlockSpec(memory_space=pl.ANY)
    spread = (
        ((4, 4, 128, PROMPTS), BF16),
        ((4, 4, 64, PROMPTS), BF16),
        ((8, 64, PROMPTS), BF16),
        ((8, 64, 1024), BF16),
        ((2, 4, 64, 2048), BF16),
    )
    return pl.pallas_call(
        panel_kernel,
        name="keys_and_panel",
        out_shape=tuple(jax.ShapeDtypeStruct(*one) for one in spread)
        + (jax.ShapeDtypeStruct((512, 512), F32), jax.ShapeDtypeStruct((8, PROMPTS), F32)),
        in_specs=[vmem] * 2 + [anywhere] * 3,
        out_specs=(anywhere,) * 5 + (vmem,) * 2,
        scratch_shapes=[
            pltpu.VMEM(*spread[0]), pltpu.VMEM(*spread[1]), pltpu.VMEM(*spread[2]), pltpu.VMEM(*spread[2]),
            pltpu.VMEM(*spread[3]), pltpu.VMEM(*spread[4]),
            pltpu.VMEM((1, 1, 64, PROMPTS), BF16),
            pltpu.VMEM((8, 64, 512), BF16),
            pltpu.VMEM((512, 1024), F32),
            pltpu.VMEM((128, 256), F32),
            pltpu.VMEM((2, 4, 4, 64, 640), BF16),
            pltpu.VMEM((2, 640, 1024), BF16),
            pltpu.VMEM((2, 640, 1024), BF16),
            pltpu.VMEM((4, 1280, 256), BF16),
            pltpu.VMEM((8, 64, 128), F32),
            pltpu.VMEM((4, 4, 128, 256), F32),
            pltpu.VMEM((4, 6, 128, 256), BF16),
            pltpu.VMEM((4, 6, 128, 256), BF16),
            pltpu.VMEM((128, PROMPTS), F32),
            pltpu.VMEM((4, 8, PROMPTS), F32),
            pltpu.VMEM((4, 8, PROMPTS), F32),
            pltpu.VMEM((8, 8, PROMPTS), F32),
            pltpu.VMEM((64, 2048), F32),
            pltpu.VMEM((1024, 128), F32),
            dma((4,)), dma((2,)), dma((2,)), dma((7,)), dma((7,)), dma((2, 16)), dma((2, 16)), dma((2, 16)), dma((2, 16)),
            dma((4, 6)), dma((4, 6)), dma((3,)), dma((3,)), dma((3,)), dma((3,)), dma((7,)), dma((7,)), dma((2, 16)), dma((2, 16)),
            dma((2, 16)), dma((2, 16)), dma((8,)), dma((8,)), dma((8,)), dma((8,)), dma((8,)), dma((8,)), dma((2, 16)), dma((2, 16)),
            dma((16, 4)), dma((16, 4)), dma((21,)),
        ],
        compiler_params=pltpu.CompilerParams(collective_id=0, has_side_effects=True, vmem_limit_bytes=VMEM_LIMIT),
    )(subject, gain, w_gate, w_up, cov)


def update_kernel(cov_ref, kc_ref, kr_ref, k5_ref, cr_ref, cc_ref, inv_ref, scale_ref, out_ref, covb, outb, panel, in_sem, out_sem):
    x, y, z, k = here()
    row = x * 4 + y
    col = z * 2 + k
    nt = (((1,), (1,)), ((), ()))
    nn = (((1,), (0,)), ((), ()))
    tn = (((0,), (0,)), ((), ()))
    dot = functools.partial(lax.dot_general, preferred_element_type=F32)

    def load(step):
        area = (pl.ds(step * 128, 1024 - step * 128), pl.ds(step * 256, 256))
        return pltpu.make_async_copy(cov_ref.at[area], covb.at[step % 2, pl.ds(step * 128, 1024 - step * 128)], in_sem.at[step % 2])

    def store(step):
        return pltpu.make_async_copy(outb.at[step % 2], out_ref.at[:, pl.ds(step * 256, 256)], out_sem.at[step % 2])

    load(0).start()
    load(1).start()
    inverse = inv_ref[...]
    inverse_high = inverse.astype(BF16)
    first = k5_ref[...].reshape(512, PROMPTS)
    raw_rows = kr_ref[...].reshape(1024, PROMPTS)
    rows = (raw_rows.astype(F32) * scale_ref[0:1]).astype(BF16)
    matrix_rows = cr_ref[...].reshape(512, 1024).astype(F32) + dot(first, raw_rows, nt)
    high, low = split(matrix_rows)
    panel[...] = dot(inverse_high, high, nn)
    own = inv_ref[pl.ds(pl.multiple_of(col * 64, 64), 64), :]
    own_high, own_low = split(own)
    own_panel = dot(own_high, high, nn) + (dot(own_low, high, nn) + dot(own_high, low, nn))
    panel_low = panel[...].astype(BF16)
    for step in range(8):
        top = step * 128
        height = 1024 - top
        load(step).wait()
        if step >= 2:
            store(step - 2).wait()
        cols = kc_ref[2 * step : 2 * step + 2].reshape(256, PROMPTS)
        matrix_cols = cc_ref[:, :, step * 256 : (step + 1) * 256].reshape(512, 256).astype(F32) + dot(first, cols, nt)
        panel_cols = dot(inverse_high, matrix_cols.astype(BF16), nn).astype(BF16)
        value = covb[step % 2, top:1024] + dot(rows[top:], cols, nt) - dot(panel_low[:, top:], panel_cols, tn)
        if step == 0:
            value = jnp.concatenate([own_panel.T, value[:, 64:]], axis=1)
        i = lax.broadcasted_iota(jnp.int32, (height, 256), 0) + top
        j = lax.broadcasted_iota(jnp.int32, (height, 256), 1) + step * 256
        row_global = (i // 64 * 16 + row) * 64 + i % 64
        col_global = (j // 64 * 8 + col) * 64 + j % 64
        outb[step % 2, top:1024] = jnp.where(row_global >= col_global, value, 0.0)
        if step:
            outb[step % 2, 0:top] = jnp.zeros((top, 256), F32)
        store(step).start()
        if step + 2 < 8:
            load(step + 2).start()
    store(6).wait()
    store(7).wait()


def update(cov, kc, kr, k5, cr, cc, inverse, scale):
    dma = pltpu.SemaphoreType.DMA
    vmem = pl.BlockSpec(memory_space=pltpu.VMEM)
    return pl.pallas_call(
        update_kernel,
        name="update_lower",
        out_shape=jax.ShapeDtypeStruct((1024, 2048), F32),
        in_specs=[pl.BlockSpec(memory_space=pl.ANY)] + [vmem] * 7,
        out_specs=pl.BlockSpec(memory_space=pl.ANY),
        scratch_shapes=[
            pltpu.VMEM((2, 1024, 256), F32), pltpu.VMEM((2, 1024, 256), F32), pltpu.VMEM((512, 1024), F32), dma((2,)), dma((2,)),
        ],
        compiler_params=pltpu.CompilerParams(vmem_limit_bytes=VMEM_LIMIT),
    )(cov, kc, kr, k5, cr, cc, inverse, scale)


def on_device(residual, positions, norm_gain, w_gate, w_up, covariance):
    prompts, tokens, _ = residual.shape
    token = lax.broadcasted_iota(jnp.int32, (prompts, tokens), 1)
    picked = jnp.where((token == positions[:, None])[:, :, None], residual, jnp.zeros_like(residual))
    subject = jnp.sum(picked.astype(F32), axis=1).astype(BF16)
    kc, kr, k5, cr, cc, inverse, scale = panel(subject, norm_gain[None, :], w_gate, w_up, covariance)
    kc = kc.reshape(16, 128, PROMPTS)
    kr = kr.reshape(16, 64, PROMPTS)
    cc = cc.reshape(8, 64, 2048)
    return update(covariance, kc, kr, k5, cr, cc, inverse, scale)


def solution(mesh):
    torus = Mesh(mesh.devices.reshape(4, 4, 4, 2), ("x", "y", "z", "k"))
    row, col = ("x", "y"), ("z", "k")
    placed = (P(row, None, col), P(row), P(col), P(col, row), P(col, row), P(row, col))
    return jax.shard_map(on_device, mesh=torus, in_specs=placed, out_specs=P(row, col), check_vma=False)
```

```python
import functools

import jax
import jax.numpy as jnp
from jax import lax
from jax.experimental import pallas as pl
from jax.experimental.pallas import tpu as pltpu
from jax.sharding import Mesh
from jax.sharding import PartitionSpec as P

MESH = pl.DeviceIdType.MESH
BF16 = jnp.bfloat16
F32 = jnp.float32
EPSILON = 1e-06
HIDDEN = 16384
WIDTH = 5120
PROMPTS = 1024
VMEM_LIMIT = 60 * 1024 * 1024
BASE = 16
LAG = 2


def here():
    return tuple(lax.axis_index(name) for name in ("x", "y", "z", "k"))


def moved(position, axis, step):
    place = list(position)
    size = 2 if axis == 3 else 4
    place[axis] = lax.rem(place[axis] + (step % size), size)
    return tuple(place)


def remote(src, dst, send, recv, target):
    return pltpu.make_async_remote_copy(
        src_ref=src, dst_ref=dst, send_sem=send, recv_sem=recv, device_id=target, device_id_type=MESH
    )


def greet(targets):
    barrier = pltpu.get_barrier_semaphore()
    for target in targets:
        pl.semaphore_signal(barrier, inc=1, device_id=target, device_id_type=MESH)
    pl.semaphore_wait(barrier, len(targets))


def when(condition, action):
    if condition is None:
        action()
    else:
        pl.when(condition)(action)


class PlaneGather:
    SENT = (
        (0, 0, 1, 1, None), (0, 0, 1, -1, None), (-1, 0, 1, 1, 0), (1, 0, 1, -1, 1),
        (0, 0, 0, 1, None), (-1, 0, 0, 1, None), (1, 0, 0, 1, None), (2, 0, 0, 1, None),
        (0, 0, 0, -1, None), (-1, 0, 0, -1, None), (1, 0, 0, -1, None), (2, 0, 0, -1, None),
        (0, -1, 0, 1, None), (-1, -1, 0, 1, None), (1, 1, 0, -1, None), (2, 1, 0, -1, None),
    )
    GOT = (
        (-1, 0, None), (1, 0, None), (2, 0, 0), (2, 0, 1),
        (0, -1, None), (-1, -1, None), (1, -1, None), (2, -1, None),
        (0, 1, None), (-1, 1, None), (1, 1, None), (2, 1, None),
        (0, 2, None), (-1, 2, None), (1, 2, None), (2, 2, None),
    )
    EVENTS = (
        ((0,), (2, 5, 9)), ((1,), (3, 6, 10)), ((4,), (12,)), ((8,), ()), ((2, 3), (7, 11)), ((5,), (13,)), ((10,), (14,)),
        ((9,), ()), ((6,), ()), ((11,), (15,)), ((7,), ()), ((12,), ()), ((13,), ()), ((14,), ()), ((15,), ()),
    )
    PLACES = tuple(((-1, 0), (1, 0), (0, -1), (0, 1), (2, 0), (-1, -1), (1, 1), (-1, 1), (1, -1), (2, 1), (2, -1), (0, 2), (-1, 2), (1, 2), (2, 2)))

    def __init__(self, buf, rows, send, recv, pos, only=None):
        self.buf, self.rows, self.send, self.recv, self.pos, self.only = buf, rows, send, recv, pos, only

    def block(self, half, first, second):
        dx, dy = (second, first) if half == 0 else (first, second)
        return lax.rem(self.pos[0] + dx % 4, 4), lax.rem(self.pos[1] + dy % 4, 4)

    def piece(self, half, first, second, part=None):
        size = self.rows // 2
        start = half * size
        if part is not None:
            size //= 2
            start += part * size
        bx, by = self.block(half, first, second)
        return self.buf.at[bx, by, pl.ds(start, size)]

    def cond(self, half, first, second):
        return None if self.only is None else self.only(*self.block(half, first, second))

    def copy(self, half, kind, first, second, axis, step, part=None):
        axis = axis if half == 0 else 1 - axis
        ref = self.piece(half, first, second, part)
        return remote(ref, ref, self.send.at[half, kind], self.recv.at[half, kind], moved(self.pos, axis, step))

    def go(self, half, kind):
        first, second, axis, step, part = self.SENT[kind]
        when(self.cond(half, first, second), lambda: self.copy(half, kind, first, second, axis, step, part).start())

    def arrive(self, half, kind):
        first, second, part = self.GOT[kind]
        when(self.cond(half, first, second), lambda: self.copy(half, kind, first, second, 0, 1, part).wait_recv())

    def begin(self):
        for kind in (0, 1, 4, 8):
            for half in (0, 1):
                self.go(half, kind)

    def event(self, number, half):
        kinds, on = self.EVENTS[number]
        for kind in kinds:
            self.arrive(half, kind)
        for kind in on:
            self.go(half, kind)

    def finish(self):
        for half in (0, 1):
            for kind in range(16):
                first, second, axis, step, part = self.SENT[kind]
                when(
                    self.cond(half, first, second),
                    lambda: self.copy(half, kind, first, second, axis, step, part).wait_send(),
                )


class ColumnGather:
    def __init__(self, buf, send, recv, pos):
        self.buf, self.send, self.recv, self.pos = buf, send, recv, pos

    def piece(self, dz, dk=0, part=None):
        z, k = self.pos[2], self.pos[3]
        slot = lax.rem(z + dz % 4, 4) * 2 + lax.rem(k + dk, 2)
        if part is None:
            return self.buf.at[slot]
        return self.buf.at[slot, pl.ds(32 * part, 32)]

    SENT = {0: (0, 2, 1, None), 1: (0, 2, -1, None), 2: (-1, 2, 1, 0), 3: (1, 2, -1, 1),
            4: (0, 3, 1, None), 5: (-1, 3, 1, None), 6: (1, 3, 1, None), 7: (2, 3, 1, None)}
    GOT = {0: (-1, 0, None), 1: (1, 0, None), 2: (2, 0, 0), 3: (2, 0, 1),
           4: (0, 1, None), 5: (-1, 1, None), 6: (1, 1, None), 7: (2, 1, None)}

    def go(self, kind):
        dz, axis, step, part = self.SENT[kind]
        ref = self.piece(dz, 0, part)
        remote(ref, ref, self.send.at[kind], self.recv.at[kind], moved(self.pos, axis, step)).start()

    def arrive(self, kind):
        dz, dk, part = self.GOT[kind]
        ref = self.piece(dz, dk, part)
        remote(ref, ref, self.send.at[kind], self.recv.at[kind], moved(self.pos, 2, 1)).wait_recv()

    def begin(self):
        for kind in (0, 1, 4):
            self.go(kind)

    def middle(self):
        self.arrive(0)
        self.go(2)
        self.go(5)
        self.arrive(1)
        self.go(3)
        self.go(6)

    def end(self):
        self.arrive(2)
        self.arrive(3)
        self.go(7)
        for kind in (4, 5, 6, 7):
            self.arrive(kind)

    def finish(self):
        for kind in range(8):
            dz, axis, step, part = self.SENT[kind]
            ref = self.piece(dz, 0, part)
            remote(ref, ref, self.send.at[kind], self.recv.at[kind], moved(self.pos, axis, step)).wait_send()


def column_peers(pos):
    peers = []
    for dz in range(4):
        for dk in range(2):
            if dz or dk:
                peers.append(moved(moved(pos, 2, dz), 3, dk))
    return peers


def to_all_columns(buf, send, recv, pos):
    copies = []
    mine = pos[2] * 2 + pos[3]
    number = 0
    for dz in range(4):
        for dk in range(2):
            if dz == 0 and dk == 0:
                continue
            target = moved(moved(pos, 2, dz), 3, dk)
            out = remote(buf.at[mine], buf.at[mine], send.at[number], recv.at[number], target)
            origin = moved(moved(pos, 2, -dz), 3, -dk)
            slot = origin[2] * 2 + origin[3]
            into = remote(buf.at[slot], buf.at[slot], send.at[number], recv.at[number], target)
            copies.append((out, into))
            number += 1
    return copies


def to_axis(buf, send, recv, pos, axis):
    copies = []
    mine = pos[axis]
    for step in (1, 2, 3):
        target = moved(pos, axis, step)
        out = remote(buf.at[mine], buf.at[mine], send.at[step - 1], recv.at[step - 1], target)
        slot = moved(pos, axis, -step)[axis]
        into = remote(buf.at[slot], buf.at[slot], send.at[step - 1], recv.at[step - 1], target)
        copies.append((out, into))
    return copies


def exchange(copies):
    for out, _ in copies:
        out.start()
    for _, into in copies:
        into.wait_recv()


def split(value):
    high = value.astype(BF16)
    return high, (value - high.astype(F32)).astype(BF16)


def dot3(left, right, dims):
    lh, ll = split(left)
    rh, rl = split(right)
    dot = functools.partial(lax.dot_general, dimension_numbers=(dims, ((), ())), preferred_element_type=F32)
    return dot(lh, rh) + (dot(lh, rl) + dot(ll, rh))


def small_factor(work, extra):
    lane = lax.broadcasted_iota(jnp.int32, (1, 128), 1)

    def body(step, carry):
        start = pl.multiple_of(step * BASE, BASE)
        rows = work[pl.ds(start, BASE), :]
        turned = pltpu.roll(rows[:, :128], lax.rem(128 - start, 128), 1)
        entry = [[jnp.broadcast_to(turned[i : i + 1, j : j + 1], (1, 128)) for j in range(i + 1)] for i in range(BASE)]
        solved = []
        for j in range(BASE):
            inverse = lax.rsqrt(entry[j][j])
            row = rows[j : j + 1, :]
            for m in range(j):
                row = row - jnp.concatenate([entry[j][m]] * 2, axis=1) * solved[m]
            solved.append(row * jnp.concatenate([inverse] * 2, axis=1))
            for i in range(j + 1, BASE):
                entry[i][j] = entry[i][j] * inverse
            for i in range(j + 1, BASE):
                for m in range(j + 1, i + 1):
                    entry[i][m] = entry[i][m] - entry[i][j] * entry[m][j]
        block = jnp.concatenate(solved, axis=0)
        work[pl.ds(start, BASE), :] = block
        later = jnp.where(lane >= start + BASE, block[:, :128], 0.0)
        lh, ll = split(later)
        rh, rl = split(block)
        left = jnp.concatenate([lh, lh, ll], axis=0)
        right = jnp.concatenate([rh, rl, rh], axis=0)
        work[...] = work[...] - lax.dot_general(left, right, (((0,), (0,)), ((), ())), preferred_element_type=F32)
        for number, action in extra.items():
            pl.when(step == number)(action)
        return carry

    lax.fori_loop(0, 128 // BASE, body, 0)


def factor(aug, work, extras):
    eye = (lax.broadcasted_iota(jnp.int32, (128, 128), 0) == lax.broadcasted_iota(jnp.int32, (128, 128), 1)).astype(F32)
    for number in range(4):
        lo, hi = number * 128, (number + 1) * 128
        work[:, 0:128] = aug[lo:hi, lo:hi]
        work[:, 128:256] = eye
        small_factor(work, extras[number])
        inverse = work[:, 128:256]
        if hi < 512:
            right = dot3(inverse, aug[lo:hi, hi : 512 + lo], ((1,), (0,)))
            full = jnp.concatenate([right, inverse], axis=1)
            aug[lo:hi, hi : 512 + hi] = full
            ahead = right[:, 0 : 512 - hi]
            aug[hi:512, hi : 512 + hi] = aug[hi:512, hi : 512 + hi] - dot3(ahead, full, ((0,), (0,)))
        else:
            aug[lo:hi, 512 : 512 + lo] = dot3(inverse, aug[lo:hi, 512 : 512 + lo], ((1,), (0,)))
            aug[lo:hi, 512 + lo : 512 + hi] = inverse


def panel_kernel(
    residual_ref, positions_ref, gain_ref, gate_ref, up_ref, cov_ref, kc_out, kr_out, k5_out, cr_out, cc_out, inv_ref, scale_ref,
    kc, kr, k5, k5_scaled, cr, cc, first, jj, aug, work,
    xx, own_w, other_w, sel_w, squares, part, hop_out, hop_in, total, sum_y, sum_x, sum_c, cov_rows, cov_cols, cov_corner, tiles,
    local_sem, w_send, w_recv, sq_send, sq_recv, x_send, x_recv, sib_send, sib_recv,
    hop_send, hop_recv, sy_send, sy_recv, sx_send, sx_recv, sc_send, sc_recv, cc_send, cc_recv,
    kc_send, kc_recv, k5_send, k5_recv, cr_send, cr_recv, jj_send, jj_recv, f_send, f_recv, row_send, row_recv, out_sem, tile_send, tile_recv,
):
    pos = here()
    x, y, z, k = pos
    sibling = moved(pos, 3, 1)
    col = z * 2 + k
    plane = [moved(pos, axis, step) for axis in (0, 1) for step in (1, 2, 3)]
    barrier = pltpu.get_barrier_semaphore()
    peers = plane + column_peers(pos)
    for peer in peers:
        pl.semaphore_signal(barrier, inc=1, device_id=peer, device_id_type=MESH)

    weights = ((gate_ref, 0), (up_ref, 1))

    def swap(ref, index):
        return remote(ref, other_w.at[index], w_send.at[index], w_recv.at[index], sibling)

    def fetch(ref, index):
        return pltpu.make_async_copy(ref, own_w.at[index], local_sem.at[index])

    fetch_rows = pltpu.make_async_copy(cov_ref.at[pl.ds(0, 64)], cov_rows, local_sem.at[2])
    fetch_cols = pltpu.make_async_copy(cov_ref.at[:, pl.ds(0, 128)], cov_cols, local_sem.at[3])

    fetch_corner = pltpu.make_async_copy(cov_ref.at[pl.ds(0, 64), pl.ds(0, 128)], cov_corner, local_sem.at[4])
    fetch_corner.start()
    line_of = lax.broadcasted_iota(jnp.int32, (64, 64), 0)
    prompt_of = lax.broadcasted_iota(jnp.int32, (64, 64), 1)
    place = positions_ref[...].reshape(1, 64).astype(F32)
    place = jnp.sum(jnp.where(line_of == prompt_of, place, 0.0), axis=1, keepdims=True)
    token = lax.broadcasted_iota(jnp.int32, (64, 1024), 1) - 16 * lax.broadcasted_iota(jnp.int32, (64, 1024), 0)
    pick = (token.astype(F32) == place).astype(BF16)
    subject = jnp.dot(pick, residual_ref[...].reshape(1024, 640), preferred_element_type=F32)
    squared = subject * subject
    folded = squared[:, 0:128]
    for group in range(1, 5):
        folded = folded + squared[:, group * 128 : (group + 1) * 128]
    squares[col] = folded
    pl.semaphore_wait(barrier, len(peers))
    square_copies = to_all_columns(squares, sq_send, sq_recv, pos)
    for out, _ in square_copies:
        out.start()
    for ref, index in weights:
        fetch(ref, index).start()
        swap(ref, index).start()
    fetch_corner.wait()

    @pl.when(x < 2)
    def _():
        tiles[x, y] = cov_corner[...].astype(BF16)

    corner_tiles = PlaneGather(tiles, 64, tile_send, tile_recv, pos, only=lambda bx, by: bx < 2)
    corner_tiles.begin()

    def tile_events(numbers):
        for number in numbers:
            for half in (0, 1):
                corner_tiles.event(number, half)

    fetch_rows.start()
    fetch_cols.start()

    def select(source, core):
        def body(step, carry):
            for index in range(2):
                low = source[index, :, pl.ds(pl.multiple_of(step * 128, 128), 128)]
                high = source[index, :, pl.ds(pl.multiple_of(512 + step * 128, 128), 128)]

                @pl.when(k == 0)
                def _():
                    sel_w[step, pl.ds(pl.multiple_of(core * 640, 128), 640), pl.ds(index * 128, 128)] = jnp.concatenate(
                        [low[:, :64], high[:, :64]], axis=1
                    )

                @pl.when(k == 1)
                def _():
                    sel_w[step, pl.ds(pl.multiple_of(core * 640, 128), 640), pl.ds(index * 128, 128)] = jnp.concatenate(
                        [low[:, 64:], high[:, 64:]], axis=1
                    )

            return carry

        lax.fori_loop(0, 4, body, 0)

    for _, into in square_copies:
        into.wait_recv()
    everyone = squares[0]
    for member in range(1, 8):
        everyone = everyone + squares[member]
    inverse_rms = lax.rsqrt(jnp.sum(everyone, axis=1, keepdims=True) / WIDTH + EPSILON)
    xx[k, x, y] = (subject * inverse_rms * gain_ref[...].reshape(1, 640)).astype(BF16)

    gather = PlaneGather(xx.at[k], 64, x_send, x_recv, pos)
    gather.begin()

    def to_sibling(half, number, first, second):
        ref = gather.piece(half, first, second)
        return remote(ref, ref, sib_send.at[half, number], sib_recv.at[half, number], sibling)

    def from_sibling(half, number, first, second):
        bx, by = gather.block(half, first, second)
        ref = xx.at[1 - k, bx, by, pl.ds(half * 32, 32)]
        return remote(ref, ref, sib_send.at[half, number], sib_recv.at[half, number], sibling)

    places = ((0, 0),) + PlaneGather.PLACES
    for half in (0, 1):
        to_sibling(half, 0, 0, 0).start()

    for ref, index in weights:
        fetch(ref, index).wait()
    select(own_w, k)

    def arrivals(numbers):
        for number in numbers:
            for half in (0, 1):
                gather.event(number, half)
                to_sibling(half, number + 1, *places[number + 1]).start()

    def siblings(numbers):
        for number in numbers:
            for half in (0, 1):
                from_sibling(half, number, *places[number]).wait_recv()

    def line(core, half, second):
        if half == 0:
            value = xx[core, lax.rem(x + second % 4, 4), :, 0:32, :]
        else:
            value = xx[core, :, lax.rem(y + second % 4, 4), 32:64, :]
        return value.reshape(128, 640)

    def product(chunk, dest):
        second = (0, -1, 1, 2)[chunk]
        value = None
        for core in (0, 1):
            left = jnp.concatenate([line(core, 0, second), line(core, 1, second)], axis=0)
            term = jnp.dot(left, sel_w[dest, core * 640 : core * 640 + 640], preferred_element_type=F32)
            value = term if value is None else value + term
        return value

    def dest(step):
        return lax.rem(z + step % 4, 4)

    def hop(chunk, kind):
        target = moved(pos, 2, 1 if kind % 2 == 0 else -1)
        return remote(
            hop_out.at[chunk, kind], hop_in.at[chunk, kind], hop_send.at[chunk, kind], hop_recv.at[chunk, kind], target
        )

    def send(chunk, kind, value):
        hop_out[chunk, kind] = value.astype(BF16)
        hop(chunk, kind).start()

    def multiply(chunk):
        value = product(chunk, dest(2))
        send(chunk, 0, value[:128])
        send(chunk, 1, value[128:])
        value = product(chunk, dest(1))
        send(chunk, 2, value[128:])
        part[chunk, 0] = value[:128]
        value = product(chunk, dest(-1))
        send(chunk, 3, value[:128])
        part[chunk, 1] = value[128:]
        value = product(chunk, dest(0))
        part[chunk, 2] = value[:128]
        part[chunk, 3] = value[128:]

    def join(chunk):
        hop(chunk, 0).wait_recv()
        send(chunk, 4, part[chunk, 0] + hop_in[chunk, 0].astype(F32))
        hop(chunk, 1).wait_recv()
        send(chunk, 5, part[chunk, 1] + hop_in[chunk, 1].astype(F32))

    def finish(chunk):
        second = (0, -1, 1, 2)[chunk]
        for half in (0, 1):
            kinds = (4, 3) if half == 0 else (2, 5)
            for kind in kinds:
                hop(chunk, kind).wait_recv()
            value = part[chunk, 2 + half] + (hop_in[chunk, kinds[0]].astype(F32) + hop_in[chunk, kinds[1]].astype(F32))
            gate, up = value[:, :128], value[:, 128:]
            raw = gate / (1.0 + jnp.exp(-gate)) * up
            place = lax.rem((x if half == 0 else y) + second % 4, 4)
            total[:, pl.ds(pl.multiple_of(half * 512 + place * 128, 128), 128)] = raw.T

    covs = PlaneGather(cc, 64, cc_send, cc_recv, pos, only=lambda bx, by: bx < 2)

    def cov_events(numbers):
        for number in numbers:
            for half in (0, 1):
                covs.event(number, half)

    tile_events((0, 1, 2, 3))
    arrivals((0, 1, 4))
    tile_events((4, 5, 6))
    for ref, index in weights:
        swap(ref, index).wait_recv()
    select(other_w, 1 - k)
    arrivals((2, 3))
    tile_events(range(7, 15))
    siblings((0, 1, 2, 5))
    multiply(0)
    arrivals((5, 8, 10))
    siblings((3, 6, 9, 11))
    multiply(1)
    join(0)
    jj[col] = tiles[...].reshape(512, 128).astype(F32).T[0:64].astype(BF16)
    corner = ColumnGather(jj, jj_send, jj_recv, pos)
    corner.begin()
    arrivals((6, 7, 9))
    siblings((4, 7, 8, 10))
    multiply(2)
    join(1)
    corner.middle()
    arrivals((11, 12, 13, 14))

    fetch_rows.wait()

    @pl.when(x < 2)
    def _():
        cc[x, y] = cov_rows[...].astype(BF16)

    covs.begin()
    siblings((12, 13, 14, 15))
    multiply(3)
    join(2)
    fetch_cols.wait()
    cr[col] = cov_cols[...].T[0:64].astype(BF16)
    cov_events((0, 1))
    finish(0)
    join(3)
    cov_events((2, 3, 4))
    finish(1)
    finish(2)
    corner.end()
    finish(3)
    raw = total[...]
    mass = jnp.sum(raw * raw, axis=0, keepdims=True)
    own_keys = raw.astype(BF16)
    row = x * 4 + y

    @pl.when(row == 0)
    def _():
        first[0, 0] = own_keys[0:64]

    first_tile = PlaneGather(first, 64, f_send, f_recv, pos, only=lambda bx, by: (bx == 0) & (by == 0))
    first_tile.begin()
    sum_y[y] = jnp.broadcast_to(mass, (8, PROMPTS))
    y_copies = to_axis(sum_y, sy_send, sy_recv, pos, 1)
    for out, _ in y_copies:
        out.start()
    kc[x, y] = own_keys
    keys = PlaneGather(kc, 128, kc_send, kc_recv, pos)
    keys.begin()
    cov_events((5, 6, 9))
    for _, into in y_copies:
        into.wait_recv()
    sum_x[x] = sum_y[0] + sum_y[1] + sum_y[2] + sum_y[3]
    x_copies = to_axis(sum_x, sx_send, sx_recv, pos, 0)
    for out, _ in x_copies:
        out.start()

    def first_events(numbers):
        for number in numbers:
            first_tile.event(number, 0)
            first_tile.event(number, 1)

    first_events((0, 1, 2, 3))
    for _, into in x_copies:
        into.wait_recv()
    sum_c[col] = sum_x[0] + sum_x[1] + sum_x[2] + sum_x[3]
    c_copies = to_all_columns(sum_c, sc_send, sc_recv, pos)
    for out, _ in c_copies:
        out.start()
    first_events(range(4, 15))
    k5[col] = first[0, 0]
    first_keys = ColumnGather(k5, k5_send, k5_recv, pos)
    first_keys.begin()

    source = lax.rem(row, 8)
    source_z = source // 2
    upper = row // 8
    away = lax.rem(z + 4 - source_z, 4)
    same = k == lax.rem(source, 2)

    def wave(number, kind, own=False):
        one, two = keys.block(0, *places[number]), keys.block(1, *places[number])
        bx = jnp.where(upper == 0, one[0], two[0])
        by = jnp.where(upper == 0, one[1], two[1])
        part = kind % 2
        dst = kr.at[bx, by, pl.ds(part * 32, 32)]
        src = kc.at[bx, by, pl.ds(pl.multiple_of(upper * 64 + part * 32, 32), 32)] if own else dst
        target = sibling if kind >= 2 else moved(pos, 2, 1 if kind == 0 else -1)
        return remote(src, dst, row_send.at[number, kind], row_recv.at[number, kind], target)

    def own_copy(number):
        one, two = keys.block(0, *places[number]), keys.block(1, *places[number])
        bx = jnp.where(upper == 0, one[0], two[0])
        by = jnp.where(upper == 0, one[1], two[1])
        return pltpu.make_async_copy(
            kc.at[bx, by, pl.ds(pl.multiple_of(upper * 64, 64), 64)], kr.at[bx, by], out_sem.at[number]
        )

    def relay(number):
        if number < 16:

            @pl.when(same & (away == 0))
            def _():
                for kind in (0, 1, 2, 3):
                    wave(number, kind, own=True).start()
                own_copy(number).start()

        for distance in (1, 2, 3):
            for kind, hops in ((0, distance), (1, 4 - distance)):
                block = number - LAG * hops
                if 0 <= block < 16:

                    @pl.when(same & (away == distance))
                    def _():
                        wave(block, kind).wait_recv()
                        if hops < 3:
                            wave(block, kind).start()
                        wave(block, kind + 2).start()

    def key_event(number):
        if number < 15:
            keys.event(number, 0)
            keys.event(number, 1)
        relay(number + 1)

    panel_rows = ColumnGather(cr, cr_send, cr_recv, pos)
    cov_events((7, 8))
    relay(0)
    key_event(0)
    for _, into in c_copies:
        into.wait_recv()
    mass = sum_c[0]
    for member in range(1, 8):
        mass = mass + sum_c[member]
    scale = lax.rsqrt(mass / HIDDEN + EPSILON) * (1.0 / 32.0)
    scale_ref[...] = scale * scale
    first_keys.middle()
    cov_events((10, 11, 12))
    key_event(1)
    first_keys.end()
    panel_rows.begin()
    key_event(2)
    cov_events((13, 14))

    def save(number, source, target):
        return pltpu.make_async_copy(source, target, out_sem.at[16 + number])

    corner_raw = k5[...].reshape(512, PROMPTS).astype(F32)
    corner_keys = (corner_raw * scale[0:1]).astype(BF16)
    outer = lax.dot_general(corner_keys, corner_keys, (((1,), (1,)), ((), ())), preferred_element_type=F32)
    aug[:, 0:512] = jj[...].reshape(512, 512).astype(F32) + outer
    aug[:, 512:1024] = (
        lax.broadcasted_iota(jnp.int32, (512, 512), 0) == lax.broadcasted_iota(jnp.int32, (512, 512), 1)
    ).astype(F32)
    k5_scaled[...] = (corner_raw * (scale * scale)[0:1]).astype(BF16).reshape(8, 64, PROMPTS)
    save(0, k5_scaled, k5_out).start()
    save(1, cc, cc_out).start()
    beside = {
        3: 0, 4: 1, 5: 3, 6: 5, 7: 7, 8: 9, 9: 11, 10: 13, 11: 15, 12: 17, 13: 19, 14: 21, 15: 23, 16: 24, 17: 25, 18: 26, 19: 28, 20: 30,
    }
    extras = [{} for _ in range(4)]
    for number, step in beside.items():
        extras[step // 8][step % 8] = functools.partial(key_event, number)
    extras[0][2] = panel_rows.middle
    extras[0][6] = panel_rows.end
    extras[2][6] = lambda: save(2, kc, kc_out).start()
    extras[2][4] = lambda: save(3, cr, cr_out).start()
    factor(aug, work, extras)
    inv_ref[...] = aug[:, 512:1024]

    for number in range(16):

        @pl.when(k != lax.rem(source, 2))
        def _():
            wave(number, 2).wait_recv()
            wave(number, 3).wait_recv()

        @pl.when(same & (away == 0))
        def _():
            for kind in range(4):
                wave(number, kind, own=True).wait_send()
            own_copy(number).wait()

        for distance in (1, 2, 3):

            @pl.when(same & (away == distance))
            def _():
                for kind, hops in ((0, distance), (1, 4 - distance)):
                    if hops < 3:
                        wave(number, kind).wait_send()
                    wave(number, kind + 2).wait_send()

    first_tile.finish()
    keys.finish()
    panel_rows.finish()
    first_keys.finish()
    corner.finish()
    corner_tiles.finish()
    save(4, kr, kr_out).start()
    for ref, index in weights:
        swap(ref, index).wait_send()
    for copies in (square_copies, y_copies, x_copies, c_copies):
        for out, _ in copies:
            out.wait_send()
    gather.finish()
    covs.finish()
    for half in (0, 1):
        for number in range(16):
            to_sibling(half, number, *places[number]).wait_send()
    for chunk in range(4):
        for kind in range(6):
            hop(chunk, kind).wait_send()
    save(0, k5_scaled, k5_out).wait()
    save(1, cc, cc_out).wait()
    save(2, kc, kc_out).wait()
    save(3, cr, cr_out).wait()
    save(4, kr, kr_out).wait()


def panel(residual, positions, gain, w_gate, w_up, cov):
    dma = pltpu.SemaphoreType.DMA
    vmem = pl.BlockSpec(memory_space=pltpu.VMEM)
    anywhere = pl.BlockSpec(memory_space=pl.ANY)
    spread = (
        ((4, 4, 128, PROMPTS), BF16),
        ((4, 4, 64, PROMPTS), BF16),
        ((8, 64, PROMPTS), BF16),
        ((8, 64, 1024), BF16),
        ((2, 4, 64, 2048), BF16),
    )
    return pl.pallas_call(
        panel_kernel,
        name="keys_and_panel",
        out_shape=tuple(jax.ShapeDtypeStruct(*one) for one in spread)
        + (jax.ShapeDtypeStruct((512, 512), F32), jax.ShapeDtypeStruct((8, PROMPTS), F32)),
        in_specs=[vmem] * 3 + [anywhere] * 3,
        out_specs=(anywhere,) * 5 + (vmem,) * 2,
        scratch_shapes=[
            pltpu.VMEM(*spread[0]), pltpu.VMEM(*spread[1]), pltpu.VMEM(*spread[2]), pltpu.VMEM(*spread[2]),
            pltpu.VMEM(*spread[3]), pltpu.VMEM(*spread[4]),
            pltpu.VMEM((1, 1, 64, PROMPTS), BF16),
            pltpu.VMEM((8, 64, 512), BF16),
            pltpu.VMEM((512, 1024), F32),
            pltpu.VMEM((128, 256), F32),
            pltpu.VMEM((2, 4, 4, 64, 640), BF16),
            pltpu.VMEM((2, 640, 1024), BF16),
            pltpu.VMEM((2, 640, 1024), BF16),
            pltpu.VMEM((4, 1280, 256), BF16),
            pltpu.VMEM((8, 64, 128), F32),
            pltpu.VMEM((4, 4, 128, 256), F32),
            pltpu.VMEM((4, 6, 128, 256), BF16),
            pltpu.VMEM((4, 6, 128, 256), BF16),
            pltpu.VMEM((128, PROMPTS), F32),
            pltpu.VMEM((4, 8, PROMPTS), F32),
            pltpu.VMEM((4, 8, PROMPTS), F32),
            pltpu.VMEM((8, 8, PROMPTS), F32),
            pltpu.VMEM((64, 2048), F32),
            pltpu.VMEM((1024, 128), F32),
            pltpu.VMEM((64, 128), F32),
            pltpu.VMEM((2, 4, 64, 128), BF16),
            dma((5,)), dma((2,)), dma((2,)), dma((7,)), dma((7,)), dma((2, 16)), dma((2, 16)), dma((2, 16)), dma((2, 16)),
            dma((4, 6)), dma((4, 6)), dma((3,)), dma((3,)), dma((3,)), dma((3,)), dma((7,)), dma((7,)), dma((2, 16)), dma((2, 16)),
            dma((2, 16)), dma((2, 16)), dma((8,)), dma((8,)), dma((8,)), dma((8,)), dma((8,)), dma((8,)), dma((2, 16)), dma((2, 16)),
            dma((16, 4)), dma((16, 4)), dma((21,)), dma((2, 16)), dma((2, 16)),
        ],
        compiler_params=pltpu.CompilerParams(collective_id=0, has_side_effects=True, vmem_limit_bytes=VMEM_LIMIT),
    )(residual, positions, gain, w_gate, w_up, cov)


def update_kernel(
    cov_ref, kc_ref, cc_ref, kr_ref, k5_ref, cr_ref, inv_ref, scale_ref, out_ref,
    covb, kcb, ccb, outb, panel, weights, rows, cov_sem, kc_sem, cc_sem, out_sem, zeros, zero_sem,
):
    x, y, z, k = here()
    row = x * 4 + y
    col = z * 2 + k
    nt = (((1,), (1,)), ((), ()))
    nn = (((1,), (0,)), ((), ()))
    tn = (((0,), (0,)), ((), ()))
    dot = functools.partial(lax.dot_general, preferred_element_type=F32)

    def load_cov(step):
        area = (pl.ds(step * 128, 1024 - step * 128), pl.ds(step * 256, 256))
        return pltpu.make_async_copy(cov_ref.at[area], covb.at[area], cov_sem.at[step])

    def load_kc(step):
        area = pl.ds(step * 2, 2)
        return pltpu.make_async_copy(kc_ref.at[area], kcb.at[area], kc_sem.at[step])

    def load_cc(step):
        area = (slice(None), slice(None), pl.ds(step * 256, 256))
        return pltpu.make_async_copy(cc_ref.at[area], ccb.at[area], cc_sem.at[step])

    def store(step):
        top = step * 128
        source = outb.at[step % 2, pl.ds(top, 1024 - top)]
        return pltpu.make_async_copy(source, out_ref.at[pl.ds(top, 1024 - top), pl.ds(step * 256, 256)], out_sem.at[step % 2])

    def clear(step):
        top = step * 128
        return pltpu.make_async_copy(zeros.at[pl.ds(0, top)], out_ref.at[pl.ds(0, top), pl.ds(step * 256, 256)], zero_sem.at[step])

    for step in range(8):
        load_kc(step).start()
        load_cc(step).start()
        load_cov(step).start()
    zeros[...] = jnp.zeros_like(zeros)
    for step in range(1, 8):
        clear(step).start()
    inverse = inv_ref[...]
    inverse_high = inverse.astype(BF16)
    first = k5_ref[...].reshape(512, PROMPTS)
    raw_rows = kr_ref[...].reshape(1024, PROMPTS)
    matrix_rows = cr_ref[...].reshape(512, 1024).astype(F32) + dot(first, raw_rows, nt)
    high, low = split(matrix_rows)
    panel_rows = dot(inverse_high, high, nn).astype(BF16)
    weights[...] = dot(panel_rows, inverse_high, tn).astype(BF16)
    own_high, own_low = split(inv_ref[pl.ds(pl.multiple_of(col * 64, 64), 64), :])
    panel[...] = dot(own_high, high, nn) + (dot(own_low, high, nn) + dot(own_high, low, nn))
    rows[...] = (raw_rows.astype(F32) * scale_ref[0:1] - dot(weights[...], first, nn)).astype(BF16)
    for step in range(8):
        top = step * 128
        height = 1024 - top
        load_kc(step).wait()
        load_cc(step).wait()
        load_cov(step).wait()
        if step >= 2:
            store(step - 2).wait()
        cols = kcb[2 * step : 2 * step + 2].reshape(256, PROMPTS)
        panel_cols = ccb[:, :, step * 256 : (step + 1) * 256].reshape(512, 256)
        value = covb[top:1024, step * 256 : (step + 1) * 256] + (dot(rows[top:], cols, nt) - dot(weights[top:], panel_cols, nn))
        if step == 0:
            value = jnp.concatenate([panel[...].T, value[:, 64:]], axis=1)
        edge = min(256, height)
        i = lax.broadcasted_iota(jnp.int32, (edge, 256), 0) + top
        j = lax.broadcasted_iota(jnp.int32, (edge, 256), 1) + step * 256
        row_global = (i // 64 * 16 + row) * 64 + i % 64
        col_global = (j // 64 * 8 + col) * 64 + j % 64
        outb[step % 2, top : top + edge] = jnp.where(row_global >= col_global, value[:edge], 0.0)
        if edge < height:
            outb[step % 2, top + edge : 1024] = value[edge:]
        store(step).start()
    store(6).wait()
    store(7).wait()
    for step in range(1, 8):
        clear(step).wait()


def update(cov, kc, kr, k5, cr, cc, inverse, scale):
    dma = pltpu.SemaphoreType.DMA
    vmem = pl.BlockSpec(memory_space=pltpu.VMEM)
    anywhere = pl.BlockSpec(memory_space=pl.ANY)
    return pl.pallas_call(
        update_kernel,
        name="update_lower",
        out_shape=jax.ShapeDtypeStruct((1024, 2048), F32),
        in_specs=[anywhere] * 3 + [vmem] * 5,
        out_specs=anywhere,
        scratch_shapes=[
            pltpu.VMEM((1024, 2048), F32), pltpu.VMEM((16, 128, PROMPTS), BF16), pltpu.VMEM((8, 64, 2048), BF16),
            pltpu.VMEM((2, 1024, 256), F32), pltpu.VMEM((64, 1024), F32), pltpu.VMEM((1024, 512), BF16), pltpu.VMEM((1024, PROMPTS), BF16),
            dma((8,)), dma((8,)), dma((8,)), dma((2,)), pltpu.VMEM((896, 256), F32), dma((8,)),
        ],
        compiler_params=pltpu.CompilerParams(vmem_limit_bytes=VMEM_LIMIT),
    )(cov, kc, cc, kr, k5, cr, inverse, scale)


def on_device(residual, positions, norm_gain, w_gate, w_up, covariance):
    kc, kr, k5, cr, cc, inverse, scale = panel(residual, positions, norm_gain, w_gate, w_up, covariance)
    kc = kc.reshape(16, 128, PROMPTS)
    kr = kr.reshape(16, 64, PROMPTS)
    cc = cc.reshape(8, 64, 2048)
    return update(covariance, kc, kr, k5, cr, cc, inverse, scale)


def solution(mesh):
    torus = Mesh(mesh.devices.reshape(4, 4, 4, 2), ("x", "y", "z", "k"))
    row, col = ("x", "y"), ("z", "k")
    placed = (P(row, None, col), P(row), P(col), P(col, row), P(col, row), P(row, col))
    return jax.shard_map(on_device, mesh=torus, in_specs=placed, out_specs=P(row, col), check_vma=False)
```

```python
import functools

import jax
import jax.numpy as jnp
from jax import lax
from jax.experimental import pallas as pl
from jax.experimental.pallas import tpu as pltpu
from jax.sharding import Mesh
from jax.sharding import PartitionSpec as P

MESH = pl.DeviceIdType.MESH
BF16 = jnp.bfloat16
F32 = jnp.float32
EPSILON = 1e-06
HIDDEN = 16384
WIDTH = 5120
PROMPTS = 1024
VMEM_LIMIT = 60 * 1024 * 1024
BASE = 16
LAG = 2


def here():
    return tuple(lax.axis_index(name) for name in ("x", "y", "z", "k"))


def moved(position, axis, step):
    place = list(position)
    size = 2 if axis == 3 else 4
    place[axis] = lax.rem(place[axis] + (step % size), size)
    return tuple(place)


def remote(src, dst, send, recv, target):
    return pltpu.make_async_remote_copy(
        src_ref=src, dst_ref=dst, send_sem=send, recv_sem=recv, device_id=target, device_id_type=MESH
    )


def greet(targets):
    barrier = pltpu.get_barrier_semaphore()
    for target in targets:
        pl.semaphore_signal(barrier, inc=1, device_id=target, device_id_type=MESH)
    pl.semaphore_wait(barrier, len(targets))


def when(condition, action):
    if condition is None:
        action()
    else:
        pl.when(condition)(action)


class PlaneGather:
    SENT = (
        (0, 0, 1, 1, None), (0, 0, 1, -1, None), (-1, 0, 1, 1, 0), (1, 0, 1, -1, 1),
        (0, 0, 0, 1, None), (-1, 0, 0, 1, None), (1, 0, 0, 1, None), (2, 0, 0, 1, None),
        (0, 0, 0, -1, None), (-1, 0, 0, -1, None), (1, 0, 0, -1, None), (2, 0, 0, -1, None),
        (0, -1, 0, 1, None), (-1, -1, 0, 1, None), (1, 1, 0, -1, None), (2, 1, 0, -1, None),
    )
    GOT = (
        (-1, 0, None), (1, 0, None), (2, 0, 0), (2, 0, 1),
        (0, -1, None), (-1, -1, None), (1, -1, None), (2, -1, None),
        (0, 1, None), (-1, 1, None), (1, 1, None), (2, 1, None),
        (0, 2, None), (-1, 2, None), (1, 2, None), (2, 2, None),
    )
    EVENTS = (
        ((0,), (2, 5, 9)), ((1,), (3, 6, 10)), ((4,), (12,)), ((8,), ()), ((2, 3), (7, 11)), ((5,), (13,)), ((10,), (14,)),
        ((9,), ()), ((6,), ()), ((11,), (15,)), ((7,), ()), ((12,), ()), ((13,), ()), ((14,), ()), ((15,), ()),
    )
    PLACES = tuple(((-1, 0), (1, 0), (0, -1), (0, 1), (2, 0), (-1, -1), (1, 1), (-1, 1), (1, -1), (2, 1), (2, -1), (0, 2), (-1, 2), (1, 2), (2, 2)))

    def __init__(self, buf, rows, send, recv, pos, only=None):
        self.buf, self.rows, self.send, self.recv, self.pos, self.only = buf, rows, send, recv, pos, only

    def block(self, half, first, second):
        dx, dy = (second, first) if half == 0 else (first, second)
        return lax.rem(self.pos[0] + dx % 4, 4), lax.rem(self.pos[1] + dy % 4, 4)

    def piece(self, half, first, second, part=None):
        size = self.rows // 2
        start = half * size
        if part is not None:
            size //= 2
            start += part * size
        bx, by = self.block(half, first, second)
        return self.buf.at[bx, by, pl.ds(start, size)]

    def cond(self, half, first, second):
        return None if self.only is None else self.only(*self.block(half, first, second))

    def copy(self, half, kind, first, second, axis, step, part=None):
        axis = axis if half == 0 else 1 - axis
        ref = self.piece(half, first, second, part)
        return remote(ref, ref, self.send.at[half, kind], self.recv.at[half, kind], moved(self.pos, axis, step))

    def go(self, half, kind):
        first, second, axis, step, part = self.SENT[kind]
        when(self.cond(half, first, second), lambda: self.copy(half, kind, first, second, axis, step, part).start())

    def arrive(self, half, kind):
        first, second, part = self.GOT[kind]
        when(self.cond(half, first, second), lambda: self.copy(half, kind, first, second, 0, 1, part).wait_recv())

    def begin(self):
        for kind in (0, 1, 4, 8):
            for half in (0, 1):
                self.go(half, kind)

    def event(self, number, half):
        kinds, on = self.EVENTS[number]
        for kind in kinds:
            self.arrive(half, kind)
        for kind in on:
            self.go(half, kind)

    def finish(self):
        for half in (0, 1):
            for kind in range(16):
                first, second, axis, step, part = self.SENT[kind]
                when(
                    self.cond(half, first, second),
                    lambda: self.copy(half, kind, first, second, axis, step, part).wait_send(),
                )


class ColumnGather:
    def __init__(self, buf, send, recv, pos):
        self.buf, self.send, self.recv, self.pos = buf, send, recv, pos

    def piece(self, dz, dk=0, part=None):
        z, k = self.pos[2], self.pos[3]
        slot = lax.rem(z + dz % 4, 4) * 2 + lax.rem(k + dk, 2)
        if part is None:
            return self.buf.at[slot]
        return self.buf.at[slot, pl.ds(32 * part, 32)]

    SENT = {0: (0, 2, 1, None), 1: (0, 2, -1, None), 2: (-1, 2, 1, 0), 3: (1, 2, -1, 1),
            4: (0, 3, 1, None), 5: (-1, 3, 1, None), 6: (1, 3, 1, None), 7: (2, 3, 1, None)}
    GOT = {0: (-1, 0, None), 1: (1, 0, None), 2: (2, 0, 0), 3: (2, 0, 1),
           4: (0, 1, None), 5: (-1, 1, None), 6: (1, 1, None), 7: (2, 1, None)}

    def go(self, kind):
        dz, axis, step, part = self.SENT[kind]
        ref = self.piece(dz, 0, part)
        remote(ref, ref, self.send.at[kind], self.recv.at[kind], moved(self.pos, axis, step)).start()

    def arrive(self, kind):
        dz, dk, part = self.GOT[kind]
        ref = self.piece(dz, dk, part)
        remote(ref, ref, self.send.at[kind], self.recv.at[kind], moved(self.pos, 2, 1)).wait_recv()

    def begin(self):
        for kind in (0, 1, 4):
            self.go(kind)

    def middle(self):
        self.arrive(0)
        self.go(2)
        self.go(5)
        self.arrive(1)
        self.go(3)
        self.go(6)

    def end(self):
        self.arrive(2)
        self.arrive(3)
        self.go(7)
        for kind in (4, 5, 6, 7):
            self.arrive(kind)

    def finish(self):
        for kind in range(8):
            dz, axis, step, part = self.SENT[kind]
            ref = self.piece(dz, 0, part)
            remote(ref, ref, self.send.at[kind], self.recv.at[kind], moved(self.pos, axis, step)).wait_send()


def column_peers(pos):
    peers = []
    for dz in range(4):
        for dk in range(2):
            if dz or dk:
                peers.append(moved(moved(pos, 2, dz), 3, dk))
    return peers


def to_all_columns(buf, send, recv, pos):
    copies = []
    mine = pos[2] * 2 + pos[3]
    number = 0
    for dz in range(4):
        for dk in range(2):
            if dz == 0 and dk == 0:
                continue
            target = moved(moved(pos, 2, dz), 3, dk)
            out = remote(buf.at[mine], buf.at[mine], send.at[number], recv.at[number], target)
            origin = moved(moved(pos, 2, -dz), 3, -dk)
            slot = origin[2] * 2 + origin[3]
            into = remote(buf.at[slot], buf.at[slot], send.at[number], recv.at[number], target)
            copies.append((out, into))
            number += 1
    return copies


def to_axis(buf, send, recv, pos, axis):
    copies = []
    mine = pos[axis]
    for step in (1, 2, 3):
        target = moved(pos, axis, step)
        out = remote(buf.at[mine], buf.at[mine], send.at[step - 1], recv.at[step - 1], target)
        slot = moved(pos, axis, -step)[axis]
        into = remote(buf.at[slot], buf.at[slot], send.at[step - 1], recv.at[step - 1], target)
        copies.append((out, into))
    return copies


def exchange(copies):
    for out, _ in copies:
        out.start()
    for _, into in copies:
        into.wait_recv()


def split(value):
    high = value.astype(BF16)
    return high, (value - high.astype(F32)).astype(BF16)


def dot3(left, right, dims):
    lh, ll = split(left)
    rh, rl = split(right)
    dot = functools.partial(lax.dot_general, dimension_numbers=(dims, ((), ())), preferred_element_type=F32)
    return dot(lh, rh) + (dot(lh, rl) + dot(ll, rh))


def small_factor(work, extra):
    lane = lax.broadcasted_iota(jnp.int32, (1, 128), 1)

    def body(step, carry):
        start = pl.multiple_of(step * BASE, BASE)
        rows = work[pl.ds(start, BASE), :]
        turned = pltpu.roll(rows[:, :128], lax.rem(128 - start, 128), 1)
        entry = [[jnp.broadcast_to(turned[i : i + 1, j : j + 1], (1, 128)) for j in range(i + 1)] for i in range(BASE)]
        solved = []
        for j in range(BASE):
            inverse = lax.rsqrt(entry[j][j])
            row = rows[j : j + 1, :]
            for m in range(j):
                row = row - jnp.concatenate([entry[j][m]] * 2, axis=1) * solved[m]
            solved.append(row * jnp.concatenate([inverse] * 2, axis=1))
            for i in range(j + 1, BASE):
                entry[i][j] = entry[i][j] * inverse
            for i in range(j + 1, BASE):
                for m in range(j + 1, i + 1):
                    entry[i][m] = entry[i][m] - entry[i][j] * entry[m][j]
        block = jnp.concatenate(solved, axis=0)
        work[pl.ds(start, BASE), :] = block
        later = jnp.where(lane >= start + BASE, block[:, :128], 0.0)
        lh, ll = split(later)
        rh, rl = split(block)
        left = jnp.concatenate([lh, lh, ll], axis=0)
        right = jnp.concatenate([rh, rl, rh], axis=0)
        work[...] = work[...] - lax.dot_general(left, right, (((0,), (0,)), ((), ())), preferred_element_type=F32)
        for number, action in extra.items():
            pl.when(step == number)(action)
        return carry

    lax.fori_loop(0, 128 // BASE, body, 0)


def factor(aug, work, extras):
    eye = (lax.broadcasted_iota(jnp.int32, (128, 128), 0) == lax.broadcasted_iota(jnp.int32, (128, 128), 1)).astype(F32)
    for number in range(4):
        lo, hi = number * 128, (number + 1) * 128
        work[:, 0:128] = aug[lo:hi, lo:hi]
        work[:, 128:256] = eye
        small_factor(work, extras[number])
        inverse = work[:, 128:256]
        if hi < 512:
            right = dot3(inverse, aug[lo:hi, hi : 512 + lo], ((1,), (0,)))
            full = jnp.concatenate([right, inverse], axis=1)
            aug[lo:hi, hi : 512 + hi] = full
            ahead = right[:, 0 : 512 - hi]
            aug[hi:512, hi : 512 + hi] = aug[hi:512, hi : 512 + hi] - dot3(ahead, full, ((0,), (0,)))
        else:
            aug[lo:hi, 512 : 512 + lo] = dot3(inverse, aug[lo:hi, 512 : 512 + lo], ((1,), (0,)))
            aug[lo:hi, 512 + lo : 512 + hi] = inverse


def panel_kernel(
    residual_ref, positions_ref, gain_ref, gate_ref, up_ref, cov_ref, kc_out, kr_out, k5_out, cr_out, cc_out, inv_ref, scale_ref,
    kc, kr, k5, k5_scaled, cr, cc, first, jj, aug, work,
    xx, own_w, other_w, sel_w, squares, part, hop_out, hop_in, total, sum_y, sum_x, sum_c, cov_rows, cov_cols, cov_corner, tiles,
    local_sem, w_send, w_recv, sq_send, sq_recv, x_send, x_recv, sib_send, sib_recv,
    hop_send, hop_recv, sy_send, sy_recv, sx_send, sx_recv, sc_send, sc_recv, cc_send, cc_recv,
    kc_send, kc_recv, k5_send, k5_recv, cr_send, cr_recv, jj_send, jj_recv, f_send, f_recv, row_send, row_recv, out_sem, tile_send, tile_recv,
):
    pos = here()
    x, y, z, k = pos
    sibling = moved(pos, 3, 1)
    col = z * 2 + k
    plane = [moved(pos, axis, step) for axis in (0, 1) for step in (1, 2, 3)]
    barrier = pltpu.get_barrier_semaphore()
    peers = plane + column_peers(pos)
    for peer in peers:
        pl.semaphore_signal(barrier, inc=1, device_id=peer, device_id_type=MESH)

    weights = ((gate_ref, 0), (up_ref, 1))

    def swap(ref, index):
        return remote(ref, other_w.at[index], w_send.at[index], w_recv.at[index], sibling)

    def fetch(ref, index):
        return pltpu.make_async_copy(ref, own_w.at[index], local_sem.at[index])

    fetch_rows = pltpu.make_async_copy(cov_ref.at[pl.ds(0, 64)], cov_rows, local_sem.at[2])
    fetch_cols = pltpu.make_async_copy(cov_ref.at[:, pl.ds(0, 128)], cov_cols, local_sem.at[3])

    fetch_corner = pltpu.make_async_copy(cov_ref.at[pl.ds(0, 64), pl.ds(0, 128)], cov_corner, local_sem.at[4])
    fetch_corner.start()
    line_of = lax.broadcasted_iota(jnp.int32, (64, 64), 0)
    prompt_of = lax.broadcasted_iota(jnp.int32, (64, 64), 1)
    place = positions_ref[...].reshape(1, 64).astype(F32)
    place = jnp.sum(jnp.where(line_of == prompt_of, place, 0.0), axis=1, keepdims=True)
    token = lax.broadcasted_iota(jnp.int32, (64, 1024), 1) - 16 * lax.broadcasted_iota(jnp.int32, (64, 1024), 0)
    pick = (token.astype(F32) == place).astype(BF16)
    subject = jnp.dot(pick, residual_ref[...].reshape(1024, 640), preferred_element_type=F32)
    squared = subject * subject
    folded = squared[:, 0:128]
    for group in range(1, 5):
        folded = folded + squared[:, group * 128 : (group + 1) * 128]
    squares[col] = folded
    pl.semaphore_wait(barrier, len(peers))
    square_copies = to_all_columns(squares, sq_send, sq_recv, pos)
    for out, _ in square_copies:
        out.start()
    for ref, index in weights:
        fetch(ref, index).start()
        swap(ref, index).start()
    fetch_corner.wait()

    @pl.when(x < 2)
    def _():
        tiles[x, y] = cov_corner[...].astype(BF16)

    corner_tiles = PlaneGather(tiles, 64, tile_send, tile_recv, pos, only=lambda bx, by: bx < 2)
    corner_tiles.begin()

    def tile_events(numbers):
        for number in numbers:
            for half in (0, 1):
                corner_tiles.event(number, half)

    fetch_rows.start()
    fetch_cols.start()

    def select(source, core):
        def body(step, carry):
            first = pl.ds(pl.multiple_of(step * 128, 128), 128)
            second = pl.ds(pl.multiple_of(512 + step * 128, 128), 128)
            rows = pl.ds(pl.multiple_of(core * 640, 128), 640)
            for index, lanes in enumerate((first, second)):
                gate, up = source[0, :, lanes], source[1, :, lanes]

                @pl.when(k == 0)
                def _():
                    sel_w[step, rows, pl.ds(index * 128, 128)] = jnp.concatenate([gate[:, :64], up[:, :64]], axis=1)

                @pl.when(k == 1)
                def _():
                    sel_w[step, rows, pl.ds(index * 128, 128)] = jnp.concatenate([gate[:, 64:], up[:, 64:]], axis=1)

            return carry

        lax.fori_loop(0, 4, body, 0)

    for _, into in square_copies:
        into.wait_recv()
    everyone = squares[0]
    for member in range(1, 8):
        everyone = everyone + squares[member]
    inverse_rms = lax.rsqrt(jnp.sum(everyone, axis=1, keepdims=True) / WIDTH + EPSILON)
    xx[k, x, y] = (subject * inverse_rms * gain_ref[...].reshape(1, 640)).astype(BF16)

    gather = PlaneGather(xx.at[k], 64, x_send, x_recv, pos)
    gather.begin()

    def to_sibling(half, number, first, second):
        ref = gather.piece(half, first, second)
        return remote(ref, ref, sib_send.at[half, number], sib_recv.at[half, number], sibling)

    def from_sibling(half, number, first, second):
        bx, by = gather.block(half, first, second)
        ref = xx.at[1 - k, bx, by, pl.ds(half * 32, 32)]
        return remote(ref, ref, sib_send.at[half, number], sib_recv.at[half, number], sibling)

    places = ((0, 0),) + PlaneGather.PLACES
    for half in (0, 1):
        to_sibling(half, 0, 0, 0).start()

    for ref, index in weights:
        fetch(ref, index).wait()
    select(own_w, k)

    def arrivals(numbers):
        for number in numbers:
            for half in (0, 1):
                gather.event(number, half)
                to_sibling(half, number + 1, *places[number + 1]).start()

    def siblings(numbers):
        for number in numbers:
            for half in (0, 1):
                from_sibling(half, number, *places[number]).wait_recv()

    def line(core, half, second):
        if half == 0:
            value = xx[core, lax.rem(x + second % 4, 4), :, 0:32, :]
        else:
            value = xx[core, :, lax.rem(y + second % 4, 4), 32:64, :]
        return value.reshape(128, 640)

    def product(chunk, dest):
        second = (0, -1, 1, 2)[chunk]
        value = None
        for core in (0, 1):
            left = jnp.concatenate([line(core, 0, second), line(core, 1, second)], axis=0)
            term = jnp.dot(left, sel_w[dest, core * 640 : core * 640 + 640], preferred_element_type=F32)
            value = term if value is None else value + term
        return value

    def dest(step):
        return lax.rem(z + step % 4, 4)

    def hop(chunk, kind, tile):
        target = moved(pos, 2, 1 if kind % 2 == 0 else -1)
        return remote(
            hop_out.at[chunk, kind, tile], hop_in.at[chunk, kind, tile],
            hop_send.at[chunk, kind + 6 * tile], hop_recv.at[chunk, kind + 6 * tile], target,
        )

    def lanes(tile):
        return slice(128 * tile, 128 * tile + 128)

    def multiply(chunk, hold):
        def send(kind, value):
            for tile in (0, 1):
                hop_out[chunk, kind, tile] = value[:, lanes(tile)].astype(BF16)
                if tile == 0 or not hold:
                    hop(chunk, kind, tile).start()

        value = product(chunk, dest(2))
        send(0, value[:128])
        send(1, value[128:])
        value = product(chunk, dest(1))
        send(2, value[128:])
        part[chunk, 0] = value[:128]
        value = product(chunk, dest(-1))
        send(3, value[:128])
        part[chunk, 1] = value[128:]
        value = product(chunk, dest(0))
        part[chunk, 2] = value[:128]
        part[chunk, 3] = value[128:]

    def release(chunk):
        for kind in range(4):
            hop(chunk, kind, 1).start()

    def join(chunk, tile):
        for kind in (0, 1):
            hop(chunk, kind, tile).wait_recv()
            value = part[chunk, kind, :, lanes(tile)] + hop_in[chunk, kind, tile].astype(F32)
            hop_out[chunk, 4 + kind, tile] = value.astype(BF16)
            hop(chunk, 4 + kind, tile).start()

    def finish(chunk, tile):
        second = (0, -1, 1, 2)[chunk]
        for half in (0, 1):
            kinds = (4, 3) if half == 0 else (2, 5)
            for kind in kinds:
                hop(chunk, kind, tile).wait_recv()
            value = part[chunk, 2 + half, :, lanes(tile)] + (
                hop_in[chunk, kinds[0], tile].astype(F32) + hop_in[chunk, kinds[1], tile].astype(F32)
            )
            turned = value.T
            gate, up = turned[:64], turned[64:]
            raw = gate / (1.0 + jnp.exp(-gate)) * up
            place = lax.rem((x if half == 0 else y) + second % 4, 4)
            total[pl.ds(64 * tile, 64), pl.ds(pl.multiple_of(half * 512 + place * 128, 128), 128)] = raw

    covs = PlaneGather(cc, 64, cc_send, cc_recv, pos, only=lambda bx, by: bx < 2)

    def cov_events(numbers):
        for number in numbers:
            for half in (0, 1):
                covs.event(number, half)

    arrivals((0, 1, 4))
    for ref, index in weights:
        swap(ref, index).wait_recv()
    select(other_w, 1 - k)
    arrivals((2, 3))
    siblings((0, 1, 2, 5))
    multiply(0, False)
    arrivals((5, 8, 10))
    tile_events((0, 1, 2, 3))
    siblings((3, 6, 9, 11))
    multiply(1, False)
    join(0, 0)
    arrivals((6, 7, 9))
    tile_events((4, 5, 6, 7, 8))
    siblings((4, 7, 8, 10))
    join(0, 1)
    multiply(2, True)
    join(1, 0)
    arrivals((11, 12, 13, 14))
    fetch_rows.wait()

    @pl.when(x < 2)
    def _():
        cc[x, y] = cov_rows[...].astype(BF16)

    siblings((12, 13, 14, 15))
    multiply(3, True)
    release(2)
    release(3)
    covs.begin()
    join(2, 0)
    join(3, 0)
    join(1, 1)
    tile_events(range(9, 15))
    for chunk in range(4):
        finish(chunk, 0)
    row = x * 4 + y

    @pl.when(row == 0)
    def _():
        first[0, 0] = total[0:64].astype(BF16)

    first_tile = PlaneGather(first, 64, f_send, f_recv, pos, only=lambda bx, by: (bx == 0) & (by == 0))
    first_tile.begin()

    def first_events(numbers):
        for number in numbers:
            first_tile.event(number, 0)
            first_tile.event(number, 1)

    join(2, 1)
    join(3, 1)
    jj[col] = tiles[...].reshape(512, 128).astype(F32).T[0:64].astype(BF16)
    corner = ColumnGather(jj, jj_send, jj_recv, pos)
    corner.begin()
    fetch_cols.wait()
    cr[col] = cov_cols[...].T[0:64].astype(BF16)
    cov_events((0, 1))
    first_events((0, 1, 2, 3))
    finish(0, 1)
    cov_events((2, 3, 4))
    first_events((4, 5, 6, 7, 8))
    finish(1, 1)
    finish(2, 1)
    corner.middle()
    finish(3, 1)
    raw = total[...]
    mass = jnp.sum(raw * raw, axis=0, keepdims=True)
    sum_y[y] = jnp.broadcast_to(mass, (8, PROMPTS))
    y_copies = to_axis(sum_y, sy_send, sy_recv, pos, 1)
    for out, _ in y_copies:
        out.start()
    kc[x, y] = raw.astype(BF16)
    keys = PlaneGather(kc, 128, kc_send, kc_recv, pos)
    keys.begin()
    first_events(range(9, 15))
    k5[col] = first[0, 0]
    first_keys = ColumnGather(k5, k5_send, k5_recv, pos)
    first_keys.begin()
    cov_events((5, 6, 9))
    for _, into in y_copies:
        into.wait_recv()
    sum_x[x] = sum_y[0] + sum_y[1] + sum_y[2] + sum_y[3]
    x_copies = to_axis(sum_x, sx_send, sx_recv, pos, 0)
    for out, _ in x_copies:
        out.start()
    corner.end()
    first_keys.middle()
    for _, into in x_copies:
        into.wait_recv()
    sum_c[col] = sum_x[0] + sum_x[1] + sum_x[2] + sum_x[3]
    c_copies = to_all_columns(sum_c, sc_send, sc_recv, pos)
    for out, _ in c_copies:
        out.start()

    source = lax.rem(row, 8)
    source_z = source // 2
    upper = row // 8
    away = lax.rem(z + 4 - source_z, 4)
    same = k == lax.rem(source, 2)

    def wave(number, kind, own=False):
        one, two = keys.block(0, *places[number]), keys.block(1, *places[number])
        bx = jnp.where(upper == 0, one[0], two[0])
        by = jnp.where(upper == 0, one[1], two[1])
        part = kind % 2
        dst = kr.at[bx, by, pl.ds(part * 32, 32)]
        src = kc.at[bx, by, pl.ds(pl.multiple_of(upper * 64 + part * 32, 32), 32)] if own else dst
        target = sibling if kind >= 2 else moved(pos, 2, 1 if kind == 0 else -1)
        return remote(src, dst, row_send.at[number, kind], row_recv.at[number, kind], target)

    def own_copy(number):
        one, two = keys.block(0, *places[number]), keys.block(1, *places[number])
        bx = jnp.where(upper == 0, one[0], two[0])
        by = jnp.where(upper == 0, one[1], two[1])
        return pltpu.make_async_copy(
            kc.at[bx, by, pl.ds(pl.multiple_of(upper * 64, 64), 64)], kr.at[bx, by], out_sem.at[number]
        )

    def relay(number):
        if number < 16:

            @pl.when(same & (away == 0))
            def _():
                for kind in (0, 1, 2, 3):
                    wave(number, kind, own=True).start()
                own_copy(number).start()

        for distance in (1, 2, 3):
            for kind, hops in ((0, distance), (1, 4 - distance)):
                block = number - LAG * hops
                if 0 <= block < 16:

                    @pl.when(same & (away == distance))
                    def _():
                        wave(block, kind).wait_recv()
                        if hops < 3:
                            wave(block, kind).start()
                        wave(block, kind + 2).start()

    def key_event(number):
        if number < 15:
            keys.event(number, 0)
            keys.event(number, 1)
        relay(number + 1)

    panel_rows = ColumnGather(cr, cr_send, cr_recv, pos)
    cov_events((7, 8))
    relay(0)
    key_event(0)
    first_keys.end()
    key_event(1)
    cov_events((10, 11))
    panel_rows.begin()
    for _, into in c_copies:
        into.wait_recv()
    mass = sum_c[0]
    for member in range(1, 8):
        mass = mass + sum_c[member]
    scale = lax.rsqrt(mass / HIDDEN + EPSILON) * (1.0 / 32.0)
    scale_ref[...] = scale * scale

    def save(number, source, target):
        return pltpu.make_async_copy(source, target, out_sem.at[16 + number])

    corner_raw = k5[...].reshape(512, PROMPTS).astype(F32)
    corner_keys = (corner_raw * scale[0:1]).astype(BF16)
    outer = lax.dot_general(corner_keys, corner_keys, (((1,), (1,)), ((), ())), preferred_element_type=F32)
    aug[:, 0:512] = jj[...].reshape(512, 512).astype(F32) + outer
    aug[:, 512:1024] = (
        lax.broadcasted_iota(jnp.int32, (512, 512), 0) == lax.broadcasted_iota(jnp.int32, (512, 512), 1)
    ).astype(F32)
    k5_scaled[...] = (corner_raw * (scale * scale)[0:1]).astype(BF16).reshape(8, 64, PROMPTS)
    save(0, k5_scaled, k5_out).start()
    beside = {
        2: 0, 3: 1, 4: 2, 5: 3, 6: 5, 7: 7, 8: 9, 9: 11, 10: 13, 11: 15, 12: 17, 13: 19, 14: 21, 15: 23, 16: 24, 17: 25, 18: 26, 19: 28, 20: 30,
    }
    extras = [{} for _ in range(4)]
    for number, step in beside.items():
        extras[step // 8][step % 8] = functools.partial(key_event, number)
    extras[0][4] = panel_rows.middle
    extras[1][0] = panel_rows.end
    extras[0][6] = lambda: cov_events((12,))
    extras[1][2] = lambda: cov_events((13, 14))
    extras[1][4] = lambda: save(1, cc, cc_out).start()
    extras[2][6] = lambda: save(2, kc, kc_out).start()
    extras[2][4] = lambda: save(3, cr, cr_out).start()
    factor(aug, work, extras)
    inv_ref[...] = aug[:, 512:1024]

    for number in range(16):

        @pl.when(k != lax.rem(source, 2))
        def _():
            wave(number, 2).wait_recv()
            wave(number, 3).wait_recv()

        @pl.when(same & (away == 0))
        def _():
            for kind in range(4):
                wave(number, kind, own=True).wait_send()
            own_copy(number).wait()

        for distance in (1, 2, 3):

            @pl.when(same & (away == distance))
            def _():
                for kind, hops in ((0, distance), (1, 4 - distance)):
                    if hops < 3:
                        wave(number, kind).wait_send()
                    wave(number, kind + 2).wait_send()

    first_tile.finish()
    keys.finish()
    panel_rows.finish()
    first_keys.finish()
    corner.finish()
    corner_tiles.finish()
    save(4, kr, kr_out).start()
    for ref, index in weights:
        swap(ref, index).wait_send()
    for copies in (square_copies, y_copies, x_copies, c_copies):
        for out, _ in copies:
            out.wait_send()
    gather.finish()
    covs.finish()
    for half in (0, 1):
        for number in range(16):
            to_sibling(half, number, *places[number]).wait_send()
    for chunk in range(4):
        for kind in range(6):
            for tile in (0, 1):
                hop(chunk, kind, tile).wait_send()
    save(0, k5_scaled, k5_out).wait()
    save(1, cc, cc_out).wait()
    save(2, kc, kc_out).wait()
    save(3, cr, cr_out).wait()
    save(4, kr, kr_out).wait()


def panel(residual, positions, gain, w_gate, w_up, cov):
    dma = pltpu.SemaphoreType.DMA
    vmem = pl.BlockSpec(memory_space=pltpu.VMEM)
    anywhere = pl.BlockSpec(memory_space=pl.ANY)
    spread = (
        ((4, 4, 128, PROMPTS), BF16),
        ((4, 4, 64, PROMPTS), BF16),
        ((8, 64, PROMPTS), BF16),
        ((8, 64, 1024), BF16),
        ((2, 4, 64, 2048), BF16),
    )
    return pl.pallas_call(
        panel_kernel,
        name="keys_and_panel",
        out_shape=tuple(jax.ShapeDtypeStruct(*one) for one in spread)
        + (jax.ShapeDtypeStruct((512, 512), F32), jax.ShapeDtypeStruct((8, PROMPTS), F32)),
        in_specs=[vmem] * 3 + [anywhere] * 3,
        out_specs=(anywhere,) * 5 + (vmem,) * 2,
        scratch_shapes=[
            pltpu.VMEM(*spread[0]), pltpu.VMEM(*spread[1]), pltpu.VMEM(*spread[2]), pltpu.VMEM(*spread[2]),
            pltpu.VMEM(*spread[3]), pltpu.VMEM(*spread[4]),
            pltpu.VMEM((1, 1, 64, PROMPTS), BF16),
            pltpu.VMEM((8, 64, 512), BF16),
            pltpu.VMEM((512, 1024), F32),
            pltpu.VMEM((128, 256), F32),
            pltpu.VMEM((2, 4, 4, 64, 640), BF16),
            pltpu.VMEM((2, 640, 1024), BF16),
            pltpu.VMEM((2, 640, 1024), BF16),
            pltpu.VMEM((4, 1280, 256), BF16),
            pltpu.VMEM((8, 64, 128), F32),
            pltpu.VMEM((4, 4, 128, 256), F32),
            pltpu.VMEM((4, 6, 2, 128, 128), BF16),
            pltpu.VMEM((4, 6, 2, 128, 128), BF16),
            pltpu.VMEM((128, PROMPTS), F32),
            pltpu.VMEM((4, 8, PROMPTS), F32),
            pltpu.VMEM((4, 8, PROMPTS), F32),
            pltpu.VMEM((8, 8, PROMPTS), F32),
            pltpu.VMEM((64, 2048), F32),
            pltpu.VMEM((1024, 128), F32),
            pltpu.VMEM((64, 128), F32),
            pltpu.VMEM((2, 4, 64, 128), BF16),
            dma((5,)), dma((2,)), dma((2,)), dma((7,)), dma((7,)), dma((2, 16)), dma((2, 16)), dma((2, 16)), dma((2, 16)),
            dma((4, 12)), dma((4, 12)), dma((3,)), dma((3,)), dma((3,)), dma((3,)), dma((7,)), dma((7,)), dma((2, 16)), dma((2, 16)),
            dma((2, 16)), dma((2, 16)), dma((8,)), dma((8,)), dma((8,)), dma((8,)), dma((8,)), dma((8,)), dma((2, 16)), dma((2, 16)),
            dma((16, 4)), dma((16, 4)), dma((21,)), dma((2, 16)), dma((2, 16)),
        ],
        compiler_params=pltpu.CompilerParams(collective_id=0, has_side_effects=True, vmem_limit_bytes=VMEM_LIMIT),
    )(residual, positions, gain, w_gate, w_up, cov)


def update_kernel(
    cov_ref, kc_ref, cc_ref, kr_ref, k5_ref, cr_ref, inv_ref, scale_ref, out_ref,
    covb, kcb, ccb, outb, panel, weights, rows, cov_sem, kc_sem, cc_sem, out_sem, zeros, zero_sem,
):
    x, y, z, k = here()
    row = x * 4 + y
    col = z * 2 + k
    nt = (((1,), (1,)), ((), ()))
    nn = (((1,), (0,)), ((), ()))
    tn = (((0,), (0,)), ((), ()))
    dot = functools.partial(lax.dot_general, preferred_element_type=F32)

    def load_cov(step):
        area = (pl.ds(step * 128, 1024 - step * 128), pl.ds(step * 256, 256))
        return pltpu.make_async_copy(cov_ref.at[area], covb.at[area], cov_sem.at[step])

    def load_kc(step):
        area = pl.ds(step * 2, 2)
        return pltpu.make_async_copy(kc_ref.at[area], kcb.at[area], kc_sem.at[step])

    def load_cc(step):
        area = (slice(None), slice(None), pl.ds(step * 256, 256))
        return pltpu.make_async_copy(cc_ref.at[area], ccb.at[area], cc_sem.at[step])

    def store(step):
        top = step * 128
        source = outb.at[step % 2, pl.ds(top, 1024 - top)]
        return pltpu.make_async_copy(source, out_ref.at[pl.ds(top, 1024 - top), pl.ds(step * 256, 256)], out_sem.at[step % 2])

    def clear(step):
        top = step * 128
        return pltpu.make_async_copy(zeros.at[pl.ds(0, top)], out_ref.at[pl.ds(0, top), pl.ds(step * 256, 256)], zero_sem.at[step])

    for step in range(8):
        load_kc(step).start()
        load_cc(step).start()
        load_cov(step).start()
    zeros[...] = jnp.zeros_like(zeros)
    for step in range(1, 8):
        clear(step).start()
    inverse = inv_ref[...]
    inverse_high = inverse.astype(BF16)
    first = k5_ref[...].reshape(512, PROMPTS)
    raw_rows = kr_ref[...].reshape(1024, PROMPTS)
    matrix_rows = cr_ref[...].reshape(512, 1024).astype(F32) + dot(first, raw_rows, nt)
    high, low = split(matrix_rows)
    panel_rows = dot(inverse_high, high, nn).astype(BF16)
    weights[...] = dot(panel_rows, inverse_high, tn).astype(BF16)
    own_high, own_low = split(inv_ref[pl.ds(pl.multiple_of(col * 64, 64), 64), :])
    panel[...] = dot(own_high, high, nn) + (dot(own_low, high, nn) + dot(own_high, low, nn))
    rows[...] = (raw_rows.astype(F32) * scale_ref[0:1] - dot(weights[...], first, nn)).astype(BF16)
    for step in range(8):
        top = step * 128
        height = 1024 - top
        load_kc(step).wait()
        load_cc(step).wait()
        load_cov(step).wait()
        if step >= 2:
            store(step - 2).wait()
        cols = kcb[2 * step : 2 * step + 2].reshape(256, PROMPTS)
        panel_cols = ccb[:, :, step * 256 : (step + 1) * 256].reshape(512, 256)
        value = covb[top:1024, step * 256 : (step + 1) * 256] + (dot(rows[top:], cols, nt) - dot(weights[top:], panel_cols, nn))
        if step == 0:
            value = jnp.concatenate([panel[...].T, value[:, 64:]], axis=1)
        edge = min(256, height)
        i = lax.broadcasted_iota(jnp.int32, (edge, 256), 0) + top
        j = lax.broadcasted_iota(jnp.int32, (edge, 256), 1) + step * 256
        row_global = (i // 64 * 16 + row) * 64 + i % 64
        col_global = (j // 64 * 8 + col) * 64 + j % 64
        outb[step % 2, top : top + edge] = jnp.where(row_global >= col_global, value[:edge], 0.0)
        if edge < height:
            outb[step % 2, top + edge : 1024] = value[edge:]
        store(step).start()
    store(6).wait()
    store(7).wait()
    for step in range(1, 8):
        clear(step).wait()


def update(cov, kc, kr, k5, cr, cc, inverse, scale):
    dma = pltpu.SemaphoreType.DMA
    vmem = pl.BlockSpec(memory_space=pltpu.VMEM)
    anywhere = pl.BlockSpec(memory_space=pl.ANY)
    return pl.pallas_call(
        update_kernel,
        name="update_lower",
        out_shape=jax.ShapeDtypeStruct((1024, 2048), F32),
        in_specs=[anywhere] * 3 + [vmem] * 5,
        out_specs=anywhere,
        scratch_shapes=[
            pltpu.VMEM((1024, 2048), F32), pltpu.VMEM((16, 128, PROMPTS), BF16), pltpu.VMEM((8, 64, 2048), BF16),
            pltpu.VMEM((2, 1024, 256), F32), pltpu.VMEM((64, 1024), F32), pltpu.VMEM((1024, 512), BF16), pltpu.VMEM((1024, PROMPTS), BF16),
            dma((8,)), dma((8,)), dma((8,)), dma((2,)), pltpu.VMEM((896, 256), F32), dma((8,)),
        ],
        compiler_params=pltpu.CompilerParams(vmem_limit_bytes=VMEM_LIMIT),
    )(cov, kc, cc, kr, k5, cr, inverse, scale)


def on_device(residual, positions, norm_gain, w_gate, w_up, covariance):
    kc, kr, k5, cr, cc, inverse, scale = panel(residual, positions, norm_gain, w_gate, w_up, covariance)
    kc = kc.reshape(16, 128, PROMPTS)
    kr = kr.reshape(16, 64, PROMPTS)
    cc = cc.reshape(8, 64, 2048)
    return update(covariance, kc, kr, k5, cr, cc, inverse, scale)


def solution(mesh):
    torus = Mesh(mesh.devices.reshape(4, 4, 4, 2), ("x", "y", "z", "k"))
    row, col = ("x", "y"), ("z", "k")
    placed = (P(row, None, col), P(row), P(col), P(col, row), P(col, row), P(row, col))
    return jax.shard_map(on_device, mesh=torus, in_specs=placed, out_specs=P(row, col), check_vma=False)
```

```python
import functools

import jax
import jax.numpy as jnp
from jax import lax
from jax.experimental import pallas as pl
from jax.experimental.pallas import tpu as pltpu
from jax.sharding import Mesh
from jax.sharding import PartitionSpec as P

MESH = pl.DeviceIdType.MESH
BF16 = jnp.bfloat16
F32 = jnp.float32
EPSILON = 1e-06
HIDDEN = 16384
WIDTH = 5120
PROMPTS = 1024
VMEM_LIMIT = 60 * 1024 * 1024
BASE = 16
LAG = 2


def here():
    return tuple(lax.axis_index(name) for name in ("x", "y", "z", "k"))


def moved(position, axis, step):
    place = list(position)
    size = 2 if axis == 3 else 4
    place[axis] = lax.rem(place[axis] + (step % size), size)
    return tuple(place)


def one_after_other(first, second):
    if first is not None:
        first()
    second()


def remote(src, dst, send, recv, target):
    return pltpu.make_async_remote_copy(
        src_ref=src, dst_ref=dst, send_sem=send, recv_sem=recv, device_id=target, device_id_type=MESH
    )


def greet(targets):
    barrier = pltpu.get_barrier_semaphore()
    for target in targets:
        pl.semaphore_signal(barrier, inc=1, device_id=target, device_id_type=MESH)
    pl.semaphore_wait(barrier, len(targets))


def when(condition, action):
    if condition is None:
        action()
    else:
        pl.when(condition)(action)


class PlaneGather:
    SENT = (
        (0, 0, 1, 1, None), (0, 0, 1, -1, None), (-1, 0, 1, 1, 0), (1, 0, 1, -1, 1),
        (0, 0, 0, 1, None), (-1, 0, 0, 1, None), (1, 0, 0, 1, None), (2, 0, 0, 1, None),
        (0, 0, 0, -1, None), (-1, 0, 0, -1, None), (1, 0, 0, -1, None), (2, 0, 0, -1, None),
        (0, -1, 0, 1, None), (-1, -1, 0, 1, None), (1, 1, 0, -1, None), (2, 1, 0, -1, None),
    )
    GOT = (
        (-1, 0, None), (1, 0, None), (2, 0, 0), (2, 0, 1),
        (0, -1, None), (-1, -1, None), (1, -1, None), (2, -1, None),
        (0, 1, None), (-1, 1, None), (1, 1, None), (2, 1, None),
        (0, 2, None), (-1, 2, None), (1, 2, None), (2, 2, None),
    )
    EVENTS = (
        ((0,), (2, 5, 9)), ((1,), (3, 6, 10)), ((4,), (12,)), ((8,), ()), ((2, 3), (7, 11)), ((5,), (13,)), ((10,), (14,)),
        ((9,), ()), ((6,), ()), ((11,), (15,)), ((7,), ()), ((12,), ()), ((13,), ()), ((14,), ()), ((15,), ()),
    )
    PLACES = tuple(((-1, 0), (1, 0), (0, -1), (0, 1), (2, 0), (-1, -1), (1, 1), (-1, 1), (1, -1), (2, 1), (2, -1), (0, 2), (-1, 2), (1, 2), (2, 2)))

    def __init__(self, buf, rows, send, recv, pos, only=None):
        self.buf, self.rows, self.send, self.recv, self.pos, self.only = buf, rows, send, recv, pos, only

    def block(self, half, first, second):
        dx, dy = (second, first) if half == 0 else (first, second)
        return lax.rem(self.pos[0] + dx % 4, 4), lax.rem(self.pos[1] + dy % 4, 4)

    def piece(self, half, first, second, part=None):
        size = self.rows // 2
        start = half * size
        if part is not None:
            size //= 2
            start += part * size
        bx, by = self.block(half, first, second)
        return self.buf.at[bx, by, pl.ds(start, size)]

    def cond(self, half, first, second):
        return None if self.only is None else self.only(*self.block(half, first, second))

    def copy(self, half, kind, first, second, axis, step, part=None):
        axis = axis if half == 0 else 1 - axis
        ref = self.piece(half, first, second, part)
        return remote(ref, ref, self.send.at[half, kind], self.recv.at[half, kind], moved(self.pos, axis, step))

    def go(self, half, kind):
        first, second, axis, step, part = self.SENT[kind]
        when(self.cond(half, first, second), lambda: self.copy(half, kind, first, second, axis, step, part).start())

    def arrive(self, half, kind):
        first, second, part = self.GOT[kind]
        when(self.cond(half, first, second), lambda: self.copy(half, kind, first, second, 0, 1, part).wait_recv())

    def begin(self):
        for kind in (0, 1, 4, 8):
            for half in (0, 1):
                self.go(half, kind)

    def event(self, number, half):
        kinds, on = self.EVENTS[number]
        for kind in kinds:
            self.arrive(half, kind)
        for kind in on:
            self.go(half, kind)

    def finish(self):
        for half in (0, 1):
            for kind in range(16):
                first, second, axis, step, part = self.SENT[kind]
                when(
                    self.cond(half, first, second),
                    lambda: self.copy(half, kind, first, second, axis, step, part).wait_send(),
                )


class ColumnGather:
    def __init__(self, buf, send, recv, pos):
        self.buf, self.send, self.recv, self.pos = buf, send, recv, pos

    def piece(self, dz, dk=0, part=None):
        z, k = self.pos[2], self.pos[3]
        slot = lax.rem(z + dz % 4, 4) * 2 + lax.rem(k + dk, 2)
        if part is None:
            return self.buf.at[slot]
        return self.buf.at[slot, pl.ds(32 * part, 32)]

    SENT = {0: (0, 2, 1, None), 1: (0, 2, -1, None), 2: (-1, 2, 1, 0), 3: (1, 2, -1, 1),
            4: (0, 3, 1, None), 5: (-1, 3, 1, None), 6: (1, 3, 1, None), 7: (2, 3, 1, None)}
    GOT = {0: (-1, 0, None), 1: (1, 0, None), 2: (2, 0, 0), 3: (2, 0, 1),
           4: (0, 1, None), 5: (-1, 1, None), 6: (1, 1, None), 7: (2, 1, None)}

    def go(self, kind):
        dz, axis, step, part = self.SENT[kind]
        ref = self.piece(dz, 0, part)
        remote(ref, ref, self.send.at[kind], self.recv.at[kind], moved(self.pos, axis, step)).start()

    def arrive(self, kind):
        dz, dk, part = self.GOT[kind]
        ref = self.piece(dz, dk, part)
        remote(ref, ref, self.send.at[kind], self.recv.at[kind], moved(self.pos, 2, 1)).wait_recv()

    def begin(self):
        for kind in (0, 1, 4):
            self.go(kind)

    def middle(self):
        self.arrive(0)
        self.go(2)
        self.go(5)
        self.arrive(1)
        self.go(3)
        self.go(6)

    def end(self):
        self.arrive(2)
        self.arrive(3)
        self.go(7)
        for kind in (4, 5, 6, 7):
            self.arrive(kind)

    def finish(self):
        for kind in range(8):
            dz, axis, step, part = self.SENT[kind]
            ref = self.piece(dz, 0, part)
            remote(ref, ref, self.send.at[kind], self.recv.at[kind], moved(self.pos, axis, step)).wait_send()


def column_peers(pos):
    peers = []
    for dz in range(4):
        for dk in range(2):
            if dz or dk:
                peers.append(moved(moved(pos, 2, dz), 3, dk))
    return peers


def to_all_columns(buf, send, recv, pos):
    copies = []
    mine = pos[2] * 2 + pos[3]
    number = 0
    for dz in range(4):
        for dk in range(2):
            if dz == 0 and dk == 0:
                continue
            target = moved(moved(pos, 2, dz), 3, dk)
            out = remote(buf.at[mine], buf.at[mine], send.at[number], recv.at[number], target)
            origin = moved(moved(pos, 2, -dz), 3, -dk)
            slot = origin[2] * 2 + origin[3]
            into = remote(buf.at[slot], buf.at[slot], send.at[number], recv.at[number], target)
            copies.append((out, into))
            number += 1
    return copies


def to_axis(buf, send, recv, pos, axis):
    copies = []
    mine = pos[axis]
    for step in (1, 2, 3):
        target = moved(pos, axis, step)
        out = remote(buf.at[mine], buf.at[mine], send.at[step - 1], recv.at[step - 1], target)
        slot = moved(pos, axis, -step)[axis]
        into = remote(buf.at[slot], buf.at[slot], send.at[step - 1], recv.at[step - 1], target)
        copies.append((out, into))
    return copies


def exchange(copies):
    for out, _ in copies:
        out.start()
    for _, into in copies:
        into.wait_recv()


def split(value):
    high = value.astype(BF16)
    return high, (value - high.astype(F32)).astype(BF16)


def dot3(left, right, dims):
    lh, ll = split(left)
    rh, rl = split(right)
    dot = functools.partial(lax.dot_general, dimension_numbers=(dims, ((), ())), preferred_element_type=F32)
    return dot(lh, rh) + (dot(lh, rl) + dot(ll, rh))


def small_factor(work, extra):
    lane = lax.broadcasted_iota(jnp.int32, (1, 128), 1)

    def body(step, carry):
        start = pl.multiple_of(step * BASE, BASE)
        rows = work[pl.ds(start, BASE), :]
        turned = pltpu.roll(rows[:, :128], lax.rem(128 - start, 128), 1)
        entry = [[jnp.broadcast_to(turned[i : i + 1, j : j + 1], (1, 128)) for j in range(i + 1)] for i in range(BASE)]
        solved = []
        for j in range(BASE):
            inverse = lax.rsqrt(entry[j][j])
            row = rows[j : j + 1, :]
            for m in range(j):
                row = row - jnp.concatenate([entry[j][m]] * 2, axis=1) * solved[m]
            solved.append(row * jnp.concatenate([inverse] * 2, axis=1))
            for i in range(j + 1, BASE):
                entry[i][j] = entry[i][j] * inverse
            for i in range(j + 1, BASE):
                for m in range(j + 1, i + 1):
                    entry[i][m] = entry[i][m] - entry[i][j] * entry[m][j]
        block = jnp.concatenate(solved, axis=0)
        work[pl.ds(start, BASE), :] = block
        later = jnp.where(lane >= start + BASE, block[:, :128], 0.0)
        lh, ll = split(later)
        rh, rl = split(block)
        left = jnp.concatenate([lh, lh, ll], axis=0)
        right = jnp.concatenate([rh, rl, rh], axis=0)
        work[...] = work[...] - lax.dot_general(left, right, (((0,), (0,)), ((), ())), preferred_element_type=F32)
        for number, action in extra.items():
            pl.when(step == number)(action)
        return carry

    lax.fori_loop(0, 128 // BASE, body, 0)


def factor(aug, work, extras):
    eye = (lax.broadcasted_iota(jnp.int32, (128, 128), 0) == lax.broadcasted_iota(jnp.int32, (128, 128), 1)).astype(F32)
    for number in range(4):
        lo, hi = number * 128, (number + 1) * 128
        work[:, 0:128] = aug[lo:hi, lo:hi]
        work[:, 128:256] = eye
        small_factor(work, extras[number])
        inverse = work[:, 128:256]
        if hi < 512:
            right = dot3(inverse, aug[lo:hi, hi : 512 + lo], ((1,), (0,)))
            full = jnp.concatenate([right, inverse], axis=1)
            aug[lo:hi, hi : 512 + hi] = full
            ahead = right[:, 0 : 512 - hi]
            aug[hi:512, hi : 512 + hi] = aug[hi:512, hi : 512 + hi] - dot3(ahead, full, ((0,), (0,)))
        else:
            aug[lo:hi, 512 : 512 + lo] = dot3(inverse, aug[lo:hi, 512 : 512 + lo], ((1,), (0,)))
            aug[lo:hi, 512 + lo : 512 + hi] = inverse


def panel_kernel(
    residual_ref, positions_ref, gain_ref, gate_ref, up_ref, cov_ref, kc_out, kr_out, k5_out, cr_out, cc_out, inv_ref, scale_ref,
    kc, kr, k5, k5_scaled, cr, cc, first, jj, aug, work,
    xx, own_w, other_w, sel_w, squares, part, hop_out, hop_in, total, sum_y, sum_x, sum_c, cov_rows, cov_cols, cov_corner, tiles,
    local_sem, w_send, w_recv, sq_send, sq_recv, x_send, x_recv, sib_send, sib_recv,
    hop_send, hop_recv, sy_send, sy_recv, sx_send, sx_recv, sc_send, sc_recv, cc_send, cc_recv,
    kc_send, kc_recv, k5_send, k5_recv, cr_send, cr_recv, jj_send, jj_recv, f_send, f_recv, row_send, row_recv, out_sem, tile_send, tile_recv,
):
    pos = here()
    x, y, z, k = pos
    sibling = moved(pos, 3, 1)
    col = z * 2 + k
    plane = [moved(pos, axis, step) for axis in (0, 1) for step in (1, 2, 3)]
    barrier = pltpu.get_barrier_semaphore()
    peers = plane + column_peers(pos)
    for peer in peers:
        pl.semaphore_signal(barrier, inc=1, device_id=peer, device_id_type=MESH)

    weights = ((gate_ref, 0), (up_ref, 1))

    def swap(ref, index):
        return remote(ref, other_w.at[index], w_send.at[index], w_recv.at[index], sibling)

    def fetch(ref, index):
        return pltpu.make_async_copy(ref, own_w.at[index], local_sem.at[index])

    fetch_rows = pltpu.make_async_copy(cov_ref.at[pl.ds(0, 64)], cov_rows, local_sem.at[2])
    fetch_cols = pltpu.make_async_copy(cov_ref.at[:, pl.ds(0, 128)], cov_cols, local_sem.at[3])

    fetch_corner = pltpu.make_async_copy(cov_ref.at[pl.ds(0, 64), pl.ds(0, 128)], cov_corner, local_sem.at[4])
    fetch_corner.start()
    line_of = lax.broadcasted_iota(jnp.int32, (64, 64), 0)
    prompt_of = lax.broadcasted_iota(jnp.int32, (64, 64), 1)
    place = positions_ref[...].reshape(1, 64).astype(F32)
    place = jnp.sum(jnp.where(line_of == prompt_of, place, 0.0), axis=1, keepdims=True)
    token = lax.broadcasted_iota(jnp.int32, (64, 1024), 1) - 16 * lax.broadcasted_iota(jnp.int32, (64, 1024), 0)
    pick = (token.astype(F32) == place).astype(BF16)
    subject = jnp.dot(pick, residual_ref[...].reshape(1024, 640), preferred_element_type=F32)
    squared = subject * subject
    folded = squared[:, 0:128]
    for group in range(1, 5):
        folded = folded + squared[:, group * 128 : (group + 1) * 128]
    own_mass = jnp.sum(folded, axis=1, keepdims=True)
    mass_row = jnp.sum(jnp.where(line_of == prompt_of, own_mass, 0.0), axis=0, keepdims=True)
    squares[col] = jnp.broadcast_to(jnp.concatenate([mass_row, mass_row], axis=1), (8, 128))
    pl.semaphore_wait(barrier, len(peers))
    square_copies = to_all_columns(squares, sq_send, sq_recv, pos)
    for out, _ in square_copies:
        out.start()
    for ref, index in weights:
        fetch(ref, index).start()
        swap(ref, index).start()
    fetch_corner.wait()

    @pl.when(x < 2)
    def _():
        tiles[x, y] = cov_corner[...].astype(BF16)

    corner_tiles = PlaneGather(tiles, 64, tile_send, tile_recv, pos, only=lambda bx, by: bx < 2)
    corner_tiles.begin()

    def tile_events(numbers):
        for number in numbers:
            for half in (0, 1):
                corner_tiles.event(number, half)

    fetch_rows.start()
    fetch_cols.start()

    def select(source, core):
        def body(step, carry):
            first = pl.ds(pl.multiple_of(step * 128, 128), 128)
            second = pl.ds(pl.multiple_of(512 + step * 128, 128), 128)
            rows = pl.ds(pl.multiple_of(core * 640, 128), 640)
            for index, lanes in enumerate((first, second)):
                gate, up = source[0, :, lanes], source[1, :, lanes]

                @pl.when(k == 0)
                def _():
                    sel_w[step, rows, pl.ds(index * 128, 128)] = jnp.concatenate([gate[:, :64], up[:, :64]], axis=1)

                @pl.when(k == 1)
                def _():
                    sel_w[step, rows, pl.ds(index * 128, 128)] = jnp.concatenate([gate[:, 64:], up[:, 64:]], axis=1)

            return carry

        lax.fori_loop(0, 4, body, 0)

    for _, into in square_copies:
        into.wait_recv()
    everyone = squares[0]
    for member in range(1, 8):
        everyone = everyone + squares[member]
    everyone = jnp.sum(jnp.where(line_of == prompt_of, everyone[0:1, 0:64], 0.0), axis=1, keepdims=True)
    inverse_rms = lax.rsqrt(everyone / WIDTH + EPSILON)
    xx[k, x, y] = (subject * inverse_rms * gain_ref[...].reshape(1, 640)).astype(BF16)

    gather = PlaneGather(xx.at[k], 64, x_send, x_recv, pos)
    gather.begin()

    def to_sibling(half, number, first, second):
        ref = gather.piece(half, first, second)
        return remote(ref, ref, sib_send.at[half, number], sib_recv.at[half, number], sibling)

    def from_sibling(half, number, first, second):
        bx, by = gather.block(half, first, second)
        ref = xx.at[1 - k, bx, by, pl.ds(half * 32, 32)]
        return remote(ref, ref, sib_send.at[half, number], sib_recv.at[half, number], sibling)

    places = ((0, 0),) + PlaneGather.PLACES
    for half in (0, 1):
        to_sibling(half, 0, 0, 0).start()

    for ref, index in weights:
        fetch(ref, index).wait()
    select(own_w, k)

    def arrivals(numbers):
        for number in numbers:
            for half in (0, 1):
                gather.event(number, half)
                to_sibling(half, number + 1, *places[number + 1]).start()

    def siblings(numbers):
        for number in numbers:
            for half in (0, 1):
                from_sibling(half, number, *places[number]).wait_recv()

    def line(core, half, second):
        if half == 0:
            value = xx[core, lax.rem(x + second % 4, 4), :, 0:32, :]
        else:
            value = xx[core, :, lax.rem(y + second % 4, 4), 32:64, :]
        return value.reshape(128, 640)

    def product(chunk, dest):
        second = (0, -1, 1, 2)[chunk]
        value = None
        for core in (0, 1):
            left = jnp.concatenate([line(core, 0, second), line(core, 1, second)], axis=0)
            term = jnp.dot(left, sel_w[dest, core * 640 : core * 640 + 640], preferred_element_type=F32)
            value = term if value is None else value + term
        return value

    def dest(step):
        return lax.rem(z + step % 4, 4)

    def hop(chunk, kind, tile):
        target = moved(pos, 2, 1 if kind % 2 == 0 else -1)
        return remote(
            hop_out.at[chunk, kind, tile], hop_in.at[chunk, kind, tile],
            hop_send.at[chunk, kind + 6 * tile], hop_recv.at[chunk, kind + 6 * tile], target,
        )

    def lanes(tile):
        return slice(128 * tile, 128 * tile + 128)

    def multiply(chunk, hold):
        def send(kind, value):
            for tile in (0, 1):
                hop_out[chunk, kind, tile] = value[:, lanes(tile)].astype(BF16)
                if tile == 0 or not hold:
                    hop(chunk, kind, tile).start()

        value = product(chunk, dest(2))
        send(0, value[:128])
        send(1, value[128:])
        value = product(chunk, dest(1))
        send(2, value[128:])
        part[chunk, 0] = value[:128]
        value = product(chunk, dest(-1))
        send(3, value[:128])
        part[chunk, 1] = value[128:]
        value = product(chunk, dest(0))
        part[chunk, 2] = value[:128]
        part[chunk, 3] = value[128:]

    def release(chunk):
        for kind in range(4):
            hop(chunk, kind, 1).start()

    def join(chunk, tile):
        for kind in (0, 1):
            hop(chunk, kind, tile).wait_recv()
            value = part[chunk, kind, :, lanes(tile)] + hop_in[chunk, kind, tile].astype(F32)
            hop_out[chunk, 4 + kind, tile] = value.astype(BF16)
            hop(chunk, 4 + kind, tile).start()

    def finish(chunk, tile):
        second = (0, -1, 1, 2)[chunk]
        for half in (0, 1):
            kinds = (4, 3) if half == 0 else (2, 5)
            for kind in kinds:
                hop(chunk, kind, tile).wait_recv()
            value = part[chunk, 2 + half, :, lanes(tile)] + (
                hop_in[chunk, kinds[0], tile].astype(F32) + hop_in[chunk, kinds[1], tile].astype(F32)
            )
            turned = value.T
            gate, up = turned[:64], turned[64:]
            raw = gate / (1.0 + jnp.exp(-gate)) * up
            place = lax.rem((x if half == 0 else y) + second % 4, 4)
            total[pl.ds(64 * tile, 64), pl.ds(pl.multiple_of(half * 512 + place * 128, 128), 128)] = raw

    covs = PlaneGather(cc, 64, cc_send, cc_recv, pos, only=lambda bx, by: bx < 2)

    def cov_events(numbers):
        for number in numbers:
            for half in (0, 1):
                covs.event(number, half)

    arrivals((0, 1, 4))
    for ref, index in weights:
        swap(ref, index).wait_recv()
    select(other_w, 1 - k)
    arrivals((2, 3))
    siblings((0, 1, 2, 5))
    multiply(0, False)
    arrivals((5, 8, 10))
    tile_events((0, 1, 2, 3))
    siblings((3, 6, 9, 11))
    multiply(1, False)
    join(0, 0)
    arrivals((6, 7, 9))
    fetch_rows.wait()

    @pl.when(x < 2)
    def _():
        cc[x, y] = cov_rows[...].astype(BF16)

    covs.begin()
    tile_events((4, 5, 6, 7, 8))
    siblings((4, 7, 8, 10))
    join(0, 1)
    multiply(2, True)
    join(1, 0)
    arrivals((11, 12, 13, 14))
    siblings((12, 13, 14, 15))
    multiply(3, True)
    release(2)
    release(3)
    join(2, 0)
    join(3, 0)
    join(1, 1)
    tile_events(range(9, 15))
    cov_events((0, 1))
    for chunk in range(4):
        finish(chunk, 0)
    row = x * 4 + y

    @pl.when(row == 0)
    def _():
        first[0, 0] = total[0:64].astype(BF16)

    first_tile = PlaneGather(first, 64, f_send, f_recv, pos, only=lambda bx, by: (bx == 0) & (by == 0))
    first_tile.begin()

    def first_events(numbers):
        for number in numbers:
            first_tile.event(number, 0)
            first_tile.event(number, 1)

    join(2, 1)
    join(3, 1)
    jj[col] = tiles[...].reshape(512, 128).astype(F32).T[0:64].astype(BF16)
    corner = ColumnGather(jj, jj_send, jj_recv, pos)
    corner.begin()
    cov_events((2, 3, 4))
    fetch_cols.wait()
    cr[col] = cov_cols[...].T[0:64].astype(BF16)
    first_events((0, 1, 2, 3))
    finish(0, 1)
    first_events((4, 5, 6, 7, 8))
    finish(1, 1)
    finish(2, 1)
    corner.middle()
    finish(3, 1)
    raw = total[...]
    mass = jnp.sum(raw * raw, axis=0, keepdims=True)
    sum_y[y] = jnp.broadcast_to(mass, (8, PROMPTS))
    y_copies = to_axis(sum_y, sy_send, sy_recv, pos, 1)
    for out, _ in y_copies:
        out.start()
    kc[x, y] = raw.astype(BF16)
    keys = PlaneGather(kc, 128, kc_send, kc_recv, pos)
    keys.begin()
    first_events(range(9, 15))
    k5[col] = first[0, 0]
    first_keys = ColumnGather(k5, k5_send, k5_recv, pos)
    first_keys.begin()
    cov_events((5, 6, 9))
    for _, into in y_copies:
        into.wait_recv()
    sum_x[x] = sum_y[0] + sum_y[1] + sum_y[2] + sum_y[3]
    x_copies = to_axis(sum_x, sx_send, sx_recv, pos, 0)
    for out, _ in x_copies:
        out.start()
    corner.end()
    first_keys.middle()
    for _, into in x_copies:
        into.wait_recv()
    sum_c[col] = sum_x[0] + sum_x[1] + sum_x[2] + sum_x[3]
    c_copies = to_all_columns(sum_c, sc_send, sc_recv, pos)
    for out, _ in c_copies:
        out.start()

    source = lax.rem(row, 8)
    source_z = source // 2
    upper = row // 8
    away = lax.rem(z + 4 - source_z, 4)
    same = k == lax.rem(source, 2)

    def wave(number, kind, own=False):
        one, two = keys.block(0, *places[number]), keys.block(1, *places[number])
        bx = jnp.where(upper == 0, one[0], two[0])
        by = jnp.where(upper == 0, one[1], two[1])
        part = kind % 2
        dst = kr.at[bx, by, pl.ds(part * 32, 32)]
        src = kc.at[bx, by, pl.ds(pl.multiple_of(upper * 64 + part * 32, 32), 32)] if own else dst
        target = sibling if kind >= 2 else moved(pos, 2, 1 if kind == 0 else -1)
        return remote(src, dst, row_send.at[number, kind], row_recv.at[number, kind], target)

    def own_copy(number):
        one, two = keys.block(0, *places[number]), keys.block(1, *places[number])
        bx = jnp.where(upper == 0, one[0], two[0])
        by = jnp.where(upper == 0, one[1], two[1])
        return pltpu.make_async_copy(
            kc.at[bx, by, pl.ds(pl.multiple_of(upper * 64, 64), 64)], kr.at[bx, by], out_sem.at[number]
        )

    def relay(number):
        if number < 16:

            @pl.when(same & (away == 0))
            def _():
                for kind in (0, 1, 2, 3):
                    wave(number, kind, own=True).start()
                own_copy(number).start()

        for distance in (1, 2, 3):
            for kind, hops in ((0, distance), (1, 4 - distance)):
                block = number - LAG * hops
                if 0 <= block < 16:

                    @pl.when(same & (away == distance))
                    def _():
                        wave(block, kind).wait_recv()
                        if hops < 3:
                            wave(block, kind).start()
                        wave(block, kind + 2).start()

    def key_event(number):
        if number < 15:
            keys.event(number, 0)
            keys.event(number, 1)
        relay(number + 1)

    panel_rows = ColumnGather(cr, cr_send, cr_recv, pos)
    cov_events((7, 8))
    relay(0)
    key_event(0)
    first_keys.end()
    key_event(1)
    panel_rows.begin()
    for _, into in c_copies:
        into.wait_recv()
    mass = sum_c[0]
    for member in range(1, 8):
        mass = mass + sum_c[member]
    scale = lax.rsqrt(mass / HIDDEN + EPSILON) * (1.0 / 32.0)
    scale_ref[...] = scale * scale

    def save(number, source, target):
        return pltpu.make_async_copy(source, target, out_sem.at[16 + number])

    corner_raw = k5[...].reshape(512, PROMPTS).astype(F32)
    corner_keys = (corner_raw * scale[0:1]).astype(BF16)
    outer = lax.dot_general(corner_keys, corner_keys, (((1,), (1,)), ((), ())), preferred_element_type=F32)
    aug[:, 0:512] = jj[...].reshape(512, 512).astype(F32) + outer
    aug[:, 512:1024] = (
        lax.broadcasted_iota(jnp.int32, (512, 512), 0) == lax.broadcasted_iota(jnp.int32, (512, 512), 1)
    ).astype(F32)
    k5_scaled[...] = (corner_raw * (scale * scale)[0:1]).astype(BF16).reshape(8, 64, PROMPTS)
    save(0, k5_scaled, k5_out).start()
    beside = {
        2: 0, 3: 1, 4: 2, 5: 3, 6: 4, 7: 6, 8: 7, 9: 8, 10: 9, 11: 11, 12: 13, 13: 15, 14: 17, 15: 19, 16: 21, 17: 23, 18: 25, 19: 27, 20: 29,
    }
    extras = [{} for _ in range(4)]
    for number, step in beside.items():
        extras[step // 8][step % 8] = functools.partial(key_event, number)
    others = (
        (3, lambda: cov_events((10,))),
        (4, panel_rows.middle),
        (6, lambda: cov_events((11,))),
        (8, panel_rows.end),
        (8, lambda: cov_events((12,))),
        (10, lambda: cov_events((13,))),
        (12, lambda: cov_events((14,))),
        (14, lambda: save(1, cc, cc_out).start()),
        (20, lambda: save(3, cr, cr_out).start()),
        (22, lambda: save(2, kc, kc_out).start()),
    )
    for step, action in others:
        extras[step // 8][step % 8] = functools.partial(one_after_other, extras[step // 8].get(step % 8), action)
    factor(aug, work, extras)
    inv_ref[...] = aug[:, 512:1024]

    for number in range(16):

        @pl.when(k != lax.rem(source, 2))
        def _():
            wave(number, 2).wait_recv()
            wave(number, 3).wait_recv()

        @pl.when(same & (away == 0))
        def _():
            for kind in range(4):
                wave(number, kind, own=True).wait_send()
            own_copy(number).wait()

        for distance in (1, 2, 3):

            @pl.when(same & (away == distance))
            def _():
                for kind, hops in ((0, distance), (1, 4 - distance)):
                    if hops < 3:
                        wave(number, kind).wait_send()
                    wave(number, kind + 2).wait_send()

    first_tile.finish()
    keys.finish()
    panel_rows.finish()
    first_keys.finish()
    corner.finish()
    corner_tiles.finish()
    save(4, kr, kr_out).start()
    for ref, index in weights:
        swap(ref, index).wait_send()
    for copies in (square_copies, y_copies, x_copies, c_copies):
        for out, _ in copies:
            out.wait_send()
    gather.finish()
    covs.finish()
    for half in (0, 1):
        for number in range(16):
            to_sibling(half, number, *places[number]).wait_send()
    for chunk in range(4):
        for kind in range(6):
            for tile in (0, 1):
                hop(chunk, kind, tile).wait_send()
    save(0, k5_scaled, k5_out).wait()
    save(1, cc, cc_out).wait()
    save(2, kc, kc_out).wait()
    save(3, cr, cr_out).wait()
    save(4, kr, kr_out).wait()


def panel(residual, positions, gain, w_gate, w_up, cov):
    dma = pltpu.SemaphoreType.DMA
    vmem = pl.BlockSpec(memory_space=pltpu.VMEM)
    anywhere = pl.BlockSpec(memory_space=pl.ANY)
    spread = (
        ((4, 4, 128, PROMPTS), BF16),
        ((4, 4, 64, PROMPTS), BF16),
        ((8, 64, PROMPTS), BF16),
        ((8, 64, 1024), BF16),
        ((2, 4, 64, 2048), BF16),
    )
    return pl.pallas_call(
        panel_kernel,
        name="keys_and_panel",
        out_shape=tuple(jax.ShapeDtypeStruct(*one) for one in spread)
        + (jax.ShapeDtypeStruct((512, 512), F32), jax.ShapeDtypeStruct((8, PROMPTS), F32)),
        in_specs=[vmem] * 3 + [anywhere] * 3,
        out_specs=(anywhere,) * 5 + (vmem,) * 2,
        scratch_shapes=[
            pltpu.VMEM(*spread[0]), pltpu.VMEM(*spread[1]), pltpu.VMEM(*spread[2]), pltpu.VMEM(*spread[2]),
            pltpu.VMEM(*spread[3]), pltpu.VMEM(*spread[4]),
            pltpu.VMEM((1, 1, 64, PROMPTS), BF16),
            pltpu.VMEM((8, 64, 512), BF16),
            pltpu.VMEM((512, 1024), F32),
            pltpu.VMEM((128, 256), F32),
            pltpu.VMEM((2, 4, 4, 64, 640), BF16),
            pltpu.VMEM((2, 640, 1024), BF16),
            pltpu.VMEM((2, 640, 1024), BF16),
            pltpu.VMEM((4, 1280, 256), BF16),
            pltpu.VMEM((8, 8, 128), F32),
            pltpu.VMEM((4, 4, 128, 256), F32),
            pltpu.VMEM((4, 6, 2, 128, 128), BF16),
            pltpu.VMEM((4, 6, 2, 128, 128), BF16),
            pltpu.VMEM((128, PROMPTS), F32),
            pltpu.VMEM((4, 8, PROMPTS), F32),
            pltpu.VMEM((4, 8, PROMPTS), F32),
            pltpu.VMEM((8, 8, PROMPTS), F32),
            pltpu.VMEM((64, 2048), F32),
            pltpu.VMEM((1024, 128), F32),
            pltpu.VMEM((64, 128), F32),
            pltpu.VMEM((2, 4, 64, 128), BF16),
            dma((5,)), dma((2,)), dma((2,)), dma((7,)), dma((7,)), dma((2, 16)), dma((2, 16)), dma((2, 16)), dma((2, 16)),
            dma((4, 12)), dma((4, 12)), dma((3,)), dma((3,)), dma((3,)), dma((3,)), dma((7,)), dma((7,)), dma((2, 16)), dma((2, 16)),
            dma((2, 16)), dma((2, 16)), dma((8,)), dma((8,)), dma((8,)), dma((8,)), dma((8,)), dma((8,)), dma((2, 16)), dma((2, 16)),
            dma((16, 4)), dma((16, 4)), dma((21,)), dma((2, 16)), dma((2, 16)),
        ],
        compiler_params=pltpu.CompilerParams(collective_id=0, has_side_effects=True, vmem_limit_bytes=VMEM_LIMIT),
    )(residual, positions, gain, w_gate, w_up, cov)


def update_kernel(
    cov_ref, kc_ref, cc_ref, kr_ref, k5_ref, cr_ref, inv_ref, scale_ref, out_ref,
    covb, kcb, ccb, outb, panel, weights, rows, cov_sem, kc_sem, cc_sem, out_sem, zeros, zero_sem,
):
    x, y, z, k = here()
    row = x * 4 + y
    col = z * 2 + k
    nt = (((1,), (1,)), ((), ()))
    nn = (((1,), (0,)), ((), ()))
    tn = (((0,), (0,)), ((), ()))
    dot = functools.partial(lax.dot_general, preferred_element_type=F32)

    def load_cov(step):
        area = (pl.ds(step * 128, 1024 - step * 128), pl.ds(step * 256, 256))
        return pltpu.make_async_copy(cov_ref.at[area], covb.at[area], cov_sem.at[step])

    def load_kc(step):
        area = pl.ds(step * 2, 2)
        return pltpu.make_async_copy(kc_ref.at[area], kcb.at[area], kc_sem.at[step])

    def load_cc(step):
        area = (slice(None), slice(None), pl.ds(step * 256, 256))
        return pltpu.make_async_copy(cc_ref.at[area], ccb.at[area], cc_sem.at[step])

    def store(step):
        top = step * 128
        source = outb.at[step % 2, pl.ds(top, 1024 - top)]
        return pltpu.make_async_copy(source, out_ref.at[pl.ds(top, 1024 - top), pl.ds(step * 256, 256)], out_sem.at[step % 2])

    def clear(step):
        top = step * 128
        return pltpu.make_async_copy(zeros.at[pl.ds(0, top)], out_ref.at[pl.ds(0, top), pl.ds(step * 256, 256)], zero_sem.at[step])

    for step in range(8):
        load_kc(step).start()
        load_cc(step).start()
        load_cov(step).start()
    zeros[...] = jnp.zeros_like(zeros)
    for step in range(1, 8):
        clear(step).start()
    inverse = inv_ref[...]
    inverse_high = inverse.astype(BF16)
    first = k5_ref[...].reshape(512, PROMPTS)
    raw_rows = kr_ref[...].reshape(1024, PROMPTS)
    matrix_rows = cr_ref[...].reshape(512, 1024).astype(F32) + dot(first, raw_rows, nt)
    high, low = split(matrix_rows)
    panel_rows = dot(inverse_high, high, nn).astype(BF16)
    weights[...] = dot(panel_rows, inverse_high, tn).astype(BF16)
    own_high, own_low = split(inv_ref[pl.ds(pl.multiple_of(col * 64, 64), 64), :])
    panel[...] = dot(own_high, high, nn) + (dot(own_low, high, nn) + dot(own_high, low, nn))
    rows[...] = (raw_rows.astype(F32) * scale_ref[0:1] - dot(weights[...], first, nn)).astype(BF16)
    for step in range(8):
        top = step * 128
        height = 1024 - top
        load_kc(step).wait()
        load_cc(step).wait()
        load_cov(step).wait()
        if step >= 2:
            store(step - 2).wait()
        cols = kcb[2 * step : 2 * step + 2].reshape(256, PROMPTS)
        panel_cols = ccb[:, :, step * 256 : (step + 1) * 256].reshape(512, 256)
        value = covb[top:1024, step * 256 : (step + 1) * 256] + (dot(rows[top:], cols, nt) - dot(weights[top:], panel_cols, nn))
        if step == 0:
            value = jnp.concatenate([panel[...].T, value[:, 64:]], axis=1)
        edge = min(256, height)
        i = lax.broadcasted_iota(jnp.int32, (edge, 256), 0) + top
        j = lax.broadcasted_iota(jnp.int32, (edge, 256), 1) + step * 256
        row_global = (i // 64 * 16 + row) * 64 + i % 64
        col_global = (j // 64 * 8 + col) * 64 + j % 64
        outb[step % 2, top : top + edge] = jnp.where(row_global >= col_global, value[:edge], 0.0)
        if edge < height:
            outb[step % 2, top + edge : 1024] = value[edge:]
        store(step).start()
    store(6).wait()
    store(7).wait()
    for step in range(1, 8):
        clear(step).wait()


def update(cov, kc, kr, k5, cr, cc, inverse, scale):
    dma = pltpu.SemaphoreType.DMA
    vmem = pl.BlockSpec(memory_space=pltpu.VMEM)
    anywhere = pl.BlockSpec(memory_space=pl.ANY)
    return pl.pallas_call(
        update_kernel,
        name="update_lower",
        out_shape=jax.ShapeDtypeStruct((1024, 2048), F32),
        in_specs=[anywhere] * 3 + [vmem] * 5,
        out_specs=anywhere,
        scratch_shapes=[
            pltpu.VMEM((1024, 2048), F32), pltpu.VMEM((16, 128, PROMPTS), BF16), pltpu.VMEM((8, 64, 2048), BF16),
            pltpu.VMEM((2, 1024, 256), F32), pltpu.VMEM((64, 1024), F32), pltpu.VMEM((1024, 512), BF16), pltpu.VMEM((1024, PROMPTS), BF16),
            dma((8,)), dma((8,)), dma((8,)), dma((2,)), pltpu.VMEM((896, 256), F32), dma((8,)),
        ],
        compiler_params=pltpu.CompilerParams(vmem_limit_bytes=VMEM_LIMIT),
    )(cov, kc, cc, kr, k5, cr, inverse, scale)


def on_device(residual, positions, norm_gain, w_gate, w_up, covariance):
    kc, kr, k5, cr, cc, inverse, scale = panel(residual, positions, norm_gain, w_gate, w_up, covariance)
    kc = kc.reshape(16, 128, PROMPTS)
    kr = kr.reshape(16, 64, PROMPTS)
    cc = cc.reshape(8, 64, 2048)
    return update(covariance, kc, kr, k5, cr, cc, inverse, scale)


def solution(mesh):
    torus = Mesh(mesh.devices.reshape(4, 4, 4, 2), ("x", "y", "z", "k"))
    row, col = ("x", "y"), ("z", "k")
    placed = (P(row, None, col), P(row), P(col), P(col, row), P(col, row), P(row, col))
    return jax.shard_map(on_device, mesh=torus, in_specs=placed, out_specs=P(row, col), check_vma=False)
```

```python
import functools

import jax
import jax.numpy as jnp
from jax import lax
from jax.experimental import pallas as pl
from jax.experimental.pallas import tpu as pltpu
from jax.sharding import Mesh
from jax.sharding import PartitionSpec as P

MESH = pl.DeviceIdType.MESH
BF16 = jnp.bfloat16
F32 = jnp.float32
EPSILON = 1e-06
HIDDEN = 16384
WIDTH = 5120
PROMPTS = 1024
VMEM_LIMIT = 60 * 1024 * 1024
BASE = 16
LAG = 2


def here():
    return tuple(lax.axis_index(name) for name in ("x", "y", "z", "k"))


def moved(position, axis, step):
    place = list(position)
    size = 2 if axis == 3 else 4
    place[axis] = lax.rem(place[axis] + (step % size), size)
    return tuple(place)


def one_after_other(first, second):
    if first is not None:
        first()
    second()


def remote(src, dst, send, recv, target):
    return pltpu.make_async_remote_copy(
        src_ref=src, dst_ref=dst, send_sem=send, recv_sem=recv, device_id=target, device_id_type=MESH
    )


def greet(targets):
    barrier = pltpu.get_barrier_semaphore()
    for target in targets:
        pl.semaphore_signal(barrier, inc=1, device_id=target, device_id_type=MESH)
    pl.semaphore_wait(barrier, len(targets))


def when(condition, action):
    if condition is None:
        action()
    else:
        pl.when(condition)(action)


class PlaneGather:
    SENT = (
        (0, 0, 1, 1, None), (0, 0, 1, -1, None), (-1, 0, 1, 1, 0), (1, 0, 1, -1, 1),
        (0, 0, 0, 1, None), (-1, 0, 0, 1, None), (1, 0, 0, 1, None), (2, 0, 0, 1, None),
        (0, 0, 0, -1, None), (-1, 0, 0, -1, None), (1, 0, 0, -1, None), (2, 0, 0, -1, None),
        (0, -1, 0, 1, None), (-1, -1, 0, 1, None), (1, 1, 0, -1, None), (2, 1, 0, -1, None),
    )
    GOT = (
        (-1, 0, None), (1, 0, None), (2, 0, 0), (2, 0, 1),
        (0, -1, None), (-1, -1, None), (1, -1, None), (2, -1, None),
        (0, 1, None), (-1, 1, None), (1, 1, None), (2, 1, None),
        (0, 2, None), (-1, 2, None), (1, 2, None), (2, 2, None),
    )
    EVENTS = (
        ((0,), (2, 5, 9)), ((1,), (3, 6, 10)), ((4,), (12,)), ((8,), ()), ((2, 3), (7, 11)), ((5,), (13,)), ((10,), (14,)),
        ((9,), ()), ((6,), ()), ((11,), (15,)), ((7,), ()), ((12,), ()), ((13,), ()), ((14,), ()), ((15,), ()),
    )
    PLACES = tuple(((-1, 0), (1, 0), (0, -1), (0, 1), (2, 0), (-1, -1), (1, 1), (-1, 1), (1, -1), (2, 1), (2, -1), (0, 2), (-1, 2), (1, 2), (2, 2)))

    def __init__(self, buf, rows, send, recv, pos, only=None):
        self.buf, self.rows, self.send, self.recv, self.pos, self.only = buf, rows, send, recv, pos, only

    def block(self, half, first, second):
        dx, dy = (second, first) if half == 0 else (first, second)
        return lax.rem(self.pos[0] + dx % 4, 4), lax.rem(self.pos[1] + dy % 4, 4)

    def piece(self, half, first, second, part=None):
        size = self.rows // 2
        start = half * size
        if part is not None:
            size //= 2
            start += part * size
        bx, by = self.block(half, first, second)
        return self.buf.at[bx, by, pl.ds(start, size)]

    def cond(self, half, first, second):
        return None if self.only is None else self.only(*self.block(half, first, second))

    def copy(self, half, kind, first, second, axis, step, part=None):
        axis = axis if half == 0 else 1 - axis
        ref = self.piece(half, first, second, part)
        sender = self.send.at[half, kind] if self.only is not None else self.send.at[0 if kind < 4 else 1]
        return remote(ref, ref, sender, self.recv.at[half, kind], moved(self.pos, axis, step))

    def go(self, half, kind):
        first, second, axis, step, part = self.SENT[kind]
        when(self.cond(half, first, second), lambda: self.copy(half, kind, first, second, axis, step, part).start())

    def arrive(self, half, kind):
        first, second, part = self.GOT[kind]
        when(self.cond(half, first, second), lambda: self.copy(half, kind, first, second, 0, 1, part).wait_recv())

    def begin(self):
        for kind in (0, 1, 4, 8):
            for half in (0, 1):
                self.go(half, kind)

    def event(self, number, half):
        kinds, on = self.EVENTS[number]
        for kind in kinds:
            self.arrive(half, kind)
        for kind in on:
            self.go(half, kind)

    def finish(self):
        if self.only is None:
            for number, ref in ((0, self.buf.at[0, pl.ds(0, 3)]), (1, self.buf.at[pl.ds(0, 3)])):
                remote(ref, ref, self.send.at[number], self.recv.at[0, 0], moved(self.pos, 0, 1)).wait_send()
            return
        for half in (0, 1):
            for kind in range(16):
                first, second, axis, step, part = self.SENT[kind]
                when(
                    self.cond(half, first, second),
                    lambda: self.copy(half, kind, first, second, axis, step, part).wait_send(),
                )


class ColumnGather:
    def __init__(self, buf, send, recv, pos):
        self.buf, self.send, self.recv, self.pos = buf, send, recv, pos

    def piece(self, dz, dk=0, part=None):
        z, k = self.pos[2], self.pos[3]
        slot = lax.rem(z + dz % 4, 4) * 2 + lax.rem(k + dk, 2)
        if part is None:
            return self.buf.at[slot]
        return self.buf.at[slot, pl.ds(32 * part, 32)]

    SENT = {0: (0, 2, 1, None), 1: (0, 2, -1, None), 2: (-1, 2, 1, 0), 3: (1, 2, -1, 1),
            4: (0, 3, 1, None), 5: (-1, 3, 1, None), 6: (1, 3, 1, None), 7: (2, 3, 1, None)}
    GOT = {0: (-1, 0, None), 1: (1, 0, None), 2: (2, 0, 0), 3: (2, 0, 1),
           4: (0, 1, None), 5: (-1, 1, None), 6: (1, 1, None), 7: (2, 1, None)}

    def go(self, kind):
        dz, axis, step, part = self.SENT[kind]
        ref = self.piece(dz, 0, part)
        remote(ref, ref, self.send.at[kind], self.recv.at[kind], moved(self.pos, axis, step)).start()

    def arrive(self, kind):
        dz, dk, part = self.GOT[kind]
        ref = self.piece(dz, dk, part)
        remote(ref, ref, self.send.at[kind], self.recv.at[kind], moved(self.pos, 2, 1)).wait_recv()

    def begin(self):
        for kind in (0, 1, 4):
            self.go(kind)

    def middle(self):
        self.arrive(0)
        self.go(2)
        self.go(5)
        self.arrive(1)
        self.go(3)
        self.go(6)

    def end(self):
        self.arrive(2)
        self.arrive(3)
        self.go(7)
        for kind in (4, 5, 6, 7):
            self.arrive(kind)

    def finish(self):
        for kind in range(8):
            dz, axis, step, part = self.SENT[kind]
            ref = self.piece(dz, 0, part)
            remote(ref, ref, self.send.at[kind], self.recv.at[kind], moved(self.pos, axis, step)).wait_send()


def column_peers(pos):
    peers = []
    for dz in range(4):
        for dk in range(2):
            if dz or dk:
                peers.append(moved(moved(pos, 2, dz), 3, dk))
    return peers


def to_all_columns(buf, send, recv, pos):
    copies = []
    mine = pos[2] * 2 + pos[3]
    number = 0
    for dz in range(4):
        for dk in range(2):
            if dz == 0 and dk == 0:
                continue
            target = moved(moved(pos, 2, dz), 3, dk)
            out = remote(buf.at[mine], buf.at[mine], send.at[number], recv.at[number], target)
            origin = moved(moved(pos, 2, -dz), 3, -dk)
            slot = origin[2] * 2 + origin[3]
            into = remote(buf.at[slot], buf.at[slot], send.at[number], recv.at[number], target)
            copies.append((out, into))
            number += 1
    return copies


def to_axis(buf, send, recv, pos, axis):
    copies = []
    mine = pos[axis]
    for step in (1, 2, 3):
        target = moved(pos, axis, step)
        out = remote(buf.at[mine], buf.at[mine], send.at[step - 1], recv.at[step - 1], target)
        slot = moved(pos, axis, -step)[axis]
        into = remote(buf.at[slot], buf.at[slot], send.at[step - 1], recv.at[step - 1], target)
        copies.append((out, into))
    return copies


def exchange(copies):
    for out, _ in copies:
        out.start()
    for _, into in copies:
        into.wait_recv()


def split(value):
    high = value.astype(BF16)
    return high, (value - high.astype(F32)).astype(BF16)


def dot3(left, right, dims):
    lh, ll = split(left)
    rh, rl = split(right)
    dot = functools.partial(lax.dot_general, dimension_numbers=(dims, ((), ())), preferred_element_type=F32)
    return dot(lh, rh) + (dot(lh, rl) + dot(ll, rh))


def small_factor(work, extra):
    lane = lax.broadcasted_iota(jnp.int32, (1, 128), 1)

    def body(step, carry):
        start = pl.multiple_of(step * BASE, BASE)
        rows = work[pl.ds(start, BASE), :]
        turned = pltpu.roll(rows[:, :128], lax.rem(128 - start, 128), 1)
        entry = [[jnp.broadcast_to(turned[i : i + 1, j : j + 1], (1, 128)) for j in range(i + 1)] for i in range(BASE)]
        solved = []
        for j in range(BASE):
            inverse = lax.rsqrt(entry[j][j])
            row = rows[j : j + 1, :]
            for m in range(j):
                row = row - jnp.concatenate([entry[j][m]] * 2, axis=1) * solved[m]
            solved.append(row * jnp.concatenate([inverse] * 2, axis=1))
            for i in range(j + 1, BASE):
                entry[i][j] = entry[i][j] * inverse
            for i in range(j + 1, BASE):
                for m in range(j + 1, i + 1):
                    entry[i][m] = entry[i][m] - entry[i][j] * entry[m][j]
        block = jnp.concatenate(solved, axis=0)
        work[pl.ds(start, BASE), :] = block
        later = jnp.where(lane >= start + BASE, block[:, :128], 0.0)
        lh, ll = split(later)
        rh, rl = split(block)
        left = jnp.concatenate([lh, lh, ll], axis=0)
        right = jnp.concatenate([rh, rl, rh], axis=0)
        work[...] = work[...] - lax.dot_general(left, right, (((0,), (0,)), ((), ())), preferred_element_type=F32)
        for number, action in extra.items():
            pl.when(step == number)(action)
        return carry

    lax.fori_loop(0, 128 // BASE, body, 0)


def factor(aug, work, extras):
    eye = (lax.broadcasted_iota(jnp.int32, (128, 128), 0) == lax.broadcasted_iota(jnp.int32, (128, 128), 1)).astype(F32)
    for number in range(4):
        lo, hi = number * 128, (number + 1) * 128
        work[:, 0:128] = aug[lo:hi, lo:hi]
        work[:, 128:256] = eye
        small_factor(work, extras[number])
        inverse = work[:, 128:256]
        if hi < 512:
            right = dot3(inverse, aug[lo:hi, hi : 512 + lo], ((1,), (0,)))
            full = jnp.concatenate([right, inverse], axis=1)
            aug[lo:hi, hi : 512 + hi] = full
            ahead = right[:, 0 : 512 - hi]
            aug[hi:512, hi : 512 + hi] = aug[hi:512, hi : 512 + hi] - dot3(ahead, full, ((0,), (0,)))
        else:
            aug[lo:hi, 512 : 512 + lo] = dot3(inverse, aug[lo:hi, 512 : 512 + lo], ((1,), (0,)))
            aug[lo:hi, 512 + lo : 512 + hi] = inverse


def panel_kernel(
    residual_ref, positions_ref, gain_ref, gate_ref, up_ref, cov_ref, kc_out, kr_out, k5_out, cr_out, cc_out, inv_ref, scale_ref,
    kc, kr, k5, k5_scaled, cr, cc, first, jj, aug, work,
    xx, own_w, other_w, sel_w, squares, part, hop_out, hop_in, total, sum_y, sum_x, sum_c, cov_rows, cov_cols, cov_corner, tiles,
    local_sem, w_send, w_recv, sq_send, sq_recv, x_send, x_recv, sib_send, sib_recv,
    hop_send, hop_recv, sy_send, sy_recv, sx_send, sx_recv, sc_send, sc_recv, cc_send, cc_recv,
    kc_send, kc_recv, k5_send, k5_recv, cr_send, cr_recv, jj_send, jj_recv, f_send, f_recv, row_send, row_recv, out_sem, tile_send, tile_recv,
):
    pos = here()
    x, y, z, k = pos
    sibling = moved(pos, 3, 1)
    col = z * 2 + k
    plane = [moved(pos, axis, step) for axis in (0, 1) for step in (1, 2, 3)]
    barrier = pltpu.get_barrier_semaphore()
    peers = plane + column_peers(pos)
    for peer in peers:
        pl.semaphore_signal(barrier, inc=1, device_id=peer, device_id_type=MESH)

    weights = ((gate_ref, 0), (up_ref, 1))

    def swap(ref, index):
        return remote(ref, other_w.at[index], w_send.at[index], w_recv.at[index], sibling)

    def fetch(ref, index):
        return pltpu.make_async_copy(ref, own_w.at[index], local_sem.at[index])

    fetch_rows = pltpu.make_async_copy(cov_ref.at[pl.ds(0, 64)], cov_rows, local_sem.at[2])
    fetch_cols = pltpu.make_async_copy(cov_ref.at[:, pl.ds(0, 128)], cov_cols, local_sem.at[3])

    fetch_corner = pltpu.make_async_copy(cov_ref.at[pl.ds(0, 64), pl.ds(0, 128)], cov_corner, local_sem.at[4])
    fetch_corner.start()
    line_of = lax.broadcasted_iota(jnp.int32, (64, 64), 0)
    prompt_of = lax.broadcasted_iota(jnp.int32, (64, 64), 1)
    place = positions_ref[...].reshape(1, 64).astype(F32)
    place = jnp.sum(jnp.where(line_of == prompt_of, place, 0.0), axis=1, keepdims=True)
    token = lax.broadcasted_iota(jnp.int32, (64, 1024), 1) - 16 * lax.broadcasted_iota(jnp.int32, (64, 1024), 0)
    pick = (token.astype(F32) == place).astype(BF16)
    subject = jnp.dot(pick, residual_ref[...].reshape(1024, 640), preferred_element_type=F32)
    squared = subject * subject
    folded = squared[:, 0:128]
    for group in range(1, 5):
        folded = folded + squared[:, group * 128 : (group + 1) * 128]
    own_mass = jnp.sum(folded, axis=1, keepdims=True)
    mass_row = jnp.sum(jnp.where(line_of == prompt_of, own_mass, 0.0), axis=0, keepdims=True)
    squares[col] = jnp.broadcast_to(jnp.concatenate([mass_row, mass_row], axis=1), (8, 128))
    pl.semaphore_wait(barrier, len(peers))
    square_copies = to_all_columns(squares, sq_send, sq_recv, pos)
    for out, _ in square_copies:
        out.start()
    for ref, index in weights:
        fetch(ref, index).start()
        swap(ref, index).start()
    fetch_corner.wait()

    @pl.when(x < 2)
    def _():
        tiles[x, y] = cov_corner[...].astype(BF16)

    corner_tiles = PlaneGather(tiles, 64, tile_send, tile_recv, pos, only=lambda bx, by: bx < 2)
    corner_tiles.begin()

    def tile_events(numbers):
        for number in numbers:
            for half in (0, 1):
                corner_tiles.event(number, half)

    fetch_rows.start()
    fetch_cols.start()

    def select(source, core):
        def body(step, carry):
            first = pl.ds(pl.multiple_of(step * 128, 128), 128)
            second = pl.ds(pl.multiple_of(512 + step * 128, 128), 128)
            rows = pl.ds(pl.multiple_of(core * 640, 128), 640)
            for index, lanes in enumerate((first, second)):
                gate, up = source[0, :, lanes], source[1, :, lanes]

                @pl.when(k == 0)
                def _():
                    sel_w[step, rows, pl.ds(index * 128, 128)] = jnp.concatenate([gate[:, :64], up[:, :64]], axis=1)

                @pl.when(k == 1)
                def _():
                    sel_w[step, rows, pl.ds(index * 128, 128)] = jnp.concatenate([gate[:, 64:], up[:, 64:]], axis=1)

            return carry

        lax.fori_loop(0, 4, body, 0)

    for _, into in square_copies:
        into.wait_recv()
    everyone = squares[0]
    for member in range(1, 8):
        everyone = everyone + squares[member]
    everyone = jnp.sum(jnp.where(line_of == prompt_of, everyone[0:1, 0:64], 0.0), axis=1, keepdims=True)
    inverse_rms = lax.rsqrt(everyone / WIDTH + EPSILON)
    xx[k, x, y] = (subject * inverse_rms * gain_ref[...].reshape(1, 640)).astype(BF16)

    gather = PlaneGather(xx.at[k], 64, x_send, x_recv, pos)
    gather.begin()

    def to_sibling(half, number, first, second):
        ref = gather.piece(half, first, second)
        return remote(ref, ref, sib_send.at[0], sib_recv.at[half, number], sibling)

    def from_sibling(half, number, first, second):
        bx, by = gather.block(half, first, second)
        ref = xx.at[1 - k, bx, by, pl.ds(half * 32, 32)]
        return remote(ref, ref, sib_send.at[0], sib_recv.at[half, number], sibling)

    places = ((0, 0),) + PlaneGather.PLACES
    for half in (0, 1):
        to_sibling(half, 0, 0, 0).start()

    for ref, index in weights:
        fetch(ref, index).wait()
    select(own_w, k)

    def arrivals(numbers):
        for number in numbers:
            for half in (0, 1):
                gather.event(number, half)
                to_sibling(half, number + 1, *places[number + 1]).start()

    def siblings(numbers):
        for number in numbers:
            for half in (0, 1):
                from_sibling(half, number, *places[number]).wait_recv()

    def line(core, half, second):
        if half == 0:
            value = xx[core, lax.rem(x + second % 4, 4), :, 0:32, :]
        else:
            value = xx[core, :, lax.rem(y + second % 4, 4), 32:64, :]
        return value.reshape(128, 640)

    def product(chunk, dest):
        second = (0, -1, 1, 2)[chunk]
        value = None
        for core in (0, 1):
            left = jnp.concatenate([line(core, 0, second), line(core, 1, second)], axis=0)
            term = jnp.dot(left, sel_w[dest, core * 640 : core * 640 + 640], preferred_element_type=F32)
            value = term if value is None else value + term
        return value

    def dest(step):
        return lax.rem(z + step % 4, 4)

    def hop(chunk, kind, tile):
        target = moved(pos, 2, 1 if kind % 2 == 0 else -1)
        return remote(
            hop_out.at[chunk, kind, tile], hop_in.at[chunk, kind, tile],
            hop_send.at[0], hop_recv.at[chunk, kind + 6 * tile], target,
        )

    def lanes(tile):
        return slice(128 * tile, 128 * tile + 128)

    def multiply(chunk, hold):
        def send(kind, value):
            for tile in (0, 1):
                hop_out[chunk, kind, tile] = value[:, lanes(tile)].astype(BF16)
                if tile == 0 or not hold:
                    hop(chunk, kind, tile).start()

        value = product(chunk, dest(2))
        send(0, value[:128])
        send(1, value[128:])
        value = product(chunk, dest(1))
        send(2, value[128:])
        part[chunk, 0] = value[:128]
        value = product(chunk, dest(-1))
        send(3, value[:128])
        part[chunk, 1] = value[128:]
        value = product(chunk, dest(0))
        part[chunk, 2] = value[:128]
        part[chunk, 3] = value[128:]

    def release(chunk):
        for kind in range(4):
            hop(chunk, kind, 1).start()

    def join(chunk, tile):
        for kind in (0, 1):
            hop(chunk, kind, tile).wait_recv()
            value = part[chunk, kind, :, lanes(tile)] + hop_in[chunk, kind, tile].astype(F32)
            hop_out[chunk, 4 + kind, tile] = value.astype(BF16)
            hop(chunk, 4 + kind, tile).start()

    def finish(chunk, tile):
        second = (0, -1, 1, 2)[chunk]
        for half in (0, 1):
            kinds = (4, 3) if half == 0 else (2, 5)
            for kind in kinds:
                hop(chunk, kind, tile).wait_recv()
            value = part[chunk, 2 + half, :, lanes(tile)] + (
                hop_in[chunk, kinds[0], tile].astype(F32) + hop_in[chunk, kinds[1], tile].astype(F32)
            )
            turned = value.T
            gate, up = turned[:64], turned[64:]
            raw = gate / (1.0 + jnp.exp(-gate)) * up
            place = lax.rem((x if half == 0 else y) + second % 4, 4)
            total[pl.ds(64 * tile, 64), pl.ds(pl.multiple_of(half * 512 + place * 128, 128), 128)] = raw

    covs = PlaneGather(cc, 64, cc_send, cc_recv, pos, only=lambda bx, by: bx < 2)

    def cov_events(numbers):
        for number in numbers:
            for half in (0, 1):
                covs.event(number, half)

    arrivals((0, 1, 4))
    for ref, index in weights:
        swap(ref, index).wait_recv()
    select(other_w, 1 - k)
    arrivals((2, 3))
    siblings((0, 1, 2, 5))
    multiply(0, False)
    arrivals((5, 8, 10))
    tile_events((0, 1, 2, 3))
    siblings((3, 6, 9, 11))
    multiply(1, False)
    join(0, 0)
    arrivals((6, 7, 9))
    fetch_rows.wait()

    @pl.when(x < 2)
    def _():
        cc[x, y] = cov_rows[...].astype(BF16)

    covs.begin()
    tile_events((4, 5, 6, 7, 8))
    siblings((4, 7, 8, 10))
    join(0, 1)
    multiply(2, True)
    join(1, 0)
    arrivals((11, 12, 13, 14))
    siblings((12, 13, 14, 15))
    multiply(3, True)
    release(2)
    release(3)
    join(2, 0)
    join(3, 0)
    join(1, 1)
    tile_events(range(9, 15))
    cov_events((0, 1))
    for chunk in range(4):
        finish(chunk, 0)
    row = x * 4 + y

    @pl.when(row == 0)
    def _():
        first[0, 0] = total[0:64].astype(BF16)

    first_tile = PlaneGather(first, 64, f_send, f_recv, pos, only=lambda bx, by: (bx == 0) & (by == 0))
    first_tile.begin()

    def first_events(numbers):
        for number in numbers:
            first_tile.event(number, 0)
            first_tile.event(number, 1)

    join(2, 1)
    join(3, 1)
    jj[col] = tiles[...].reshape(512, 128).astype(F32).T[0:64].astype(BF16)
    corner = ColumnGather(jj, jj_send, jj_recv, pos)
    corner.begin()
    cov_events((2, 3, 4))
    fetch_cols.wait()
    cr[col] = cov_cols[...].T[0:64].astype(BF16)
    first_events((0, 1, 2, 3))
    finish(0, 1)
    first_events((4, 5, 6, 7, 8))
    finish(1, 1)
    finish(2, 1)
    corner.middle()
    finish(3, 1)
    raw = total[...]
    mass = jnp.sum(raw * raw, axis=0, keepdims=True)
    sum_y[y] = jnp.broadcast_to(mass, (8, PROMPTS))
    y_copies = to_axis(sum_y, sy_send, sy_recv, pos, 1)
    for out, _ in y_copies:
        out.start()
    kc[x, y] = raw.astype(BF16)
    keys = PlaneGather(kc, 128, kc_send, kc_recv, pos)
    keys.begin()
    first_events(range(9, 15))
    k5[col] = first[0, 0]
    first_keys = ColumnGather(k5, k5_send, k5_recv, pos)
    first_keys.begin()
    cov_events((5, 6, 9))
    for _, into in y_copies:
        into.wait_recv()
    sum_x[x] = sum_y[0] + sum_y[1] + sum_y[2] + sum_y[3]
    x_copies = to_axis(sum_x, sx_send, sx_recv, pos, 0)
    for out, _ in x_copies:
        out.start()
    corner.end()
    first_keys.middle()
    for _, into in x_copies:
        into.wait_recv()
    sum_c[col] = sum_x[0] + sum_x[1] + sum_x[2] + sum_x[3]
    c_copies = to_all_columns(sum_c, sc_send, sc_recv, pos)
    for out, _ in c_copies:
        out.start()

    source = lax.rem(row, 8)
    source_z = source // 2
    upper = row // 8
    away = lax.rem(z + 4 - source_z, 4)
    same = k == lax.rem(source, 2)

    def wave(number, kind, own=False):
        one, two = keys.block(0, *places[number]), keys.block(1, *places[number])
        bx = jnp.where(upper == 0, one[0], two[0])
        by = jnp.where(upper == 0, one[1], two[1])
        part = kind % 2
        dst = kr.at[bx, by, pl.ds(part * 32, 32)]
        src = kc.at[bx, by, pl.ds(pl.multiple_of(upper * 64 + part * 32, 32), 32)] if own else dst
        target = sibling if kind >= 2 else moved(pos, 2, 1 if kind == 0 else -1)
        return remote(src, dst, row_send.at[number, kind], row_recv.at[number, kind], target)

    def own_copy(number):
        one, two = keys.block(0, *places[number]), keys.block(1, *places[number])
        bx = jnp.where(upper == 0, one[0], two[0])
        by = jnp.where(upper == 0, one[1], two[1])
        return pltpu.make_async_copy(
            kc.at[bx, by, pl.ds(pl.multiple_of(upper * 64, 64), 64)], kr.at[bx, by], out_sem.at[number]
        )

    def relay(number):
        if number < 16:

            @pl.when(same & (away == 0))
            def _():
                for kind in (0, 1, 2, 3):
                    wave(number, kind, own=True).start()
                own_copy(number).start()

        for distance in (1, 2, 3):
            for kind, hops in ((0, distance), (1, 4 - distance)):
                block = number - LAG * hops
                if 0 <= block < 16:

                    @pl.when(same & (away == distance))
                    def _():
                        wave(block, kind).wait_recv()
                        if hops < 3:
                            wave(block, kind).start()
                        wave(block, kind + 2).start()

    def key_event(number):
        if number < 15:
            keys.event(number, 0)
            keys.event(number, 1)
        relay(number + 1)

    panel_rows = ColumnGather(cr, cr_send, cr_recv, pos)
    cov_events((7, 8))
    relay(0)
    key_event(0)
    first_keys.end()
    key_event(1)
    panel_rows.begin()
    for _, into in c_copies:
        into.wait_recv()
    mass = sum_c[0]
    for member in range(1, 8):
        mass = mass + sum_c[member]
    scale = lax.rsqrt(mass / HIDDEN + EPSILON) * (1.0 / 32.0)
    scale_ref[...] = scale * scale

    def save(number, source, target):
        return pltpu.make_async_copy(source, target, out_sem.at[16 + number])

    corner_raw = k5[...].reshape(512, PROMPTS).astype(F32)
    corner_keys = (corner_raw * scale[0:1]).astype(BF16)
    outer = lax.dot_general(corner_keys, corner_keys, (((1,), (1,)), ((), ())), preferred_element_type=F32)
    aug[:, 0:512] = jj[...].reshape(512, 512).astype(F32) + outer
    aug[:, 512:1024] = (
        lax.broadcasted_iota(jnp.int32, (512, 512), 0) == lax.broadcasted_iota(jnp.int32, (512, 512), 1)
    ).astype(F32)
    k5_scaled[...] = (corner_raw * (scale * scale)[0:1]).astype(BF16).reshape(8, 64, PROMPTS)
    save(0, k5_scaled, k5_out).start()
    beside = {
        2: 0, 3: 1, 4: 2, 5: 3, 6: 4, 7: 6, 8: 7, 9: 8, 10: 9, 11: 11, 12: 13, 13: 15, 14: 17, 15: 19, 16: 21, 17: 23, 18: 25, 19: 27, 20: 29,
    }
    extras = [{} for _ in range(4)]
    for number, step in beside.items():
        extras[step // 8][step % 8] = functools.partial(key_event, number)
    others = (
        (3, lambda: cov_events((10,))),
        (4, panel_rows.middle),
        (6, lambda: cov_events((11,))),
        (8, panel_rows.end),
        (8, lambda: cov_events((12,))),
        (10, lambda: cov_events((13,))),
        (12, lambda: cov_events((14,))),
        (14, lambda: save(1, cc, cc_out).start()),
        (20, lambda: save(3, cr, cr_out).start()),
        (22, lambda: save(2, kc, kc_out).start()),
    )
    for step, action in others:
        extras[step // 8][step % 8] = functools.partial(one_after_other, extras[step // 8].get(step % 8), action)
    factor(aug, work, extras)
    inv_ref[...] = aug[:, 512:1024]

    for number in range(16):

        @pl.when(k != lax.rem(source, 2))
        def _():
            wave(number, 2).wait_recv()
            wave(number, 3).wait_recv()

        @pl.when(same & (away == 0))
        def _():
            for kind in range(4):
                wave(number, kind, own=True).wait_send()
            own_copy(number).wait()

        for distance in (1, 2, 3):

            @pl.when(same & (away == distance))
            def _():
                for kind, hops in ((0, distance), (1, 4 - distance)):
                    if hops < 3:
                        wave(number, kind).wait_send()
                    wave(number, kind + 2).wait_send()

    first_tile.finish()
    keys.finish()
    panel_rows.finish()
    first_keys.finish()
    corner.finish()
    corner_tiles.finish()
    save(4, kr, kr_out).start()
    for ref, index in weights:
        swap(ref, index).wait_send()
    for copies in (square_copies, y_copies, x_copies, c_copies):
        for out, _ in copies:
            out.wait_send()
    gather.finish()
    covs.finish()
    remote(xx.at[k], xx.at[k], sib_send.at[0], sib_recv.at[0, 0], sibling).wait_send()
    remote(hop_out, hop_in, hop_send.at[0], hop_recv.at[0, 0], sibling).wait_send()
    save(0, k5_scaled, k5_out).wait()
    save(1, cc, cc_out).wait()
    save(2, kc, kc_out).wait()
    save(3, cr, cr_out).wait()
    save(4, kr, kr_out).wait()


def panel(residual, positions, gain, w_gate, w_up, cov):
    dma = pltpu.SemaphoreType.DMA
    vmem = pl.BlockSpec(memory_space=pltpu.VMEM)
    anywhere = pl.BlockSpec(memory_space=pl.ANY)
    spread = (
        ((4, 4, 128, PROMPTS), BF16),
        ((4, 4, 64, PROMPTS), BF16),
        ((8, 64, PROMPTS), BF16),
        ((8, 64, 1024), BF16),
        ((2, 4, 64, 2048), BF16),
    )
    return pl.pallas_call(
        panel_kernel,
        name="keys_and_panel",
        out_shape=tuple(jax.ShapeDtypeStruct(*one) for one in spread)
        + (jax.ShapeDtypeStruct((512, 512), F32), jax.ShapeDtypeStruct((8, PROMPTS), F32)),
        in_specs=[vmem] * 3 + [anywhere] * 3,
        out_specs=(anywhere,) * 5 + (vmem,) * 2,
        scratch_shapes=[
            pltpu.VMEM(*spread[0]), pltpu.VMEM(*spread[1]), pltpu.VMEM(*spread[2]), pltpu.VMEM(*spread[2]),
            pltpu.VMEM(*spread[3]), pltpu.VMEM(*spread[4]),
            pltpu.VMEM((1, 1, 64, PROMPTS), BF16),
            pltpu.VMEM((8, 64, 512), BF16),
            pltpu.VMEM((512, 1024), F32),
            pltpu.VMEM((128, 256), F32),
            pltpu.VMEM((2, 4, 4, 64, 640), BF16),
            pltpu.VMEM((2, 640, 1024), BF16),
            pltpu.VMEM((2, 640, 1024), BF16),
            pltpu.VMEM((4, 1280, 256), BF16),
            pltpu.VMEM((8, 8, 128), F32),
            pltpu.VMEM((4, 4, 128, 256), F32),
            pltpu.VMEM((4, 6, 2, 128, 128), BF16),
            pltpu.VMEM((4, 6, 2, 128, 128), BF16),
            pltpu.VMEM((128, PROMPTS), F32),
            pltpu.VMEM((4, 8, PROMPTS), F32),
            pltpu.VMEM((4, 8, PROMPTS), F32),
            pltpu.VMEM((8, 8, PROMPTS), F32),
            pltpu.VMEM((64, 2048), F32),
            pltpu.VMEM((1024, 128), F32),
            pltpu.VMEM((64, 128), F32),
            pltpu.VMEM((2, 4, 64, 128), BF16),
            dma((5,)), dma((2,)), dma((2,)), dma((7,)), dma((7,)), dma((2,)), dma((2, 16)), dma((1,)), dma((2, 16)),
            dma((1,)), dma((4, 12)), dma((3,)), dma((3,)), dma((3,)), dma((3,)), dma((7,)), dma((7,)), dma((2, 16)), dma((2, 16)),
            dma((2,)), dma((2, 16)), dma((8,)), dma((8,)), dma((8,)), dma((8,)), dma((8,)), dma((8,)), dma((2, 16)), dma((2, 16)),
            dma((16, 4)), dma((16, 4)), dma((21,)), dma((2, 16)), dma((2, 16)),
        ],
        compiler_params=pltpu.CompilerParams(collective_id=0, has_side_effects=True, vmem_limit_bytes=VMEM_LIMIT),
    )(residual, positions, gain, w_gate, w_up, cov)


def update_kernel(
    cov_ref, kc_ref, cc_ref, kr_ref, k5_ref, cr_ref, inv_ref, scale_ref, out_ref,
    covb, kcb, ccb, outb, panel, weights, rows, cov_sem, kc_sem, cc_sem, out_sem, zeros, zero_sem,
):
    x, y, z, k = here()
    row = x * 4 + y
    col = z * 2 + k
    nt = (((1,), (1,)), ((), ()))
    nn = (((1,), (0,)), ((), ()))
    tn = (((0,), (0,)), ((), ()))
    dot = functools.partial(lax.dot_general, preferred_element_type=F32)

    def load_cov(step):
        area = (pl.ds(step * 128, 1024 - step * 128), pl.ds(step * 256, 256))
        return pltpu.make_async_copy(cov_ref.at[area], covb.at[area], cov_sem.at[step])

    def load_kc(step):
        area = pl.ds(step * 2, 2)
        return pltpu.make_async_copy(kc_ref.at[area], kcb.at[area], kc_sem.at[step])

    def load_cc(step):
        area = (slice(None), slice(None), pl.ds(step * 256, 256))
        return pltpu.make_async_copy(cc_ref.at[area], ccb.at[area], cc_sem.at[step])

    def store(step):
        top = step * 128
        source = outb.at[step % 2, pl.ds(top, 1024 - top)]
        return pltpu.make_async_copy(source, out_ref.at[pl.ds(top, 1024 - top), pl.ds(step * 256, 256)], out_sem.at[step % 2])

    def clear(step):
        top = step * 128
        return pltpu.make_async_copy(zeros.at[pl.ds(0, top)], out_ref.at[pl.ds(0, top), pl.ds(step * 256, 256)], zero_sem.at[step])

    for step in range(8):
        load_kc(step).start()
        load_cc(step).start()
        load_cov(step).start()
    zeros[...] = jnp.zeros_like(zeros)
    for step in range(1, 8):
        clear(step).start()
    inverse = inv_ref[...]
    inverse_high = inverse.astype(BF16)
    first = k5_ref[...].reshape(512, PROMPTS)
    raw_rows = kr_ref[...].reshape(1024, PROMPTS)
    matrix_rows = cr_ref[...].reshape(512, 1024).astype(F32) + dot(first, raw_rows, nt)
    high, low = split(matrix_rows)
    panel_rows = dot(inverse_high, high, nn).astype(BF16)
    weights[...] = dot(panel_rows, inverse_high, tn).astype(BF16)
    own_high, own_low = split(inv_ref[pl.ds(pl.multiple_of(col * 64, 64), 64), :])
    panel[...] = dot(own_high, high, nn) + (dot(own_low, high, nn) + dot(own_high, low, nn))
    rows[...] = (raw_rows.astype(F32) * scale_ref[0:1] - dot(weights[...], first, nn)).astype(BF16)
    for step in range(8):
        top = step * 128
        height = 1024 - top
        load_kc(step).wait()
        load_cc(step).wait()
        load_cov(step).wait()
        if step >= 2:
            store(step - 2).wait()
        cols = kcb[2 * step : 2 * step + 2].reshape(256, PROMPTS)
        panel_cols = ccb[:, :, step * 256 : (step + 1) * 256].reshape(512, 256)
        value = covb[top:1024, step * 256 : (step + 1) * 256] + (dot(rows[top:], cols, nt) - dot(weights[top:], panel_cols, nn))
        if step == 0:
            value = jnp.concatenate([panel[...].T, value[:, 64:]], axis=1)
        edge = min(256, height)
        i = lax.broadcasted_iota(jnp.int32, (edge, 256), 0) + top
        j = lax.broadcasted_iota(jnp.int32, (edge, 256), 1) + step * 256
        row_global = (i // 64 * 16 + row) * 64 + i % 64
        col_global = (j // 64 * 8 + col) * 64 + j % 64
        outb[step % 2, top : top + edge] = jnp.where(row_global >= col_global, value[:edge], 0.0)
        if edge < height:
            outb[step % 2, top + edge : 1024] = value[edge:]
        store(step).start()
    store(6).wait()
    store(7).wait()
    for step in range(1, 8):
        clear(step).wait()


def update(cov, kc, kr, k5, cr, cc, inverse, scale):
    dma = pltpu.SemaphoreType.DMA
    vmem = pl.BlockSpec(memory_space=pltpu.VMEM)
    anywhere = pl.BlockSpec(memory_space=pl.ANY)
    return pl.pallas_call(
        update_kernel,
        name="update_lower",
        out_shape=jax.ShapeDtypeStruct((1024, 2048), F32),
        in_specs=[anywhere] * 3 + [vmem] * 5,
        out_specs=anywhere,
        scratch_shapes=[
            pltpu.VMEM((1024, 2048), F32), pltpu.VMEM((16, 128, PROMPTS), BF16), pltpu.VMEM((8, 64, 2048), BF16),
            pltpu.VMEM((2, 1024, 256), F32), pltpu.VMEM((64, 1024), F32), pltpu.VMEM((1024, 512), BF16), pltpu.VMEM((1024, PROMPTS), BF16),
            dma((8,)), dma((8,)), dma((8,)), dma((2,)), pltpu.VMEM((896, 256), F32), dma((8,)),
        ],
        compiler_params=pltpu.CompilerParams(vmem_limit_bytes=VMEM_LIMIT),
    )(cov, kc, cc, kr, k5, cr, inverse, scale)


def on_device(residual, positions, norm_gain, w_gate, w_up, covariance):
    kc, kr, k5, cr, cc, inverse, scale = panel(residual, positions, norm_gain, w_gate, w_up, covariance)
    kc = kc.reshape(16, 128, PROMPTS)
    kr = kr.reshape(16, 64, PROMPTS)
    cc = cc.reshape(8, 64, 2048)
    return update(covariance, kc, kr, k5, cr, cc, inverse, scale)


def solution(mesh):
    torus = Mesh(mesh.devices.reshape(4, 4, 4, 2), ("x", "y", "z", "k"))
    row, col = ("x", "y"), ("z", "k")
    placed = (P(row, None, col), P(row), P(col), P(col, row), P(col, row), P(row, col))
    return jax.shard_map(on_device, mesh=torus, in_specs=placed, out_specs=P(row, col), check_vma=False)
```

```python
import functools

import jax
import jax.numpy as jnp
from jax import lax
from jax.experimental import pallas as pl
from jax.experimental.pallas import tpu as pltpu
from jax.sharding import Mesh
from jax.sharding import PartitionSpec as P

MESH = pl.DeviceIdType.MESH
BF16 = jnp.bfloat16
F32 = jnp.float32
EPSILON = 1e-06
HIDDEN = 16384
WIDTH = 5120
PROMPTS = 1024
VMEM_LIMIT = 60 * 1024 * 1024
BASE = 16
LAG = 3


def here():
    return tuple(lax.axis_index(name) for name in ("x", "y", "z", "k"))


def moved(position, axis, step):
    place = list(position)
    size = 2 if axis == 3 else 4
    place[axis] = lax.rem(place[axis] + (step % size), size)
    return tuple(place)


def one_after_other(first, second):
    if first is not None:
        first()
    second()


def remote(src, dst, send, recv, target):
    return pltpu.make_async_remote_copy(
        src_ref=src, dst_ref=dst, send_sem=send, recv_sem=recv, device_id=target, device_id_type=MESH
    )


def greet(targets):
    barrier = pltpu.get_barrier_semaphore()
    for target in targets:
        pl.semaphore_signal(barrier, inc=1, device_id=target, device_id_type=MESH)
    pl.semaphore_wait(barrier, len(targets))


def when(condition, action):
    if condition is None:
        action()
    else:
        pl.when(condition)(action)


class PlaneGather:
    SENT = (
        (0, 0, 1, 1, None), (0, 0, 1, -1, None), (-1, 0, 1, 1, 0), (1, 0, 1, -1, 1),
        (0, 0, 0, 1, None), (-1, 0, 0, 1, None), (1, 0, 0, 1, None), (2, 0, 0, 1, None),
        (0, 0, 0, -1, None), (-1, 0, 0, -1, None), (1, 0, 0, -1, None), (2, 0, 0, -1, None),
        (0, -1, 0, 1, None), (-1, -1, 0, 1, None), (1, 1, 0, -1, None), (2, 1, 0, -1, None),
    )
    GOT = (
        (-1, 0, None), (1, 0, None), (2, 0, 0), (2, 0, 1),
        (0, -1, None), (-1, -1, None), (1, -1, None), (2, -1, None),
        (0, 1, None), (-1, 1, None), (1, 1, None), (2, 1, None),
        (0, 2, None), (-1, 2, None), (1, 2, None), (2, 2, None),
    )
    EVENTS = (
        ((0,), (2, 5, 9)), ((1,), (3, 6, 10)), ((4,), (12,)), ((8,), ()), ((2, 3), (7, 11)), ((5,), (13,)), ((10,), (14,)),
        ((9,), ()), ((6,), ()), ((11,), (15,)), ((7,), ()), ((12,), ()), ((13,), ()), ((14,), ()), ((15,), ()),
    )
    PLACES = tuple(((-1, 0), (1, 0), (0, -1), (0, 1), (2, 0), (-1, -1), (1, 1), (-1, 1), (1, -1), (2, 1), (2, -1), (0, 2), (-1, 2), (1, 2), (2, 2)))

    def __init__(self, buf, rows, send, recv, pos, only=None):
        self.buf, self.rows, self.send, self.recv, self.pos, self.only = buf, rows, send, recv, pos, only

    def block(self, half, first, second):
        dx, dy = (second, first) if half == 0 else (first, second)
        return lax.rem(self.pos[0] + dx % 4, 4), lax.rem(self.pos[1] + dy % 4, 4)

    def piece(self, half, first, second, part=None):
        size = self.rows // 2
        start = half * size
        if part is not None:
            size //= 2
            start += part * size
        bx, by = self.block(half, first, second)
        return self.buf.at[bx, by, pl.ds(start, size)]

    def cond(self, half, first, second):
        return None if self.only is None else self.only(*self.block(half, first, second))

    def copy(self, half, kind, first, second, axis, step, part=None):
        axis = axis if half == 0 else 1 - axis
        ref = self.piece(half, first, second, part)
        sender = self.send.at[half, kind] if self.only is not None else self.send.at[0 if kind < 4 else 1]
        return remote(ref, ref, sender, self.recv.at[half, kind], moved(self.pos, axis, step))

    def go(self, half, kind):
        first, second, axis, step, part = self.SENT[kind]
        when(self.cond(half, first, second), lambda: self.copy(half, kind, first, second, axis, step, part).start())

    def arrive(self, half, kind):
        first, second, part = self.GOT[kind]
        when(self.cond(half, first, second), lambda: self.copy(half, kind, first, second, 0, 1, part).wait_recv())

    def begin(self):
        for kind in (0, 1, 4, 8):
            for half in (0, 1):
                self.go(half, kind)

    def event(self, number, half):
        kinds, on = self.EVENTS[number]
        for kind in kinds:
            self.arrive(half, kind)
        for kind in on:
            self.go(half, kind)

    def finish(self):
        if self.only is None:
            for number, ref in ((0, self.buf.at[0, pl.ds(0, 3)]), (1, self.buf.at[pl.ds(0, 3)])):
                remote(ref, ref, self.send.at[number], self.recv.at[0, 0], moved(self.pos, 0, 1)).wait_send()
            return
        for half in (0, 1):
            for kind in range(16):
                first, second, axis, step, part = self.SENT[kind]
                when(
                    self.cond(half, first, second),
                    lambda: self.copy(half, kind, first, second, axis, step, part).wait_send(),
                )


class ColumnGather:
    def __init__(self, buf, send, recv, pos):
        self.buf, self.send, self.recv, self.pos = buf, send, recv, pos

    def piece(self, dz, dk=0, part=None):
        z, k = self.pos[2], self.pos[3]
        slot = lax.rem(z + dz % 4, 4) * 2 + lax.rem(k + dk, 2)
        if part is None:
            return self.buf.at[slot]
        return self.buf.at[slot, pl.ds(32 * part, 32)]

    SENT = {0: (0, 2, 1, None), 1: (0, 2, -1, None), 2: (-1, 2, 1, 0), 3: (1, 2, -1, 1),
            4: (0, 3, 1, None), 5: (-1, 3, 1, None), 6: (1, 3, 1, None), 7: (2, 3, 1, None)}
    GOT = {0: (-1, 0, None), 1: (1, 0, None), 2: (2, 0, 0), 3: (2, 0, 1),
           4: (0, 1, None), 5: (-1, 1, None), 6: (1, 1, None), 7: (2, 1, None)}

    def go(self, kind):
        dz, axis, step, part = self.SENT[kind]
        ref = self.piece(dz, 0, part)
        remote(ref, ref, self.send.at[kind], self.recv.at[kind], moved(self.pos, axis, step)).start()

    def arrive(self, kind):
        dz, dk, part = self.GOT[kind]
        ref = self.piece(dz, dk, part)
        remote(ref, ref, self.send.at[kind], self.recv.at[kind], moved(self.pos, 2, 1)).wait_recv()

    def begin(self):
        for kind in (0, 1, 4):
            self.go(kind)

    def middle(self):
        self.arrive(0)
        self.go(2)
        self.go(5)
        self.arrive(1)
        self.go(3)
        self.go(6)

    def end(self):
        self.arrive(2)
        self.arrive(3)
        self.go(7)
        for kind in (4, 5, 6, 7):
            self.arrive(kind)

    def finish(self):
        for kind in range(8):
            dz, axis, step, part = self.SENT[kind]
            ref = self.piece(dz, 0, part)
            remote(ref, ref, self.send.at[kind], self.recv.at[kind], moved(self.pos, axis, step)).wait_send()


def column_peers(pos):
    peers = []
    for dz in range(4):
        for dk in range(2):
            if dz or dk:
                peers.append(moved(moved(pos, 2, dz), 3, dk))
    return peers


def to_all_columns(buf, send, recv, pos):
    copies = []
    mine = pos[2] * 2 + pos[3]
    number = 0
    for dz in range(4):
        for dk in range(2):
            if dz == 0 and dk == 0:
                continue
            target = moved(moved(pos, 2, dz), 3, dk)
            out = remote(buf.at[mine], buf.at[mine], send.at[number], recv.at[number], target)
            origin = moved(moved(pos, 2, -dz), 3, -dk)
            slot = origin[2] * 2 + origin[3]
            into = remote(buf.at[slot], buf.at[slot], send.at[number], recv.at[number], target)
            copies.append((out, into))
            number += 1
    return copies


def to_axis(buf, send, recv, pos, axis):
    copies = []
    mine = pos[axis]
    for step in (1, 2, 3):
        target = moved(pos, axis, step)
        out = remote(buf.at[mine], buf.at[mine], send.at[step - 1], recv.at[step - 1], target)
        slot = moved(pos, axis, -step)[axis]
        into = remote(buf.at[slot], buf.at[slot], send.at[step - 1], recv.at[step - 1], target)
        copies.append((out, into))
    return copies


def exchange(copies):
    for out, _ in copies:
        out.start()
    for _, into in copies:
        into.wait_recv()


def split(value):
    high = value.astype(BF16)
    return high, (value - high.astype(F32)).astype(BF16)


def dot3(left, right, dims):
    lh, ll = split(left)
    rh, rl = split(right)
    dot = functools.partial(lax.dot_general, dimension_numbers=(dims, ((), ())), preferred_element_type=F32)
    return dot(lh, rh) + (dot(lh, rl) + dot(ll, rh))


def small_factor(work, extra):
    lane = lax.broadcasted_iota(jnp.int32, (1, 128), 1)

    def body(step, carry):
        start = pl.multiple_of(step * BASE, BASE)
        rows = work[pl.ds(start, BASE), :]
        turned = pltpu.roll(rows[:, :128], lax.rem(128 - start, 128), 1)
        entry = [[jnp.broadcast_to(turned[i : i + 1, j : j + 1], (1, 128)) for j in range(i + 1)] for i in range(BASE)]
        solved = []
        for j in range(BASE):
            inverse = lax.rsqrt(entry[j][j])
            row = rows[j : j + 1, :]
            for m in range(j):
                row = row - jnp.concatenate([entry[j][m]] * 2, axis=1) * solved[m]
            solved.append(row * jnp.concatenate([inverse] * 2, axis=1))
            for i in range(j + 1, BASE):
                entry[i][j] = entry[i][j] * inverse
            for i in range(j + 1, BASE):
                for m in range(j + 1, i + 1):
                    entry[i][m] = entry[i][m] - entry[i][j] * entry[m][j]
        block = jnp.concatenate(solved, axis=0)
        work[pl.ds(start, BASE), :] = block
        later = jnp.where(lane >= start + BASE, block[:, :128], 0.0)
        lh, ll = split(later)
        rh, rl = split(block)
        left = jnp.concatenate([lh, lh, ll], axis=0)
        right = jnp.concatenate([rh, rl, rh], axis=0)
        work[...] = work[...] - lax.dot_general(left, right, (((0,), (0,)), ((), ())), preferred_element_type=F32)
        for number, action in extra.items():
            pl.when(step == number)(action)
        return carry

    lax.fori_loop(0, 128 // BASE, body, 0)


def factor(aug, work, extras):
    eye = (lax.broadcasted_iota(jnp.int32, (128, 128), 0) == lax.broadcasted_iota(jnp.int32, (128, 128), 1)).astype(F32)
    for number in range(4):
        lo, hi = number * 128, (number + 1) * 128
        work[:, 0:128] = aug[lo:hi, lo:hi]
        work[:, 128:256] = eye
        small_factor(work, extras[number])
        inverse = work[:, 128:256]
        if hi < 512:
            right = dot3(inverse, aug[lo:hi, hi : 512 + lo], ((1,), (0,)))
            full = jnp.concatenate([right, inverse], axis=1)
            aug[lo:hi, hi : 512 + hi] = full
            ahead = right[:, 0 : 512 - hi]
            aug[hi:512, hi : 512 + hi] = aug[hi:512, hi : 512 + hi] - dot3(ahead, full, ((0,), (0,)))
        else:
            aug[lo:hi, 512 : 512 + lo] = dot3(inverse, aug[lo:hi, 512 : 512 + lo], ((1,), (0,)))
            aug[lo:hi, 512 + lo : 512 + hi] = inverse


def panel_kernel(
    residual_ref, positions_ref, gain_ref, gate_ref, up_ref, cov_ref, kc_out, kr_out, k5_out, cr_out, cc_out, inv_ref, scale_ref,
    kc, kr, k5, k5_scaled, cr, cc, first, jj, aug, work,
    xx, own_w, other_w, sel_w, squares, part, hop_out, hop_in, total, sum_y, sum_x, sum_c, cov_rows, cov_cols, cov_corner, tiles,
    local_sem, w_send, w_recv, sq_send, sq_recv, x_send, x_recv, sib_send, sib_recv,
    hop_send, hop_recv, sy_send, sy_recv, sx_send, sx_recv, sc_send, sc_recv, cc_send, cc_recv,
    kc_send, kc_recv, k5_send, k5_recv, cr_send, cr_recv, jj_send, jj_recv, f_send, f_recv, row_send, row_recv, out_sem, tile_send, tile_recv,
):
    pos = here()
    x, y, z, k = pos
    sibling = moved(pos, 3, 1)
    col = z * 2 + k
    plane = [moved(pos, axis, step) for axis in (0, 1) for step in (1, 2, 3)]
    barrier = pltpu.get_barrier_semaphore()
    peers = plane + column_peers(pos)
    for peer in peers:
        pl.semaphore_signal(barrier, inc=1, device_id=peer, device_id_type=MESH)

    weights = ((gate_ref, 0), (up_ref, 1))

    def swap(ref, index):
        return remote(ref, other_w.at[index], w_send.at[index], w_recv.at[index], sibling)

    def fetch(ref, index):
        return pltpu.make_async_copy(ref, own_w.at[index], local_sem.at[index])

    fetch_rows = pltpu.make_async_copy(cov_ref.at[pl.ds(0, 64)], cov_rows, local_sem.at[2])
    fetch_cols = pltpu.make_async_copy(cov_ref.at[:, pl.ds(0, 128)], cov_cols, local_sem.at[3])

    fetch_corner = pltpu.make_async_copy(cov_ref.at[pl.ds(0, 64), pl.ds(0, 128)], cov_corner, local_sem.at[4])
    fetch_corner.start()
    line_of = lax.broadcasted_iota(jnp.int32, (64, 64), 0)
    prompt_of = lax.broadcasted_iota(jnp.int32, (64, 64), 1)
    place = positions_ref[...].reshape(1, 64).astype(F32)
    place = jnp.sum(jnp.where(line_of == prompt_of, place, 0.0), axis=1, keepdims=True)
    token = lax.broadcasted_iota(jnp.int32, (64, 1024), 1) - 16 * lax.broadcasted_iota(jnp.int32, (64, 1024), 0)
    pick = (token.astype(F32) == place).astype(BF16)
    subject = jnp.dot(pick, residual_ref[...].reshape(1024, 640), preferred_element_type=F32)
    squared = subject * subject
    folded = squared[:, 0:128]
    for group in range(1, 5):
        folded = folded + squared[:, group * 128 : (group + 1) * 128]
    own_mass = jnp.sum(folded, axis=1, keepdims=True)
    mass_row = jnp.sum(jnp.where(line_of == prompt_of, own_mass, 0.0), axis=0, keepdims=True)
    squares[col] = jnp.broadcast_to(jnp.concatenate([mass_row, mass_row], axis=1), (8, 128))
    pl.semaphore_wait(barrier, len(peers))
    square_copies = to_all_columns(squares, sq_send, sq_recv, pos)
    for out, _ in square_copies:
        out.start()
    for ref, index in weights:
        fetch(ref, index).start()
        swap(ref, index).start()
    fetch_corner.wait()

    @pl.when(x < 2)
    def _():
        tiles[x, y] = cov_corner[...].astype(BF16)

    corner_tiles = PlaneGather(tiles, 64, tile_send, tile_recv, pos, only=lambda bx, by: bx < 2)
    corner_tiles.begin()

    def tile_events(numbers):
        for number in numbers:
            for half in (0, 1):
                corner_tiles.event(number, half)

    fetch_rows.start()
    fetch_cols.start()

    def select(source, core):
        def body(step, carry):
            first = pl.ds(pl.multiple_of(step * 128, 128), 128)
            second = pl.ds(pl.multiple_of(512 + step * 128, 128), 128)
            rows = pl.ds(pl.multiple_of(core * 640, 128), 640)
            for index, lanes in enumerate((first, second)):
                gate, up = source[0, :, lanes], source[1, :, lanes]

                @pl.when(k == 0)
                def _():
                    sel_w[step, rows, pl.ds(index * 128, 128)] = jnp.concatenate([gate[:, :64], up[:, :64]], axis=1)

                @pl.when(k == 1)
                def _():
                    sel_w[step, rows, pl.ds(index * 128, 128)] = jnp.concatenate([gate[:, 64:], up[:, 64:]], axis=1)

            return carry

        lax.fori_loop(0, 4, body, 0)

    for _, into in square_copies:
        into.wait_recv()
    everyone = squares[0]
    for member in range(1, 8):
        everyone = everyone + squares[member]
    everyone = jnp.sum(jnp.where(line_of == prompt_of, everyone[0:1, 0:64], 0.0), axis=1, keepdims=True)
    inverse_rms = lax.rsqrt(everyone / WIDTH + EPSILON)
    xx[k, x, y] = (subject * inverse_rms * gain_ref[...].reshape(1, 640)).astype(BF16)

    gather = PlaneGather(xx.at[k], 64, x_send, x_recv, pos)
    gather.begin()

    def to_sibling(half, number, first, second):
        ref = gather.piece(half, first, second)
        return remote(ref, ref, sib_send.at[0], sib_recv.at[half, number], sibling)

    def from_sibling(half, number, first, second):
        bx, by = gather.block(half, first, second)
        ref = xx.at[1 - k, bx, by, pl.ds(half * 32, 32)]
        return remote(ref, ref, sib_send.at[0], sib_recv.at[half, number], sibling)

    places = ((0, 0),) + PlaneGather.PLACES
    for half in (0, 1):
        to_sibling(half, 0, 0, 0).start()

    for ref, index in weights:
        fetch(ref, index).wait()
    select(own_w, k)

    def arrivals(numbers):
        for number in numbers:
            for half in (0, 1):
                gather.event(number, half)
                to_sibling(half, number + 1, *places[number + 1]).start()

    def siblings(numbers):
        for number in numbers:
            for half in (0, 1):
                from_sibling(half, number, *places[number]).wait_recv()

    def line(core, half, second):
        if half == 0:
            value = xx[core, lax.rem(x + second % 4, 4), :, 0:32, :]
        else:
            value = xx[core, :, lax.rem(y + second % 4, 4), 32:64, :]
        return value.reshape(128, 640)

    def product(chunk, dest):
        second = (0, -1, 1, 2)[chunk]
        value = None
        for core in (0, 1):
            left = jnp.concatenate([line(core, 0, second), line(core, 1, second)], axis=0)
            term = jnp.dot(left, sel_w[dest, core * 640 : core * 640 + 640], preferred_element_type=F32)
            value = term if value is None else value + term
        return value

    def dest(step):
        return lax.rem(z + step % 4, 4)

    def hop(chunk, kind, tile):
        target = moved(pos, 2, 1 if kind % 2 == 0 else -1)
        return remote(
            hop_out.at[chunk, kind, tile], hop_in.at[chunk, kind, tile],
            hop_send.at[0], hop_recv.at[chunk, kind + 6 * tile], target,
        )

    def lanes(tile):
        return slice(128 * tile, 128 * tile + 128)

    def multiply(chunk, hold):
        def send(kind, value):
            for tile in (0, 1):
                hop_out[chunk, kind, tile] = value[:, lanes(tile)].astype(BF16)
                if tile == 0 or not hold:
                    hop(chunk, kind, tile).start()

        value = product(chunk, dest(2))
        send(0, value[:128])
        send(1, value[128:])
        value = product(chunk, dest(1))
        send(2, value[128:])
        part[chunk, 0] = value[:128]
        value = product(chunk, dest(-1))
        send(3, value[:128])
        part[chunk, 1] = value[128:]
        value = product(chunk, dest(0))
        part[chunk, 2] = value[:128]
        part[chunk, 3] = value[128:]

    def release(chunk):
        for kind in range(4):
            hop(chunk, kind, 1).start()

    def join(chunk, tile):
        for kind in (0, 1):
            hop(chunk, kind, tile).wait_recv()
            value = part[chunk, kind, :, lanes(tile)] + hop_in[chunk, kind, tile].astype(F32)
            hop_out[chunk, 4 + kind, tile] = value.astype(BF16)
            hop(chunk, 4 + kind, tile).start()

    def finish(chunk, tile):
        second = (0, -1, 1, 2)[chunk]
        for half in (0, 1):
            kinds = (4, 3) if half == 0 else (2, 5)
            for kind in kinds:
                hop(chunk, kind, tile).wait_recv()
            value = part[chunk, 2 + half, :, lanes(tile)] + (
                hop_in[chunk, kinds[0], tile].astype(F32) + hop_in[chunk, kinds[1], tile].astype(F32)
            )
            turned = value.T
            gate, up = turned[:64], turned[64:]
            raw = gate / (1.0 + jnp.exp(-gate)) * up
            place = lax.rem((x if half == 0 else y) + second % 4, 4)
            total[pl.ds(64 * tile, 64), pl.ds(pl.multiple_of(half * 512 + place * 128, 128), 128)] = raw

    covs = PlaneGather(cc, 64, cc_send, cc_recv, pos, only=lambda bx, by: bx < 2)

    def cov_events(numbers):
        for number in numbers:
            for half in (0, 1):
                covs.event(number, half)

    arrivals((0, 1, 4))
    for ref, index in weights:
        swap(ref, index).wait_recv()
    select(other_w, 1 - k)
    arrivals((2, 3))
    siblings((0, 1, 2, 5))
    multiply(0, False)
    arrivals((5, 8, 10))
    tile_events((0, 1, 2, 3))
    siblings((3, 6, 9, 11))
    multiply(1, False)
    join(0, 0)
    arrivals((6, 7, 9))
    fetch_rows.wait()

    @pl.when(x < 2)
    def _():
        cc[x, y] = cov_rows[...].astype(BF16)

    covs.begin()
    tile_events((4, 5, 6, 7, 8))
    siblings((4, 7, 8, 10))
    join(0, 1)
    multiply(2, True)
    join(1, 0)
    arrivals((11, 12, 13, 14))
    siblings((12, 13, 14, 15))
    multiply(3, True)
    release(2)
    release(3)
    join(2, 0)
    join(3, 0)
    join(1, 1)
    tile_events(range(9, 15))
    cov_events((0, 1))
    for chunk in range(4):
        finish(chunk, 0)
    row = x * 4 + y

    @pl.when(row == 0)
    def _():
        first[0, 0] = total[0:64].astype(BF16)

    first_tile = PlaneGather(first, 64, f_send, f_recv, pos, only=lambda bx, by: (bx == 0) & (by == 0))
    first_tile.begin()

    def first_events(numbers):
        for number in numbers:
            first_tile.event(number, 0)
            first_tile.event(number, 1)

    join(2, 1)
    join(3, 1)
    jj[col] = tiles[...].reshape(512, 128).astype(F32).T[0:64].astype(BF16)
    corner = ColumnGather(jj, jj_send, jj_recv, pos)
    corner.begin()
    cov_events((2, 3, 4))
    fetch_cols.wait()
    cr[col] = cov_cols[...].T[0:64].astype(BF16)
    first_events((0, 1, 2, 3))
    finish(0, 1)
    first_events((4, 5, 6, 7, 8))
    finish(1, 1)
    finish(2, 1)
    corner.middle()
    finish(3, 1)
    raw = total[...]
    mass = jnp.sum(raw * raw, axis=0, keepdims=True)
    sum_y[y] = jnp.broadcast_to(mass, (8, PROMPTS))
    y_copies = to_axis(sum_y, sy_send, sy_recv, pos, 1)
    for out, _ in y_copies:
        out.start()
    kc[x, y] = raw.astype(BF16)
    keys = PlaneGather(kc, 128, kc_send, kc_recv, pos)
    keys.begin()
    first_events(range(9, 15))
    k5[col] = first[0, 0]
    first_keys = ColumnGather(k5, k5_send, k5_recv, pos)
    first_keys.begin()
    cov_events((5, 6, 9))
    for _, into in y_copies:
        into.wait_recv()
    sum_x[x] = sum_y[0] + sum_y[1] + sum_y[2] + sum_y[3]
    x_copies = to_axis(sum_x, sx_send, sx_recv, pos, 0)
    for out, _ in x_copies:
        out.start()
    corner.end()
    first_keys.middle()
    for _, into in x_copies:
        into.wait_recv()
    sum_c[col] = sum_x[0] + sum_x[1] + sum_x[2] + sum_x[3]
    c_copies = to_all_columns(sum_c, sc_send, sc_recv, pos)
    for out, _ in c_copies:
        out.start()

    source = lax.rem(row, 8)
    source_z = source // 2
    upper = row // 8
    away = lax.rem(z + 4 - source_z, 4)
    same = k == lax.rem(source, 2)

    def wave(number, kind, own=False):
        one, two = keys.block(0, *places[number]), keys.block(1, *places[number])
        bx = jnp.where(upper == 0, one[0], two[0])
        by = jnp.where(upper == 0, one[1], two[1])
        part = kind % 2
        dst = kr.at[bx, by, pl.ds(part * 32, 32)]
        src = kc.at[bx, by, pl.ds(pl.multiple_of(upper * 64 + part * 32, 32), 32)] if own else dst
        target = sibling if kind >= 2 else moved(pos, 2, 1 if kind == 0 else -1)
        return remote(src, dst, row_send.at[number, kind], row_recv.at[number, kind], target)

    def own_copy(number):
        one, two = keys.block(0, *places[number]), keys.block(1, *places[number])
        bx = jnp.where(upper == 0, one[0], two[0])
        by = jnp.where(upper == 0, one[1], two[1])
        return pltpu.make_async_copy(
            kc.at[bx, by, pl.ds(pl.multiple_of(upper * 64, 64), 64)], kr.at[bx, by], out_sem.at[number]
        )

    def relay(number):
        if number < 16:

            @pl.when(same & (away == 0))
            def _():
                for kind in (0, 1, 2, 3):
                    wave(number, kind, own=True).start()
                own_copy(number).start()

        for distance in (1, 2, 3):
            for kind, hops in ((0, distance), (1, 4 - distance)):
                block = number - LAG * hops
                if 0 <= block < 16:

                    @pl.when(same & (away == distance))
                    def _():
                        wave(block, kind).wait_recv()
                        if hops < 3:
                            wave(block, kind).start()
                        wave(block, kind + 2).start()

    def key_event(number):
        if number < 15:
            keys.event(number, 0)
            keys.event(number, 1)
        relay(number + 1)

    panel_rows = ColumnGather(cr, cr_send, cr_recv, pos)
    cov_events((7, 8))
    relay(0)
    key_event(0)
    first_keys.end()
    key_event(1)
    panel_rows.begin()
    for _, into in c_copies:
        into.wait_recv()
    mass = sum_c[0]
    for member in range(1, 8):
        mass = mass + sum_c[member]
    scale = lax.rsqrt(mass / HIDDEN + EPSILON) * (1.0 / 32.0)
    scale_ref[...] = scale * scale

    def save(number, source, target):
        return pltpu.make_async_copy(source, target, out_sem.at[16 + number])

    corner_raw = k5[...].reshape(512, PROMPTS).astype(F32)
    corner_keys = (corner_raw * scale[0:1]).astype(BF16)
    outer = lax.dot_general(corner_keys, corner_keys, (((1,), (1,)), ((), ())), preferred_element_type=F32)
    aug[:, 0:512] = jj[...].reshape(512, 512).astype(F32) + outer
    aug[:, 512:1024] = (
        lax.broadcasted_iota(jnp.int32, (512, 512), 0) == lax.broadcasted_iota(jnp.int32, (512, 512), 1)
    ).astype(F32)
    k5_scaled[...] = (corner_raw * (scale * scale)[0:1]).astype(BF16).reshape(8, 64, PROMPTS)
    save(0, k5_scaled, k5_out).start()
    beside = {
        2: 0, 3: 1, 4: 2, 5: 3, 6: 4, 7: 6, 8: 7, 9: 8, 10: 9, 11: 11, 12: 13, 13: 15, 14: 17, 15: 18, 16: 19, 17: 20, 18: 21, 19: 22, 20: 23, 21: 25, 22: 27, 23: 29,
    }
    extras = [{} for _ in range(4)]
    for number, step in beside.items():
        extras[step // 8][step % 8] = functools.partial(key_event, number)
    others = (
        (3, lambda: cov_events((10,))),
        (4, panel_rows.middle),
        (6, lambda: cov_events((11,))),
        (8, panel_rows.end),
        (8, lambda: cov_events((12,))),
        (10, lambda: cov_events((13,))),
        (12, lambda: cov_events((14,))),
        (14, lambda: save(1, cc, cc_out).start()),
        (20, lambda: save(3, cr, cr_out).start()),
        (22, lambda: save(2, kc, kc_out).start()),
    )
    for step, action in others:
        extras[step // 8][step % 8] = functools.partial(one_after_other, extras[step // 8].get(step % 8), action)
    factor(aug, work, extras)
    inv_ref[...] = aug[:, 512:1024]

    for number in range(16):

        @pl.when(k != lax.rem(source, 2))
        def _():
            wave(number, 2).wait_recv()
            wave(number, 3).wait_recv()

        @pl.when(same & (away == 0))
        def _():
            for kind in range(4):
                wave(number, kind, own=True).wait_send()
            own_copy(number).wait()

        for distance in (1, 2, 3):

            @pl.when(same & (away == distance))
            def _():
                for kind, hops in ((0, distance), (1, 4 - distance)):
                    if hops < 3:
                        wave(number, kind).wait_send()
                    wave(number, kind + 2).wait_send()

    first_tile.finish()
    keys.finish()
    panel_rows.finish()
    first_keys.finish()
    corner.finish()
    corner_tiles.finish()
    save(4, kr, kr_out).start()
    for ref, index in weights:
        swap(ref, index).wait_send()
    for copies in (square_copies, y_copies, x_copies, c_copies):
        for out, _ in copies:
            out.wait_send()
    gather.finish()
    covs.finish()
    remote(xx.at[k], xx.at[k], sib_send.at[0], sib_recv.at[0, 0], sibling).wait_send()
    remote(hop_out, hop_in, hop_send.at[0], hop_recv.at[0, 0], sibling).wait_send()
    save(0, k5_scaled, k5_out).wait()
    save(1, cc, cc_out).wait()
    save(2, kc, kc_out).wait()
    save(3, cr, cr_out).wait()
    save(4, kr, kr_out).wait()


def panel(residual, positions, gain, w_gate, w_up, cov):
    dma = pltpu.SemaphoreType.DMA
    vmem = pl.BlockSpec(memory_space=pltpu.VMEM)
    anywhere = pl.BlockSpec(memory_space=pl.ANY)
    spread = (
        ((4, 4, 128, PROMPTS), BF16),
        ((4, 4, 64, PROMPTS), BF16),
        ((8, 64, PROMPTS), BF16),
        ((8, 64, 1024), BF16),
        ((2, 4, 64, 2048), BF16),
    )
    return pl.pallas_call(
        panel_kernel,
        name="keys_and_panel",
        out_shape=tuple(jax.ShapeDtypeStruct(*one) for one in spread)
        + (jax.ShapeDtypeStruct((512, 512), F32), jax.ShapeDtypeStruct((8, PROMPTS), F32)),
        in_specs=[vmem] * 3 + [anywhere] * 3,
        out_specs=(anywhere,) * 5 + (vmem,) * 2,
        scratch_shapes=[
            pltpu.VMEM(*spread[0]), pltpu.VMEM(*spread[1]), pltpu.VMEM(*spread[2]), pltpu.VMEM(*spread[2]),
            pltpu.VMEM(*spread[3]), pltpu.VMEM(*spread[4]),
            pltpu.VMEM((1, 1, 64, PROMPTS), BF16),
            pltpu.VMEM((8, 64, 512), BF16),
            pltpu.VMEM((512, 1024), F32),
            pltpu.VMEM((128, 256), F32),
            pltpu.VMEM((2, 4, 4, 64, 640), BF16),
            pltpu.VMEM((2, 640, 1024), BF16),
            pltpu.VMEM((2, 640, 1024), BF16),
            pltpu.VMEM((4, 1280, 256), BF16),
            pltpu.VMEM((8, 8, 128), F32),
            pltpu.VMEM((4, 4, 128, 256), F32),
            pltpu.VMEM((4, 6, 2, 128, 128), BF16),
            pltpu.VMEM((4, 6, 2, 128, 128), BF16),
            pltpu.VMEM((128, PROMPTS), F32),
            pltpu.VMEM((4, 8, PROMPTS), F32),
            pltpu.VMEM((4, 8, PROMPTS), F32),
            pltpu.VMEM((8, 8, PROMPTS), F32),
            pltpu.VMEM((64, 2048), F32),
            pltpu.VMEM((1024, 128), F32),
            pltpu.VMEM((64, 128), F32),
            pltpu.VMEM((2, 4, 64, 128), BF16),
            dma((5,)), dma((2,)), dma((2,)), dma((7,)), dma((7,)), dma((2,)), dma((2, 16)), dma((1,)), dma((2, 16)),
            dma((1,)), dma((4, 12)), dma((3,)), dma((3,)), dma((3,)), dma((3,)), dma((7,)), dma((7,)), dma((2, 16)), dma((2, 16)),
            dma((2,)), dma((2, 16)), dma((8,)), dma((8,)), dma((8,)), dma((8,)), dma((8,)), dma((8,)), dma((2, 16)), dma((2, 16)),
            dma((16, 4)), dma((16, 4)), dma((21,)), dma((2, 16)), dma((2, 16)),
        ],
        compiler_params=pltpu.CompilerParams(collective_id=0, has_side_effects=True, vmem_limit_bytes=VMEM_LIMIT),
    )(residual, positions, gain, w_gate, w_up, cov)


def update_kernel(
    cov_ref, kc_ref, cc_ref, kr_ref, k5_ref, cr_ref, inv_ref, scale_ref, out_ref,
    covb, kcb, ccb, outb, panel, weights, rows, cov_sem, kc_sem, cc_sem, out_sem, zeros, zero_sem,
):
    x, y, z, k = here()
    row = x * 4 + y
    col = z * 2 + k
    nt = (((1,), (1,)), ((), ()))
    nn = (((1,), (0,)), ((), ()))
    tn = (((0,), (0,)), ((), ()))
    dot = functools.partial(lax.dot_general, preferred_element_type=F32)

    def load_cov(step):
        area = (pl.ds(step * 128, 1024 - step * 128), pl.ds(step * 256, 256))
        return pltpu.make_async_copy(cov_ref.at[area], covb.at[area], cov_sem.at[step])

    def load_kc(step):
        area = pl.ds(step * 2, 2)
        return pltpu.make_async_copy(kc_ref.at[area], kcb.at[area], kc_sem.at[step])

    def load_cc(step):
        area = (slice(None), slice(None), pl.ds(step * 256, 256))
        return pltpu.make_async_copy(cc_ref.at[area], ccb.at[area], cc_sem.at[step])

    def store(step):
        top = step * 128
        source = outb.at[step % 2, pl.ds(top, 1024 - top)]
        return pltpu.make_async_copy(source, out_ref.at[pl.ds(top, 1024 - top), pl.ds(step * 256, 256)], out_sem.at[step % 2])

    def clear(step):
        top = step * 128
        return pltpu.make_async_copy(zeros.at[pl.ds(0, top)], out_ref.at[pl.ds(0, top), pl.ds(step * 256, 256)], zero_sem.at[step])

    for step in range(8):
        load_kc(step).start()
        load_cc(step).start()
        load_cov(step).start()
    zeros[...] = jnp.zeros_like(zeros)
    for step in range(1, 8):
        clear(step).start()
    inverse = inv_ref[...]
    inverse_high = inverse.astype(BF16)
    first = k5_ref[...].reshape(512, PROMPTS)
    raw_rows = kr_ref[...].reshape(1024, PROMPTS)
    matrix_rows = cr_ref[...].reshape(512, 1024).astype(F32) + dot(first, raw_rows, nt)
    high, low = split(matrix_rows)
    panel_rows = dot(inverse_high, high, nn).astype(BF16)
    weights[...] = dot(panel_rows, inverse_high, tn).astype(BF16)
    own_high, own_low = split(inv_ref[pl.ds(pl.multiple_of(col * 64, 64), 64), :])
    panel[...] = dot(own_high, high, nn) + (dot(own_low, high, nn) + dot(own_high, low, nn))
    rows[...] = (raw_rows.astype(F32) * scale_ref[0:1] - dot(weights[...], first, nn)).astype(BF16)
    for step in range(8):
        top = step * 128
        height = 1024 - top
        load_kc(step).wait()
        load_cc(step).wait()
        load_cov(step).wait()
        if step >= 2:
            store(step - 2).wait()
        cols = kcb[2 * step : 2 * step + 2].reshape(256, PROMPTS)
        panel_cols = ccb[:, :, step * 256 : (step + 1) * 256].reshape(512, 256)
        value = covb[top:1024, step * 256 : (step + 1) * 256] + (dot(rows[top:], cols, nt) - dot(weights[top:], panel_cols, nn))
        if step == 0:
            value = jnp.concatenate([panel[...].T, value[:, 64:]], axis=1)
        edge = min(256, height)
        i = lax.broadcasted_iota(jnp.int32, (edge, 256), 0) + top
        j = lax.broadcasted_iota(jnp.int32, (edge, 256), 1) + step * 256
        row_global = (i // 64 * 16 + row) * 64 + i % 64
        col_global = (j // 64 * 8 + col) * 64 + j % 64
        outb[step % 2, top : top + edge] = jnp.where(row_global >= col_global, value[:edge], 0.0)
        if edge < height:
            outb[step % 2, top + edge : 1024] = value[edge:]
        store(step).start()
    store(6).wait()
    store(7).wait()
    for step in range(1, 8):
        clear(step).wait()


def update(cov, kc, kr, k5, cr, cc, inverse, scale):
    dma = pltpu.SemaphoreType.DMA
    vmem = pl.BlockSpec(memory_space=pltpu.VMEM)
    anywhere = pl.BlockSpec(memory_space=pl.ANY)
    return pl.pallas_call(
        update_kernel,
        name="update_lower",
        out_shape=jax.ShapeDtypeStruct((1024, 2048), F32),
        in_specs=[anywhere] * 3 + [vmem] * 5,
        out_specs=anywhere,
        scratch_shapes=[
            pltpu.VMEM((1024, 2048), F32), pltpu.VMEM((16, 128, PROMPTS), BF16), pltpu.VMEM((8, 64, 2048), BF16),
            pltpu.VMEM((2, 1024, 256), F32), pltpu.VMEM((64, 1024), F32), pltpu.VMEM((1024, 512), BF16), pltpu.VMEM((1024, PROMPTS), BF16),
            dma((8,)), dma((8,)), dma((8,)), dma((2,)), pltpu.VMEM((896, 256), F32), dma((8,)),
        ],
        compiler_params=pltpu.CompilerParams(vmem_limit_bytes=VMEM_LIMIT),
    )(cov, kc, cc, kr, k5, cr, inverse, scale)


def on_device(residual, positions, norm_gain, w_gate, w_up, covariance):
    kc, kr, k5, cr, cc, inverse, scale = panel(residual, positions, norm_gain, w_gate, w_up, covariance)
    kc = kc.reshape(16, 128, PROMPTS)
    kr = kr.reshape(16, 64, PROMPTS)
    cc = cc.reshape(8, 64, 2048)
    return update(covariance, kc, kr, k5, cr, cc, inverse, scale)


def solution(mesh):
    torus = Mesh(mesh.devices.reshape(4, 4, 4, 2), ("x", "y", "z", "k"))
    row, col = ("x", "y"), ("z", "k")
    placed = (P(row, None, col), P(row), P(col), P(col, row), P(col, row), P(row, col))
    return jax.shard_map(on_device, mesh=torus, in_specs=placed, out_specs=P(row, col), check_vma=False)
```

```python
import functools

import jax
import jax.numpy as jnp
from jax import lax
from jax.experimental import pallas as pl
from jax.experimental.pallas import tpu as pltpu
from jax.sharding import Mesh
from jax.sharding import PartitionSpec as P

MESH = pl.DeviceIdType.MESH
BF16 = jnp.bfloat16
F32 = jnp.float32
EPSILON = 1e-06
HIDDEN = 16384
WIDTH = 5120
PROMPTS = 1024
VMEM_LIMIT = 60 * 1024 * 1024
BASE = 16
LAG = 4


def here():
    return tuple(lax.axis_index(name) for name in ("x", "y", "z", "k"))


def moved(position, axis, step):
    place = list(position)
    size = 2 if axis == 3 else 4
    place[axis] = lax.rem(place[axis] + (step % size), size)
    return tuple(place)


def one_after_other(first, second):
    if first is not None:
        first()
    second()


def remote(src, dst, send, recv, target):
    return pltpu.make_async_remote_copy(
        src_ref=src, dst_ref=dst, send_sem=send, recv_sem=recv, device_id=target, device_id_type=MESH
    )


def greet(targets):
    barrier = pltpu.get_barrier_semaphore()
    for target in targets:
        pl.semaphore_signal(barrier, inc=1, device_id=target, device_id_type=MESH)
    pl.semaphore_wait(barrier, len(targets))


def when(condition, action):
    if condition is None:
        action()
    else:
        pl.when(condition)(action)


class PlaneGather:
    SENT = (
        (0, 0, 1, 1, None), (0, 0, 1, -1, None), (-1, 0, 1, 1, 0), (1, 0, 1, -1, 1),
        (0, 0, 0, 1, None), (-1, 0, 0, 1, None), (1, 0, 0, 1, None), (2, 0, 0, 1, None),
        (0, 0, 0, -1, None), (-1, 0, 0, -1, None), (1, 0, 0, -1, None), (2, 0, 0, -1, None),
        (0, -1, 0, 1, None), (-1, -1, 0, 1, None), (1, 1, 0, -1, None), (2, 1, 0, -1, None),
    )
    GOT = (
        (-1, 0, None), (1, 0, None), (2, 0, 0), (2, 0, 1),
        (0, -1, None), (-1, -1, None), (1, -1, None), (2, -1, None),
        (0, 1, None), (-1, 1, None), (1, 1, None), (2, 1, None),
        (0, 2, None), (-1, 2, None), (1, 2, None), (2, 2, None),
    )
    EVENTS = (
        ((0,), (2, 5, 9)), ((1,), (3, 6, 10)), ((4,), (12,)), ((8,), ()), ((2, 3), (7, 11)), ((5,), (13,)), ((10,), (14,)),
        ((9,), ()), ((6,), ()), ((11,), (15,)), ((7,), ()), ((12,), ()), ((13,), ()), ((14,), ()), ((15,), ()),
    )
    PLACES = tuple(((-1, 0), (1, 0), (0, -1), (0, 1), (2, 0), (-1, -1), (1, 1), (-1, 1), (1, -1), (2, 1), (2, -1), (0, 2), (-1, 2), (1, 2), (2, 2)))

    def __init__(self, buf, rows, send, recv, pos, only=None):
        self.buf, self.rows, self.send, self.recv, self.pos, self.only = buf, rows, send, recv, pos, only

    def block(self, half, first, second):
        dx, dy = (second, first) if half == 0 else (first, second)
        return lax.rem(self.pos[0] + dx % 4, 4), lax.rem(self.pos[1] + dy % 4, 4)

    def piece(self, half, first, second, part=None):
        size = self.rows // 2
        start = half * size
        if part is not None:
            size //= 2
            start += part * size
        bx, by = self.block(half, first, second)
        return self.buf.at[bx, by, pl.ds(start, size)]

    def cond(self, half, first, second):
        return None if self.only is None else self.only(*self.block(half, first, second))

    def copy(self, half, kind, first, second, axis, step, part=None):
        axis = axis if half == 0 else 1 - axis
        ref = self.piece(half, first, second, part)
        sender = self.send.at[half, kind] if self.only is not None else self.send.at[0 if kind < 4 else 1]
        return remote(ref, ref, sender, self.recv.at[half, kind], moved(self.pos, axis, step))

    def go(self, half, kind):
        first, second, axis, step, part = self.SENT[kind]
        when(self.cond(half, first, second), lambda: self.copy(half, kind, first, second, axis, step, part).start())

    def arrive(self, half, kind):
        first, second, part = self.GOT[kind]
        when(self.cond(half, first, second), lambda: self.copy(half, kind, first, second, 0, 1, part).wait_recv())

    def begin(self):
        for kind in (0, 1, 4, 8):
            for half in (0, 1):
                self.go(half, kind)

    def event(self, number, half):
        kinds, on = self.EVENTS[number]
        for kind in kinds:
            self.arrive(half, kind)
        for kind in on:
            self.go(half, kind)

    def finish(self):
        if self.only is None:
            for number, ref in ((0, self.buf.at[0, pl.ds(0, 3)]), (1, self.buf.at[pl.ds(0, 3)])):
                remote(ref, ref, self.send.at[number], self.recv.at[0, 0], moved(self.pos, 0, 1)).wait_send()
            return
        for half in (0, 1):
            for kind in range(16):
                first, second, axis, step, part = self.SENT[kind]
                when(
                    self.cond(half, first, second),
                    lambda: self.copy(half, kind, first, second, axis, step, part).wait_send(),
                )


class ColumnGather:
    def __init__(self, buf, send, recv, pos):
        self.buf, self.send, self.recv, self.pos = buf, send, recv, pos

    def piece(self, dz, dk=0, part=None):
        z, k = self.pos[2], self.pos[3]
        slot = lax.rem(z + dz % 4, 4) * 2 + lax.rem(k + dk, 2)
        if part is None:
            return self.buf.at[slot]
        return self.buf.at[slot, pl.ds(32 * part, 32)]

    SENT = {0: (0, 2, 1, None), 1: (0, 2, -1, None), 2: (-1, 2, 1, 0), 3: (1, 2, -1, 1),
            4: (0, 3, 1, None), 5: (-1, 3, 1, None), 6: (1, 3, 1, None), 7: (2, 3, 1, None)}
    GOT = {0: (-1, 0, None), 1: (1, 0, None), 2: (2, 0, 0), 3: (2, 0, 1),
           4: (0, 1, None), 5: (-1, 1, None), 6: (1, 1, None), 7: (2, 1, None)}

    def go(self, kind):
        dz, axis, step, part = self.SENT[kind]
        ref = self.piece(dz, 0, part)
        remote(ref, ref, self.send.at[kind], self.recv.at[kind], moved(self.pos, axis, step)).start()

    def arrive(self, kind):
        dz, dk, part = self.GOT[kind]
        ref = self.piece(dz, dk, part)
        remote(ref, ref, self.send.at[kind], self.recv.at[kind], moved(self.pos, 2, 1)).wait_recv()

    def begin(self):
        for kind in (0, 1, 4):
            self.go(kind)

    def middle(self):
        self.arrive(0)
        self.go(2)
        self.go(5)
        self.arrive(1)
        self.go(3)
        self.go(6)

    def end(self):
        self.arrive(2)
        self.arrive(3)
        self.go(7)
        for kind in (4, 5, 6, 7):
            self.arrive(kind)

    def finish(self):
        for kind in range(8):
            dz, axis, step, part = self.SENT[kind]
            ref = self.piece(dz, 0, part)
            remote(ref, ref, self.send.at[kind], self.recv.at[kind], moved(self.pos, axis, step)).wait_send()


def column_peers(pos):
    peers = []
    for dz in range(4):
        for dk in range(2):
            if dz or dk:
                peers.append(moved(moved(pos, 2, dz), 3, dk))
    return peers


def to_all_columns(buf, send, recv, pos):
    copies = []
    mine = pos[2] * 2 + pos[3]
    number = 0
    for dz in range(4):
        for dk in range(2):
            if dz == 0 and dk == 0:
                continue
            target = moved(moved(pos, 2, dz), 3, dk)
            out = remote(buf.at[mine], buf.at[mine], send.at[number], recv.at[number], target)
            origin = moved(moved(pos, 2, -dz), 3, -dk)
            slot = origin[2] * 2 + origin[3]
            into = remote(buf.at[slot], buf.at[slot], send.at[number], recv.at[number], target)
            copies.append((out, into))
            number += 1
    return copies


def to_axis(buf, send, recv, pos, axis):
    copies = []
    mine = pos[axis]
    for step in (1, 2, 3):
        target = moved(pos, axis, step)
        out = remote(buf.at[mine], buf.at[mine], send.at[step - 1], recv.at[step - 1], target)
        slot = moved(pos, axis, -step)[axis]
        into = remote(buf.at[slot], buf.at[slot], send.at[step - 1], recv.at[step - 1], target)
        copies.append((out, into))
    return copies


def exchange(copies):
    for out, _ in copies:
        out.start()
    for _, into in copies:
        into.wait_recv()


def split(value):
    high = value.astype(BF16)
    return high, (value - high.astype(F32)).astype(BF16)


def dot3(left, right, dims):
    lh, ll = split(left)
    rh, rl = split(right)
    dot = functools.partial(lax.dot_general, dimension_numbers=(dims, ((), ())), preferred_element_type=F32)
    return dot(lh, rh) + (dot(lh, rl) + dot(ll, rh))


def small_factor(work, extra):
    lane = lax.broadcasted_iota(jnp.int32, (1, 128), 1)

    def body(step, carry):
        start = pl.multiple_of(step * BASE, BASE)
        rows = work[pl.ds(start, BASE), :]
        turned = pltpu.roll(rows[:, :128], lax.rem(128 - start, 128), 1)
        entry = [[jnp.broadcast_to(turned[i : i + 1, j : j + 1], (1, 128)) for j in range(i + 1)] for i in range(BASE)]
        solved = []
        for j in range(BASE):
            inverse = lax.rsqrt(entry[j][j])
            row = rows[j : j + 1, :]
            for m in range(j):
                row = row - jnp.concatenate([entry[j][m]] * 2, axis=1) * solved[m]
            solved.append(row * jnp.concatenate([inverse] * 2, axis=1))
            for i in range(j + 1, BASE):
                entry[i][j] = entry[i][j] * inverse
            for i in range(j + 1, BASE):
                for m in range(j + 1, i + 1):
                    entry[i][m] = entry[i][m] - entry[i][j] * entry[m][j]
        block = jnp.concatenate(solved, axis=0)
        work[pl.ds(start, BASE), :] = block
        later = jnp.where(lane >= start + BASE, block[:, :128], 0.0)
        lh, ll = split(later)
        rh, rl = split(block)
        left = jnp.concatenate([lh, lh, ll], axis=0)
        right = jnp.concatenate([rh, rl, rh], axis=0)
        work[...] = work[...] - lax.dot_general(left, right, (((0,), (0,)), ((), ())), preferred_element_type=F32)
        for number, action in extra.items():
            pl.when(step == number)(action)
        return carry

    lax.fori_loop(0, 128 // BASE, body, 0)


def factor(aug, work, extras):
    eye = (lax.broadcasted_iota(jnp.int32, (128, 128), 0) == lax.broadcasted_iota(jnp.int32, (128, 128), 1)).astype(F32)
    for number in range(4):
        lo, hi = number * 128, (number + 1) * 128
        work[:, 0:128] = aug[lo:hi, lo:hi]
        work[:, 128:256] = eye
        small_factor(work, extras[number])
        inverse = work[:, 128:256]
        if hi < 512:
            right = dot3(inverse, aug[lo:hi, hi : 512 + lo], ((1,), (0,)))
            full = jnp.concatenate([right, inverse], axis=1)
            aug[lo:hi, hi : 512 + hi] = full
            ahead = right[:, 0 : 512 - hi]
            aug[hi:512, hi : 512 + hi] = aug[hi:512, hi : 512 + hi] - dot3(ahead, full, ((0,), (0,)))
        else:
            aug[lo:hi, 512 : 512 + lo] = dot3(inverse, aug[lo:hi, 512 : 512 + lo], ((1,), (0,)))
            aug[lo:hi, 512 + lo : 512 + hi] = inverse


def panel_kernel(
    residual_ref, positions_ref, gain_ref, gate_ref, up_ref, cov_ref, kc_out, kr_out, k5_out, cr_out, cc_out, inv_ref, scale_ref,
    kc, kr, k5, k5_scaled, cr, cc, first, jj, aug, work,
    xx, own_w, other_w, sel_w, squares, part, hop_out, hop_in, total, sum_y, sum_x, sum_c, cov_rows, cov_cols, cov_corner, tiles,
    local_sem, w_send, w_recv, sq_send, sq_recv, x_send, x_recv, sib_send, sib_recv,
    hop_send, hop_recv, sy_send, sy_recv, sx_send, sx_recv, sc_send, sc_recv, cc_send, cc_recv,
    kc_send, kc_recv, k5_send, k5_recv, cr_send, cr_recv, jj_send, jj_recv, f_send, f_recv, row_send, row_recv, out_sem, tile_send, tile_recv,
):
    pos = here()
    x, y, z, k = pos
    sibling = moved(pos, 3, 1)
    col = z * 2 + k
    plane = [moved(pos, axis, step) for axis in (0, 1) for step in (1, 2, 3)]
    barrier = pltpu.get_barrier_semaphore()
    peers = plane + column_peers(pos)
    for peer in peers:
        pl.semaphore_signal(barrier, inc=1, device_id=peer, device_id_type=MESH)

    weights = ((gate_ref, 0), (up_ref, 1))

    def swap(ref, index):
        return remote(ref, other_w.at[index], w_send.at[index], w_recv.at[index], sibling)

    def fetch(ref, index):
        return pltpu.make_async_copy(ref, own_w.at[index], local_sem.at[index])

    fetch_rows = pltpu.make_async_copy(cov_ref.at[pl.ds(0, 64)], cov_rows, local_sem.at[2])
    fetch_cols = pltpu.make_async_copy(cov_ref.at[:, pl.ds(0, 128)], cov_cols, local_sem.at[3])

    fetch_corner = pltpu.make_async_copy(cov_ref.at[pl.ds(0, 64), pl.ds(0, 128)], cov_corner, local_sem.at[4])
    fetch_corner.start()
    line_of = lax.broadcasted_iota(jnp.int32, (64, 64), 0)
    prompt_of = lax.broadcasted_iota(jnp.int32, (64, 64), 1)
    place = positions_ref[...].reshape(1, 64).astype(F32)
    place = jnp.sum(jnp.where(line_of == prompt_of, place, 0.0), axis=1, keepdims=True)
    token = lax.broadcasted_iota(jnp.int32, (64, 1024), 1) - 16 * lax.broadcasted_iota(jnp.int32, (64, 1024), 0)
    pick = (token.astype(F32) == place).astype(BF16)
    subject = jnp.dot(pick, residual_ref[...].reshape(1024, 640), preferred_element_type=F32)
    squared = subject * subject
    folded = squared[:, 0:128]
    for group in range(1, 5):
        folded = folded + squared[:, group * 128 : (group + 1) * 128]
    own_mass = jnp.sum(folded, axis=1, keepdims=True)
    mass_row = jnp.sum(jnp.where(line_of == prompt_of, own_mass, 0.0), axis=0, keepdims=True)
    squares[col] = jnp.broadcast_to(jnp.concatenate([mass_row, mass_row], axis=1), (8, 128))
    pl.semaphore_wait(barrier, len(peers))
    square_copies = to_all_columns(squares, sq_send, sq_recv, pos)
    for out, _ in square_copies:
        out.start()
    for ref, index in weights:
        fetch(ref, index).start()
        swap(ref, index).start()
    fetch_corner.wait()

    @pl.when(x < 2)
    def _():
        tiles[x, y] = cov_corner[...].astype(BF16)

    corner_tiles = PlaneGather(tiles, 64, tile_send, tile_recv, pos, only=lambda bx, by: bx < 2)
    corner_tiles.begin()

    def tile_events(numbers):
        for number in numbers:
            for half in (0, 1):
                corner_tiles.event(number, half)

    fetch_rows.start()
    fetch_cols.start()

    def select(source, core):
        def body(step, carry):
            first = pl.ds(pl.multiple_of(step * 128, 128), 128)
            second = pl.ds(pl.multiple_of(512 + step * 128, 128), 128)
            rows = pl.ds(pl.multiple_of(core * 640, 128), 640)
            for index, lanes in enumerate((first, second)):
                gate, up = source[0, :, lanes], source[1, :, lanes]

                @pl.when(k == 0)
                def _():
                    sel_w[step, rows, pl.ds(index * 128, 128)] = jnp.concatenate([gate[:, :64], up[:, :64]], axis=1)

                @pl.when(k == 1)
                def _():
                    sel_w[step, rows, pl.ds(index * 128, 128)] = jnp.concatenate([gate[:, 64:], up[:, 64:]], axis=1)

            return carry

        lax.fori_loop(0, 4, body, 0)

    for _, into in square_copies:
        into.wait_recv()
    everyone = squares[0]
    for member in range(1, 8):
        everyone = everyone + squares[member]
    everyone = jnp.sum(jnp.where(line_of == prompt_of, everyone[0:1, 0:64], 0.0), axis=1, keepdims=True)
    inverse_rms = lax.rsqrt(everyone / WIDTH + EPSILON)
    xx[k, x, y] = (subject * inverse_rms * gain_ref[...].reshape(1, 640)).astype(BF16)

    gather = PlaneGather(xx.at[k], 64, x_send, x_recv, pos)
    gather.begin()

    def to_sibling(half, number, first, second):
        ref = gather.piece(half, first, second)
        return remote(ref, ref, sib_send.at[0], sib_recv.at[half, number], sibling)

    def from_sibling(half, number, first, second):
        bx, by = gather.block(half, first, second)
        ref = xx.at[1 - k, bx, by, pl.ds(half * 32, 32)]
        return remote(ref, ref, sib_send.at[0], sib_recv.at[half, number], sibling)

    places = ((0, 0),) + PlaneGather.PLACES
    for half in (0, 1):
        to_sibling(half, 0, 0, 0).start()

    for ref, index in weights:
        fetch(ref, index).wait()
    select(own_w, k)

    def arrivals(numbers):
        for number in numbers:
            for half in (0, 1):
                gather.event(number, half)
                to_sibling(half, number + 1, *places[number + 1]).start()

    def siblings(numbers):
        for number in numbers:
            for half in (0, 1):
                from_sibling(half, number, *places[number]).wait_recv()

    def line(core, half, second):
        if half == 0:
            value = xx[core, lax.rem(x + second % 4, 4), :, 0:32, :]
        else:
            value = xx[core, :, lax.rem(y + second % 4, 4), 32:64, :]
        return value.reshape(128, 640)

    def product(chunk, dest):
        second = (0, -1, 1, 2)[chunk]
        value = None
        for core in (0, 1):
            left = jnp.concatenate([line(core, 0, second), line(core, 1, second)], axis=0)
            term = jnp.dot(left, sel_w[dest, core * 640 : core * 640 + 640], preferred_element_type=F32)
            value = term if value is None else value + term
        return value

    def dest(step):
        return lax.rem(z + step % 4, 4)

    def hop(chunk, kind, tile):
        target = moved(pos, 2, 1 if kind % 2 == 0 else -1)
        return remote(
            hop_out.at[chunk, kind, tile], hop_in.at[chunk, kind, tile],
            hop_send.at[0], hop_recv.at[chunk, kind + 6 * tile], target,
        )

    def lanes(tile):
        return slice(128 * tile, 128 * tile + 128)

    def multiply(chunk, hold):
        def send(kind, value):
            for tile in (0, 1):
                hop_out[chunk, kind, tile] = value[:, lanes(tile)].astype(BF16)
                if tile == 0 or not hold:
                    hop(chunk, kind, tile).start()

        value = product(chunk, dest(2))
        send(0, value[:128])
        send(1, value[128:])
        value = product(chunk, dest(1))
        send(2, value[128:])
        part[chunk, 0] = value[:128]
        value = product(chunk, dest(-1))
        send(3, value[:128])
        part[chunk, 1] = value[128:]
        value = product(chunk, dest(0))
        part[chunk, 2] = value[:128]
        part[chunk, 3] = value[128:]

    def release(chunk):
        for kind in range(4):
            hop(chunk, kind, 1).start()

    def join(chunk, tile):
        for kind in (0, 1):
            hop(chunk, kind, tile).wait_recv()
            value = part[chunk, kind, :, lanes(tile)] + hop_in[chunk, kind, tile].astype(F32)
            hop_out[chunk, 4 + kind, tile] = value.astype(BF16)
            hop(chunk, 4 + kind, tile).start()

    def finish(chunk, tile):
        second = (0, -1, 1, 2)[chunk]
        for half in (0, 1):
            kinds = (4, 3) if half == 0 else (2, 5)
            for kind in kinds:
                hop(chunk, kind, tile).wait_recv()
            value = part[chunk, 2 + half, :, lanes(tile)] + (
                hop_in[chunk, kinds[0], tile].astype(F32) + hop_in[chunk, kinds[1], tile].astype(F32)
            )
            turned = value.T
            gate, up = turned[:64], turned[64:]
            raw = gate / (1.0 + jnp.exp(-gate)) * up
            place = lax.rem((x if half == 0 else y) + second % 4, 4)
            total[pl.ds(64 * tile, 64), pl.ds(pl.multiple_of(half * 512 + place * 128, 128), 128)] = raw

    covs = PlaneGather(cc, 64, cc_send, cc_recv, pos, only=lambda bx, by: bx < 2)

    def cov_events(numbers):
        for number in numbers:
            for half in (0, 1):
                covs.event(number, half)

    arrivals((0, 1, 4))
    for ref, index in weights:
        swap(ref, index).wait_recv()
    select(other_w, 1 - k)
    arrivals((2, 3))
    siblings((0, 1, 2, 5))
    multiply(0, False)
    arrivals((5, 8, 10))
    tile_events((0, 1, 2, 3))
    siblings((3, 6, 9, 11))
    multiply(1, False)
    join(0, 0)
    arrivals((6, 7, 9))
    fetch_rows.wait()

    @pl.when(x < 2)
    def _():
        cc[x, y] = cov_rows[...].astype(BF16)

    covs.begin()
    tile_events((4, 5, 6, 7, 8))
    siblings((4, 7, 8, 10))
    join(0, 1)
    multiply(2, True)
    join(1, 0)
    arrivals((11, 12, 13, 14))
    siblings((12, 13, 14, 15))
    multiply(3, True)
    release(2)
    release(3)
    join(2, 0)
    join(3, 0)
    join(1, 1)
    tile_events(range(9, 15))
    cov_events((0, 1))
    for chunk in range(4):
        finish(chunk, 0)
    row = x * 4 + y

    @pl.when(row == 0)
    def _():
        first[0, 0] = total[0:64].astype(BF16)

    first_tile = PlaneGather(first, 64, f_send, f_recv, pos, only=lambda bx, by: (bx == 0) & (by == 0))
    first_tile.begin()

    def first_events(numbers):
        for number in numbers:
            first_tile.event(number, 0)
            first_tile.event(number, 1)

    join(2, 1)
    join(3, 1)
    jj[col] = tiles[...].reshape(512, 128).astype(F32).T[0:64].astype(BF16)
    corner = ColumnGather(jj, jj_send, jj_recv, pos)
    corner.begin()
    cov_events((2, 3, 4))
    fetch_cols.wait()
    cr[col] = cov_cols[...].T[0:64].astype(BF16)
    first_events((0, 1, 2, 3))
    finish(0, 1)
    first_events((4, 5, 6, 7, 8))
    finish(1, 1)
    finish(2, 1)
    corner.middle()
    finish(3, 1)
    raw = total[...]
    mass = jnp.sum(raw * raw, axis=0, keepdims=True)
    sum_y[y] = jnp.broadcast_to(mass, (8, PROMPTS))
    y_copies = to_axis(sum_y, sy_send, sy_recv, pos, 1)
    for out, _ in y_copies:
        out.start()
    kc[x, y] = raw.astype(BF16)
    keys = PlaneGather(kc, 128, kc_send, kc_recv, pos)
    keys.begin()
    first_events(range(9, 15))
    k5[col] = first[0, 0]
    first_keys = ColumnGather(k5, k5_send, k5_recv, pos)
    first_keys.begin()
    cov_events((5, 6, 9))
    for _, into in y_copies:
        into.wait_recv()
    sum_x[x] = sum_y[0] + sum_y[1] + sum_y[2] + sum_y[3]
    x_copies = to_axis(sum_x, sx_send, sx_recv, pos, 0)
    for out, _ in x_copies:
        out.start()
    corner.end()
    first_keys.middle()
    for _, into in x_copies:
        into.wait_recv()
    sum_c[col] = sum_x[0] + sum_x[1] + sum_x[2] + sum_x[3]
    c_copies = to_all_columns(sum_c, sc_send, sc_recv, pos)
    for out, _ in c_copies:
        out.start()

    source = lax.rem(row, 8)
    source_z = source // 2
    upper = row // 8
    away = lax.rem(z + 4 - source_z, 4)
    same = k == lax.rem(source, 2)

    def wave(number, kind, own=False):
        one, two = keys.block(0, *places[number]), keys.block(1, *places[number])
        bx = jnp.where(upper == 0, one[0], two[0])
        by = jnp.where(upper == 0, one[1], two[1])
        part = kind % 2
        dst = kr.at[bx, by, pl.ds(part * 32, 32)]
        src = kc.at[bx, by, pl.ds(pl.multiple_of(upper * 64 + part * 32, 32), 32)] if own else dst
        target = sibling if kind >= 2 else moved(pos, 2, 1 if kind == 0 else -1)
        return remote(src, dst, row_send.at[number, kind], row_recv.at[number, kind], target)

    def own_copy(number):
        one, two = keys.block(0, *places[number]), keys.block(1, *places[number])
        bx = jnp.where(upper == 0, one[0], two[0])
        by = jnp.where(upper == 0, one[1], two[1])
        return pltpu.make_async_copy(
            kc.at[bx, by, pl.ds(pl.multiple_of(upper * 64, 64), 64)], kr.at[bx, by], out_sem.at[number]
        )

    def relay(number):
        if number < 16:

            @pl.when(same & (away == 0))
            def _():
                for kind in (0, 1, 2, 3):
                    wave(number, kind, own=True).start()
                own_copy(number).start()

        for distance in (1, 2, 3):
            for kind, hops in ((0, distance), (1, 4 - distance)):
                block = number - LAG * hops
                if 0 <= block < 16:

                    @pl.when(same & (away == distance))
                    def _():
                        wave(block, kind).wait_recv()
                        if hops < 3:
                            wave(block, kind).start()
                        wave(block, kind + 2).start()

    def key_event(number):
        if number < 15:
            keys.event(number, 0)
            keys.event(number, 1)
        relay(number + 1)

    panel_rows = ColumnGather(cr, cr_send, cr_recv, pos)
    cov_events((7, 8))
    relay(0)
    key_event(0)
    first_keys.end()
    key_event(1)
    panel_rows.begin()
    for _, into in c_copies:
        into.wait_recv()
    mass = sum_c[0]
    for member in range(1, 8):
        mass = mass + sum_c[member]
    scale = lax.rsqrt(mass / HIDDEN + EPSILON) * (1.0 / 32.0)
    scale_ref[...] = scale * scale

    def save(number, source, target):
        return pltpu.make_async_copy(source, target, out_sem.at[16 + number])

    corner_raw = k5[...].reshape(512, PROMPTS).astype(F32)
    corner_keys = (corner_raw * scale[0:1]).astype(BF16)
    outer = lax.dot_general(corner_keys, corner_keys, (((1,), (1,)), ((), ())), preferred_element_type=F32)
    aug[:, 0:512] = jj[...].reshape(512, 512).astype(F32) + outer
    aug[:, 512:1024] = (
        lax.broadcasted_iota(jnp.int32, (512, 512), 0) == lax.broadcasted_iota(jnp.int32, (512, 512), 1)
    ).astype(F32)
    k5_scaled[...] = (corner_raw * (scale * scale)[0:1]).astype(BF16).reshape(8, 64, PROMPTS)
    save(0, k5_scaled, k5_out).start()
    beside = {
        2: 0, 3: 1, 4: 2, 5: 3, 6: 4, 7: 6, 8: 7, 9: 8, 10: 9, 11: 11, 12: 13, 13: 15, 14: 17, 15: 18, 16: 19, 17: 20, 18: 21, 19: 22, 20: 23, 21: 24, 22: 25, 23: 26, 24: 27, 25: 28, 26: 29,
    }
    extras = [{} for _ in range(4)]
    for number, step in beside.items():
        extras[step // 8][step % 8] = functools.partial(key_event, number)
    others = (
        (3, lambda: cov_events((10,))),
        (4, panel_rows.middle),
        (6, lambda: cov_events((11,))),
        (8, panel_rows.end),
        (8, lambda: cov_events((12,))),
        (10, lambda: cov_events((13,))),
        (12, lambda: cov_events((14,))),
        (14, lambda: save(1, cc, cc_out).start()),
        (20, lambda: save(3, cr, cr_out).start()),
        (22, lambda: save(2, kc, kc_out).start()),
    )
    for step, action in others:
        extras[step // 8][step % 8] = functools.partial(one_after_other, extras[step // 8].get(step % 8), action)
    factor(aug, work, extras)
    inv_ref[...] = aug[:, 512:1024]

    for number in range(16):

        @pl.when(k != lax.rem(source, 2))
        def _():
            wave(number, 2).wait_recv()
            wave(number, 3).wait_recv()

        @pl.when(same & (away == 0))
        def _():
            for kind in range(4):
                wave(number, kind, own=True).wait_send()
            own_copy(number).wait()

        for distance in (1, 2, 3):

            @pl.when(same & (away == distance))
            def _():
                for kind, hops in ((0, distance), (1, 4 - distance)):
                    if hops < 3:
                        wave(number, kind).wait_send()
                    wave(number, kind + 2).wait_send()

    first_tile.finish()
    keys.finish()
    panel_rows.finish()
    first_keys.finish()
    corner.finish()
    corner_tiles.finish()
    save(4, kr, kr_out).start()
    for ref, index in weights:
        swap(ref, index).wait_send()
    for copies in (square_copies, y_copies, x_copies, c_copies):
        for out, _ in copies:
            out.wait_send()
    gather.finish()
    covs.finish()
    remote(xx.at[k], xx.at[k], sib_send.at[0], sib_recv.at[0, 0], sibling).wait_send()
    remote(hop_out, hop_in, hop_send.at[0], hop_recv.at[0, 0], sibling).wait_send()
    save(0, k5_scaled, k5_out).wait()
    save(1, cc, cc_out).wait()
    save(2, kc, kc_out).wait()
    save(3, cr, cr_out).wait()
    save(4, kr, kr_out).wait()


def panel(residual, positions, gain, w_gate, w_up, cov):
    dma = pltpu.SemaphoreType.DMA
    vmem = pl.BlockSpec(memory_space=pltpu.VMEM)
    anywhere = pl.BlockSpec(memory_space=pl.ANY)
    spread = (
        ((4, 4, 128, PROMPTS), BF16),
        ((4, 4, 64, PROMPTS), BF16),
        ((8, 64, PROMPTS), BF16),
        ((8, 64, 1024), BF16),
        ((2, 4, 64, 2048), BF16),
    )
    return pl.pallas_call(
        panel_kernel,
        name="keys_and_panel",
        out_shape=tuple(jax.ShapeDtypeStruct(*one) for one in spread)
        + (jax.ShapeDtypeStruct((512, 512), F32), jax.ShapeDtypeStruct((8, PROMPTS), F32)),
        in_specs=[vmem] * 3 + [anywhere] * 3,
        out_specs=(anywhere,) * 5 + (vmem,) * 2,
        scratch_shapes=[
            pltpu.VMEM(*spread[0]), pltpu.VMEM(*spread[1]), pltpu.VMEM(*spread[2]), pltpu.VMEM(*spread[2]),
            pltpu.VMEM(*spread[3]), pltpu.VMEM(*spread[4]),
            pltpu.VMEM((1, 1, 64, PROMPTS), BF16),
            pltpu.VMEM((8, 64, 512), BF16),
            pltpu.VMEM((512, 1024), F32),
            pltpu.VMEM((128, 256), F32),
            pltpu.VMEM((2, 4, 4, 64, 640), BF16),
            pltpu.VMEM((2, 640, 1024), BF16),
            pltpu.VMEM((2, 640, 1024), BF16),
            pltpu.VMEM((4, 1280, 256), BF16),
            pltpu.VMEM((8, 8, 128), F32),
            pltpu.VMEM((4, 4, 128, 256), F32),
            pltpu.VMEM((4, 6, 2, 128, 128), BF16),
            pltpu.VMEM((4, 6, 2, 128, 128), BF16),
            pltpu.VMEM((128, PROMPTS), F32),
            pltpu.VMEM((4, 8, PROMPTS), F32),
            pltpu.VMEM((4, 8, PROMPTS), F32),
            pltpu.VMEM((8, 8, PROMPTS), F32),
            pltpu.VMEM((64, 2048), F32),
            pltpu.VMEM((1024, 128), F32),
            pltpu.VMEM((64, 128), F32),
            pltpu.VMEM((2, 4, 64, 128), BF16),
            dma((5,)), dma((2,)), dma((2,)), dma((7,)), dma((7,)), dma((2,)), dma((2, 16)), dma((1,)), dma((2, 16)),
            dma((1,)), dma((4, 12)), dma((3,)), dma((3,)), dma((3,)), dma((3,)), dma((7,)), dma((7,)), dma((2, 16)), dma((2, 16)),
            dma((2,)), dma((2, 16)), dma((8,)), dma((8,)), dma((8,)), dma((8,)), dma((8,)), dma((8,)), dma((2, 16)), dma((2, 16)),
            dma((16, 4)), dma((16, 4)), dma((21,)), dma((2, 16)), dma((2, 16)),
        ],
        compiler_params=pltpu.CompilerParams(collective_id=0, has_side_effects=True, vmem_limit_bytes=VMEM_LIMIT),
    )(residual, positions, gain, w_gate, w_up, cov)


def update_kernel(
    cov_ref, kc_ref, cc_ref, kr_ref, k5_ref, cr_ref, inv_ref, scale_ref, out_ref,
    covb, kcb, ccb, outb, panel, weights, rows, cov_sem, kc_sem, cc_sem, out_sem, zeros, zero_sem,
):
    x, y, z, k = here()
    row = x * 4 + y
    col = z * 2 + k
    nt = (((1,), (1,)), ((), ()))
    nn = (((1,), (0,)), ((), ()))
    tn = (((0,), (0,)), ((), ()))
    dot = functools.partial(lax.dot_general, preferred_element_type=F32)

    def load_cov(step):
        area = (pl.ds(step * 128, 1024 - step * 128), pl.ds(step * 256, 256))
        return pltpu.make_async_copy(cov_ref.at[area], covb.at[area], cov_sem.at[step])

    def load_kc(step):
        area = pl.ds(step * 2, 2)
        return pltpu.make_async_copy(kc_ref.at[area], kcb.at[area], kc_sem.at[step])

    def load_cc(step):
        area = (slice(None), slice(None), pl.ds(step * 256, 256))
        return pltpu.make_async_copy(cc_ref.at[area], ccb.at[area], cc_sem.at[step])

    def store(step):
        top = step * 128
        source = outb.at[step % 2, pl.ds(top, 1024 - top)]
        return pltpu.make_async_copy(source, out_ref.at[pl.ds(top, 1024 - top), pl.ds(step * 256, 256)], out_sem.at[step % 2])

    def clear(step):
        top = step * 128
        return pltpu.make_async_copy(zeros.at[pl.ds(0, top)], out_ref.at[pl.ds(0, top), pl.ds(step * 256, 256)], zero_sem.at[step])

    for step in range(8):
        load_kc(step).start()
        load_cc(step).start()
        load_cov(step).start()
    zeros[...] = jnp.zeros_like(zeros)
    for step in range(1, 8):
        clear(step).start()
    inverse = inv_ref[...]
    inverse_high = inverse.astype(BF16)
    first = k5_ref[...].reshape(512, PROMPTS)
    raw_rows = kr_ref[...].reshape(1024, PROMPTS)
    matrix_rows = cr_ref[...].reshape(512, 1024).astype(F32) + dot(first, raw_rows, nt)
    high, low = split(matrix_rows)
    panel_rows = dot(inverse_high, high, nn).astype(BF16)
    weights[...] = dot(panel_rows, inverse_high, tn).astype(BF16)
    own_high, own_low = split(inv_ref[pl.ds(pl.multiple_of(col * 64, 64), 64), :])
    panel[...] = dot(own_high, high, nn) + (dot(own_low, high, nn) + dot(own_high, low, nn))
    rows[...] = (raw_rows.astype(F32) * scale_ref[0:1] - dot(weights[...], first, nn)).astype(BF16)
    for step in range(8):
        top = step * 128
        height = 1024 - top
        load_kc(step).wait()
        load_cc(step).wait()
        load_cov(step).wait()
        if step >= 2:
            store(step - 2).wait()
        cols = kcb[2 * step : 2 * step + 2].reshape(256, PROMPTS)
        panel_cols = ccb[:, :, step * 256 : (step + 1) * 256].reshape(512, 256)
        value = covb[top:1024, step * 256 : (step + 1) * 256] + (dot(rows[top:], cols, nt) - dot(weights[top:], panel_cols, nn))
        if step == 0:
            value = jnp.concatenate([panel[...].T, value[:, 64:]], axis=1)
        edge = min(256, height)
        i = lax.broadcasted_iota(jnp.int32, (edge, 256), 0) + top
        j = lax.broadcasted_iota(jnp.int32, (edge, 256), 1) + step * 256
        row_global = (i // 64 * 16 + row) * 64 + i % 64
        col_global = (j // 64 * 8 + col) * 64 + j % 64
        outb[step % 2, top : top + edge] = jnp.where(row_global >= col_global, value[:edge], 0.0)
        if edge < height:
            outb[step % 2, top + edge : 1024] = value[edge:]
        store(step).start()
    store(6).wait()
    store(7).wait()
    for step in range(1, 8):
        clear(step).wait()


def update(cov, kc, kr, k5, cr, cc, inverse, scale):
    dma = pltpu.SemaphoreType.DMA
    vmem = pl.BlockSpec(memory_space=pltpu.VMEM)
    anywhere = pl.BlockSpec(memory_space=pl.ANY)
    return pl.pallas_call(
        update_kernel,
        name="update_lower",
        out_shape=jax.ShapeDtypeStruct((1024, 2048), F32),
        in_specs=[anywhere] * 3 + [vmem] * 5,
        out_specs=anywhere,
        scratch_shapes=[
            pltpu.VMEM((1024, 2048), F32), pltpu.VMEM((16, 128, PROMPTS), BF16), pltpu.VMEM((8, 64, 2048), BF16),
            pltpu.VMEM((2, 1024, 256), F32), pltpu.VMEM((64, 1024), F32), pltpu.VMEM((1024, 512), BF16), pltpu.VMEM((1024, PROMPTS), BF16),
            dma((8,)), dma((8,)), dma((8,)), dma((2,)), pltpu.VMEM((896, 256), F32), dma((8,)),
        ],
        compiler_params=pltpu.CompilerParams(vmem_limit_bytes=VMEM_LIMIT),
    )(cov, kc, cc, kr, k5, cr, inverse, scale)


def on_device(residual, positions, norm_gain, w_gate, w_up, covariance):
    kc, kr, k5, cr, cc, inverse, scale = panel(residual, positions, norm_gain, w_gate, w_up, covariance)
    kc = kc.reshape(16, 128, PROMPTS)
    kr = kr.reshape(16, 64, PROMPTS)
    cc = cc.reshape(8, 64, 2048)
    return update(covariance, kc, kr, k5, cr, cc, inverse, scale)


def solution(mesh):
    torus = Mesh(mesh.devices.reshape(4, 4, 4, 2), ("x", "y", "z", "k"))
    row, col = ("x", "y"), ("z", "k")
    placed = (P(row, None, col), P(row), P(col), P(col, row), P(col, row), P(row, col))
    return jax.shard_map(on_device, mesh=torus, in_specs=placed, out_specs=P(row, col), check_vma=False)
```
